32 devices in a mesh: blk: 4 (over y, x), rows: 8 (over z, core).
Axes of the slice: x: 2, y: 2, z: 4, core: 2. Of those that a mesh axis runs over, the one named last changes fastest.
Arguments:
- tokens: bfloat16 [24, 1024, 768], P('rows', 'blk'), may hold values from -6 to 6
- timesteps: int32 [24], P('rows'), may hold values from 0 to 63
- lengths: int32 [24, 8], P('rows'), may hold values from 1 to 1017, as said below
- time_table: bfloat16 [64, 128], replicated, may hold values from -6 to 6
- w_ada: bfloat16 [128, 4608], replicated, may hold values from -0.5 to 0.5
- b_ada: bfloat16 [4608], replicated, may hold values from -3 to 3
- gain_attn: bfloat16 [768], replicated, may hold values from 0.25 to 1.75
- w_qkv: bfloat16 [768, 2304], replicated, may hold values from -0.21875 to 0.21875
- w_out: bfloat16 [768, 768], replicated, may hold values from -0.875 to 0.875
- gain_mlp: bfloat16 [768], replicated, may hold values from 0.25 to 1.75
- w_up: bfloat16 [768, 3072], replicated, may hold values from -0.21875 to 0.21875
- b_up: bfloat16 [3072], replicated, may hold values from -3 to 3
- w_down: bfloat16 [3072, 768], replicated, may hold values from -0.109375 to 0.109375
- b_down: bfloat16 [768], replicated, may hold values from -2 to 2
- grad_out: bfloat16 [24, 1024, 768], P('rows', 'blk'), may hold values from -6 to 6
Outputs:
- out: bfloat16 [24, 1024, 768], P('rows', 'blk')
- grad_tokens: bfloat16 [24, 1024, 768], P('rows', 'blk')
- grad_time_table: float32 [64, 128], replicated
- grad_w_ada: float32 [128, 4608], P('rows')
- grad_b_ada: float32 [4608], replicated
- grad_gain_attn: float32 [768], replicated
- grad_w_qkv: float32 [768, 2304], P('rows')
- grad_w_out: float32 [768, 768], P('rows')
- grad_gain_mlp: float32 [768], replicated
- grad_w_up: float32 [768, 3072], P('rows')
- grad_b_up: float32 [3072], replicated
- grad_w_down: float32 [3072, 768], P('rows')
- grad_b_down: float32 [768], replicated
The draws below stay inside these ranges and needn't reach their ends.
Inputs may be any that keep to these rules, and one draw needn't show every extreme that they name: Each row's 8 lengths are positive and sum to 1024.
All inputs are finite; a program needn't handle non-finite values.
Results may differ from the reference program's by a relative error of at most 0.01505.
The reference program's roundings to bfloat16 on the way count: a program that leaves them out, or rounds other values in their place, can miss the bound.
Values may be sent and summed in bfloat16 or wider, within the bound.
A program may use at most 256 MiB of HBM per device.

```python
import math
import jax
import jax.numpy as jnp
from jax import lax

D = 768
H = 12
HD = 64
FF = 3072
COND = 128
SEQ = 1024
NDOC = 8
TSTEPS = 64
ROWS_DEV = 3
STRETCH = 256
ROWS = 24


def draw_lengths(key, part):
    key = jax.random.fold_in(key, 11)
    pick_key, drawn_key, split_key = jax.random.split(key, 3)
    groups = ROWS // ROWS_DEV
    pick = jax.random.randint(pick_key, (groups,), 0, ROWS_DEV)
    member = jnp.arange(ROWS, dtype=jnp.int32) % ROWS_DEV
    spanning = member == jnp.repeat(pick, ROWS_DEV)
    drawn_keys = jax.random.split(drawn_key, ROWS)
    lowest = max(0, NDOC - STRETCH)
    highest_front = min(NDOC - 1, STRETCH - 1)
    fronts = jax.random.randint(split_key, (ROWS,), lowest, highest_front + 1).astype(jnp.int32)

    def drawn_cuts(row_key):
        return jax.random.permutation(row_key, SEQ - 1)[:NDOC - 1].astype(jnp.int32) + 1
    index = jnp.arange(NDOC - 1, dtype=jnp.int32)[None, :]
    span_cuts = jnp.where(index < fronts[:, None], index + 1, index + SEQ - NDOC + 1).astype(jnp.int32)
    cuts = jnp.where(spanning[:, None], span_cuts, jax.vmap(drawn_cuts)(drawn_keys))
    cuts = jnp.sort(cuts, axis=-1).astype(jnp.int32)
    starting = jnp.zeros((ROWS, 1), jnp.int32)
    closing = jnp.full((ROWS, 1), SEQ, jnp.int32)
    bounds = jnp.concatenate([starting, cuts, closing], axis=-1)
    return (bounds[:, 1:] - bounds[:, :-1]).astype(jnp.int32)


def set_ends(array, stream_key, smallest, high):
    longest = array.shape.index(max(array.shape))
    spots = []
    for shift in (0, 1):
        where = [jax.random.randint(jax.random.fold_in(stream_key, axis), (), 0, length) for axis, length in enumerate(array.shape)]
        where[longest] = (where[longest] + shift) % array.shape[longest]
        spots.append(tuple(where))
    return array.at[spots[0]].set(smallest).at[spots[1]].set(high)


def strengthened(array, key, source, target, parts, factor):
    def block_of(dim):
        return (jnp.arange(array.shape[dim]) // (array.shape[dim] // parts)).reshape((-1,) + (1,) * (array.ndim - 1 - dim))

    near = jax.random.permutation(key, parts)[block_of(target)]
    other_side = (block_of(target) + parts // 2) % parts
    return jnp.where((block_of(source) == near) | (block_of(source) == other_side), factor * array, array)


def level_of(stream_key, dims, cuts, low, largest):
    loudness, own = 1.0, jax.random.fold_in(stream_key, 6)
    for position, blocks in cuts:
        steps = jnp.exp(jax.random.uniform(jax.random.fold_in(own, position), (blocks,), jnp.float32, low / len(cuts), largest / len(cuts)))
        loudness = loudness * jnp.repeat(steps, dims[position] // blocks).reshape([-1 if axis == position else 1 for axis in range(len(dims))])
    return loudness


def normal_values(key, extent, width, most, cuts=(), held_as=jnp.bfloat16):
    values = jax.random.normal(key, extent, jnp.float32) * width
    if len(cuts) > 0:
        values = level_of(key, extent, cuts, -0.22, 0.18) * values
    return jnp.clip(values, min=-most, max=most).astype(held_as)


def gaussian_with(rng, shape, deviation, most, cuts, heavy, held_as=jnp.bfloat16):
    values = deviation * jax.random.normal(rng, shape, jnp.float32)
    if cuts:
        values = values * level_of(rng, shape, cuts, -0.22, 0.18)
    return jnp.clip(strengthened(values, jax.random.fold_in(rng, 3), *heavy), -most, most).astype(held_as)


def setup_inputs(seed: int = 0) -> dict:
    seeds = jax.random.split(jax.random.key(seed), 16)
    tokens = gaussian_with(seeds[0], (ROWS, SEQ, D), 1.0, 6.0, ((0, 8), (1, 4)), (0, 2, 8, 2.0))
    timesteps = set_ends(jax.random.randint(seeds[1], (ROWS,), 0, TSTEPS), jax.random.fold_in(seeds[1], 1), 0, TSTEPS - 1).astype(jnp.int32)
    lengths = draw_lengths(jax.random.fold_in(seeds[15], 71), 0)
    time_table = normal_values(seeds[3], (TSTEPS, COND), 1.0, 6.0)
    w_ada = normal_values(seeds[4], (COND, 6 * D), COND ** -0.5, 0.5)
    b_ada = normal_values(seeds[5], (6 * D,), 0.5, 3.0)
    gain_attn = jnp.clip(1.0 + 0.15 * jax.random.normal(seeds[6], (D,), jnp.float32), 0.25, 1.75).astype(jnp.bfloat16)
    w_qkv = normal_values(seeds[7], (D, 3 * D), D ** -0.5, 0.21875)
    w_out = normal_values(seeds[8], (D, D), (D // 16) ** -0.5, 0.875)
    gain_mlp = jnp.clip(1.0 + 0.15 * jax.random.normal(seeds[9], (D,), jnp.float32), 0.25, 1.75).astype(jnp.bfloat16)
    w_up = normal_values(seeds[10], (D, FF), D ** -0.5, 0.21875)
    b_up = normal_values(seeds[11], (FF,), 0.5, 3.0)
    w_down = normal_values(seeds[12], (FF, D), FF ** -0.5, 0.109375)
    b_down = normal_values(seeds[13], (D,), 0.3, 2.0)
    grad_out = normal_values(seeds[14], (ROWS, SEQ, D), 1.0, 6.0, ((0, 8), (1, 4)))
    return {"tokens": tokens, "timesteps": timesteps, "lengths": lengths, "time_table": time_table, "w_ada": w_ada, "b_ada": b_ada, "gain_attn": gain_attn, "w_qkv": w_qkv, "w_out": w_out, "gain_mlp": gain_mlp, "w_up": w_up, "b_up": b_up, "w_down": w_down, "b_down": b_down, "grad_out": grad_out}


@jax.custom_vjp
def low(v):
    return lax.optimization_barrier(v.astype(jnp.bfloat16)).astype(jnp.float32)

@jax.custom_vjp
def low_back(v):
    return v

def low_keep(v):
    return (low(v), None)

def low_pass(kept, grad):
    return (grad,)

def back_keep(v):
    return (v, None)

def back_low(kept, grad):
    return (low(grad),)
low.defvjp(low_keep, low_pass)
low_back.defvjp(back_keep, back_low)
epsilon = 1e-05
highest = lax.Precision.HIGHEST

def layer_norm(values):
    centre = lax.optimization_barrier(jnp.mean(values, axis=-1, keepdims=True))
    centred = values - centre
    spread = lax.optimization_barrier(jnp.mean(centred * centred, axis=-1, keepdims=True))
    return centred * lax.rsqrt(spread + epsilon)

def rotate(values, cosine, sine):
    half = values.shape[-1] // 2
    first = values[..., :half]
    second = values[..., half:]
    return jnp.concatenate([first * cosine - second * sine, second * cosine + first * sine], axis=-1)

def attend_row(pieces):
    queries, keys, values, doc_ids = pieces
    raw = low_back(jnp.einsum('qhd,khd->hqk', queries, keys, precision=highest))
    same = (doc_ids[:, None] == doc_ids[None, :])[None]
    score = jnp.where(same, raw / math.sqrt(HD), -1e+30)
    top = lax.optimization_barrier(jnp.max(score, axis=-1, keepdims=True))
    expo = jnp.exp(score - top)
    total = lax.optimization_barrier(jnp.sum(expo, axis=-1))
    mixed = jnp.einsum('hqk,khd->qhd', low(expo), values, precision=highest)
    return mixed / jnp.transpose(total)[:, :, None]

def reference(tokens, timesteps, lengths, time_table, w_ada, b_ada, gain_attn, w_qkv, w_out, gain_mlp, w_up, b_up, w_down, b_down, grad_out):
    slots = jnp.arange(SEQ, dtype=jnp.int32)
    ends = jnp.cumsum(lengths, axis=-1).astype(jnp.int32)
    before = ends[:, None, :] <= slots[None, :, None]
    doc_ids = lax.optimization_barrier(jnp.sum(before.astype(jnp.int32), axis=-1)).astype(jnp.int32)
    begins = lax.optimization_barrier(jnp.max(jnp.where(before, ends[:, None, :], 0), axis=-1)).astype(jnp.int32)
    place = (slots[None, :] - begins).astype(jnp.float32)
    freqs = 10000.0 ** (-jnp.arange(HD // 2, dtype=jnp.float32) * 2.0 / HD)
    angle = place[..., None] * freqs
    cosine = jnp.cos(angle)[:, :, None, :]
    sine = jnp.sin(angle)[:, :, None, :]
    onehot = (timesteps[:, None] == jnp.arange(TSTEPS, dtype=jnp.int32)[None, :]).astype(jnp.float32)

    def forward(inputs, table, ada_w, ada_b, gain_a, proj_qkv, proj_out, gain_m, up_w, up_b, down_w, down_b):
        cond = jnp.dot(onehot, table, precision=highest)
        modulate = jnp.dot(jax.nn.silu(cond), ada_w, precision=highest) + ada_b
        shift_a, scale_a, gate_a, shift_m, scale_m, gate_m = jnp.split(modulate[:, None, :], 6, axis=-1)
        hidden_a = low(layer_norm(inputs) * gain_a * (1.0 + scale_a) + shift_a)
        projected = low_back(jnp.einsum('rsd,de->rse', hidden_a, proj_qkv, precision=highest))
        projected = projected.reshape(ROWS, SEQ, 3, H, HD)
        queries = low(rotate(projected[:, :, 0], cosine, sine))
        keys = low(rotate(projected[:, :, 1], cosine, sine))
        values = low(projected[:, :, 2])
        attended = lax.map(jax.checkpoint(attend_row), (queries, keys, values, doc_ids))
        attended = low(low_back(attended.reshape(ROWS, SEQ, D)))
        branch_a = low_back(jnp.einsum('rsd,de->rse', attended, proj_out, precision=highest))
        middle = inputs + gate_a * branch_a
        hidden_m = low(layer_norm(middle) * gain_m * (1.0 + scale_m) + shift_m)
        pre = low_back(jnp.einsum('rsd,df->rsf', hidden_m, up_w, precision=highest) + up_b)
        active = low(jax.nn.gelu(pre, approximate=True))
        branch_m = low_back(jnp.einsum('rsf,fd->rsd', active, down_w, precision=highest) + down_b)
        return middle + gate_m * branch_m
    params = (tokens, time_table, w_ada, b_ada, gain_attn, w_qkv, w_out, gain_mlp, w_up, b_up, w_down, b_down)
    params = tuple((item.astype(jnp.float32) for item in params))
    result, pull = jax.vjp(forward, *params)
    grads = pull(grad_out.astype(jnp.float32))
    return (result.astype(jnp.bfloat16), grads[0].astype(jnp.bfloat16), grads[1], grads[2], grads[3], grads[4], grads[5], grads[6], grads[7], grads[8], grads[9], grads[10], grads[11])
```

```python
import functools
import math

import jax
import jax.numpy as jnp
from jax import lax
from jax.experimental import pallas as pl
from jax.experimental.pallas import tpu as pltpu
from jax.sharding import PartitionSpec as P

H = 12
NDOC = 8
LANES = 128
CHUNK = 256
MIB = 1 << 20

epsilon = 1e-05
highest = lax.Precision.HIGHEST
bf16 = jnp.bfloat16
f32 = jnp.float32
MESH = pl.DeviceIdType.MESH


def dot(a, b):
    return jnp.dot(a, b, preferred_element_type=f32)


def dot_nt(a, b):
    return lax.dot_general(a, b, (((1,), (1,)), ((), ())), preferred_element_type=f32)


def dot_tn(a, b):
    return lax.dot_general(a, b, (((0,), (0,)), ((), ())), preferred_element_type=f32)


def norm_rows(values):
    centre = jnp.mean(values, axis=-1, keepdims=True)
    centred = values - centre
    spread = jnp.mean(centred * centred, axis=-1, keepdims=True)
    inverse = lax.rsqrt(spread + epsilon)
    return (centred * inverse, inverse)


def norm_back(grad_normed, normed, inverse):
    first = jnp.mean(grad_normed, axis=-1, keepdims=True)
    second = jnp.mean(grad_normed * normed, axis=-1, keepdims=True)
    return inverse * (grad_normed - first - normed * second)


def lane_of(shape):
    return lax.broadcasted_iota(jnp.int32, shape, len(shape) - 1)


def swap_halves(values, half):
    lane = lane_of(values.shape)
    width = values.shape[-1]
    ahead = pltpu.roll(values, width - half, values.ndim - 1)
    behind = pltpu.roll(values, half, values.ndim - 1)
    return jnp.where(lane % (2 * half) < half, ahead, behind)


def in_three(values):
    high = values.astype(bf16)
    rest = values - high.astype(f32)
    middle = rest.astype(bf16)
    low = (rest - middle.astype(f32)).astype(bf16)
    return (high, middle, low)


def project_kernel(x_ref, factor_ref, shift_ref, w_ref, cos_ref, sin_ref, h_ref, q_ref, k_ref, v_ref):
    normed, unused = norm_rows(x_ref[...].astype(f32))
    hidden = (normed * factor_ref[...] + shift_ref[...]).astype(bf16)
    h_ref[...] = hidden
    width = x_ref.shape[-1]
    half = width // H // 2
    scale = 1.0 / math.sqrt(2 * half)
    cosine, sine = cos_ref[...], sin_ref[...]
    for part in range(3):
        out = dot(hidden, w_ref[:, part * width : (part + 1) * width])
        for group in range(width // LANES):
            cols = slice(group * LANES, (group + 1) * LANES)
            piece = out[:, cols]
            if part == 2:
                v_ref[:, cols] = piece.astype(bf16)
                continue
            turned = (piece * cosine + swap_halves(piece, half) * sine).astype(bf16)
            if part == 0:
                q_ref[:, cols] = (turned.astype(f32) * scale).astype(bf16)
            else:
                k_ref[:, cols] = turned


def project(x, factor, shift, w_qkv, cosine, sine):
    seq, width = x.shape
    rows = lambda cols: pl.BlockSpec((CHUNK, cols), lambda i: (i, 0))
    fixed = lambda shape: pl.BlockSpec(shape, lambda i: (0, 0))
    return pl.pallas_call(
        project_kernel,
        grid=(seq // CHUNK,),
        in_specs=[
            rows(width),
            fixed((1, width)),
            fixed((1, width)),
            fixed(w_qkv.shape),
            rows(LANES),
            rows(LANES),
        ],
        out_specs=[rows(width)] * 4,
        out_shape=[jax.ShapeDtypeStruct((seq, width), bf16)] * 4,
        compiler_params=pltpu.CompilerParams(vmem_limit_bytes=40 * MIB),
        cost_estimate=pl.CostEstimate(
            flops=2 * seq * width * 3 * width, bytes_accessed=12 * seq * width, transcendentals=0
        ),
    )(x, factor, shift, w_qkv, cosine, sine)


def attend_kernel(q_ref, k_ref, v_ref, fq_ref, fk_ref, att_ref, lse_ref):
    seq = q_ref.shape[0]
    first = lane_of((1, LANES)) < LANES // 2
    one = jnp.ones((), bf16)
    for begin in range(0, seq, CHUNK):
        rows = slice(begin, begin + CHUNK)
        pieces = []
        for head in range(2):
            own = first if head == 0 else jnp.logical_not(first)
            keys = jnp.where(own, k_ref[...], fk_ref[...])
            values = jnp.where(own, v_ref[...], one)
            queries = jnp.where(own, q_ref[rows, :], fq_ref[rows, :])
            score = dot_nt(queries, keys)
            top = jnp.max(score, axis=-1, keepdims=True)
            weight = jnp.exp(score - top).astype(bf16)
            mixed = dot(weight, values)
            pieces.append((mixed / pltpu.roll(mixed, LANES // 2, 1), top + jnp.log(mixed)))
        att_ref[rows, :] = jnp.where(first, pieces[0][0], pieces[1][0])
        lse_ref[rows, :] = jnp.where(first, pieces[1][1], pieces[0][1])


def attend(q, k, v, fq, fk):
    seq, width = q.shape
    pair = pl.BlockSpec((seq, LANES), lambda i: (0, i))
    fixed = pl.BlockSpec((seq, LANES), lambda i: (0, 0))
    return pl.pallas_call(
        attend_kernel,
        grid=(width // LANES,),
        in_specs=[pair, pair, pair, fixed, fixed],
        out_specs=[pair, pair],
        out_shape=[jax.ShapeDtypeStruct((seq, width), f32)] * 2,
        compiler_params=pltpu.CompilerParams(vmem_limit_bytes=40 * MIB),
        cost_estimate=pl.CostEstimate(
            flops=16 * seq * seq * width, bytes_accessed=14 * seq * width, transcendentals=H * seq * seq
        ),
    )(q, k, v, fq, fk)


def attend_back_kernel(
    q_ref, k_ref, v_ref, d_ref, att_ref, lse_ref, fq_ref, fk_ref, cos_ref, sin_ref,
    dq_ref, dk_ref, dv_ref, qa_ref, da_ref, dq_acc
):
    seq = q_ref.shape[0]
    half = LANES // 4
    scale = 1.0 / math.sqrt(2 * half)
    lane = lane_of((1, LANES))
    first = lane < 2 * half
    place = lane % (2 * half)
    one = jnp.ones((), bf16)
    outs = []
    for head in range(2):
        own = first if head == 0 else jnp.logical_not(first)
        lse = in_three(-lse_ref[...])
        feature = fq_ref[...]
        for i in range(3):
            feature = jnp.where(place == NDOC + i, lse[i], feature)
        qa_ref[...] = jnp.where(own, q_ref[...], feature)
        grads = d_ref[...]
        both = jnp.where(own, grads.astype(f32) * att_ref[...], 0.0)
        delta = in_three(jnp.broadcast_to(-jnp.sum(both, axis=-1, keepdims=True), both.shape))
        feature = jnp.zeros_like(grads)
        for i in range(3):
            feature = jnp.where(place == NDOC + i, delta[i], feature)
        da_ref[...] = jnp.where(own, grads, feature)
        pieces = []
        for begin in range(0, seq, CHUNK):
            rows = slice(begin, begin + CHUNK)
            keys = jnp.where(own, k_ref[rows, :], fk_ref[rows, :])
            values = jnp.where(own, v_ref[rows, :], one)
            prob = jnp.exp(dot_nt(keys, qa_ref[...]))
            grad_v = dot(prob.astype(bf16), d_ref[...])
            grad_s = (prob * dot_nt(values, da_ref[...])).astype(bf16)
            grad_k = dot(grad_s, q_ref[...])
            added = dot_tn(grad_s, k_ref[rows, :])
            if begin == 0:
                dq_acc[head] = added
            else:
                dq_acc[head] += added
            pieces.append((grad_k, grad_v))
        outs.append(pieces)
    for step, begin in enumerate(range(0, seq, CHUNK)):
        rows = slice(begin, begin + CHUNK)
        cosine, sine = cos_ref[rows, :], sin_ref[rows, :]
        grad_k = jnp.where(first, outs[0][step][0], outs[1][step][0])
        dk_ref[rows, :] = (grad_k * cosine - swap_halves(grad_k, half) * sine).astype(bf16)
        dv_ref[rows, :] = jnp.where(first, outs[0][step][1], outs[1][step][1]).astype(bf16)
        grad_q = jnp.where(first, dq_acc[0, rows, :], dq_acc[1, rows, :]) * scale
        dq_ref[rows, :] = (grad_q * cosine - swap_halves(grad_q, half) * sine).astype(bf16)


def attend_back(q, k, v, grads, att, lse, fq, fk, cosine, sine):
    seq, width = q.shape
    pair = pl.BlockSpec((seq, LANES), lambda i: (0, i))
    fixed = pl.BlockSpec((seq, LANES), lambda i: (0, 0))
    return pl.pallas_call(
        attend_back_kernel,
        grid=(width // LANES,),
        in_specs=[pair] * 6 + [fixed] * 4,
        out_specs=[pair] * 3,
        out_shape=[jax.ShapeDtypeStruct((seq, width), bf16)] * 3,
        scratch_shapes=[
            pltpu.VMEM((seq, LANES), bf16),
            pltpu.VMEM((seq, LANES), bf16),
            pltpu.VMEM((2, seq, LANES), f32),
        ],
        compiler_params=pltpu.CompilerParams(vmem_limit_bytes=48 * MIB),
        cost_estimate=pl.CostEstimate(
            flops=40 * seq * seq * width, bytes_accessed=24 * seq * width, transcendentals=H * seq * seq
        ),
    )(q, k, v, grads, att, lse, fq, fk, cosine, sine)


def gather_kernel(nblk, nrows, in_ref, out_ref, send_r, recv_r, send_b, recv_b):
    blk, row = lax.axis_index("blk"), lax.axis_index("rows")
    barrier = pltpu.get_barrier_semaphore()
    for step in range(1, nblk):
        pl.semaphore_signal(
            barrier, inc=1, device_id=(lax.rem(blk + step, nblk), row), device_id_type=MESH
        )

    def greet(step, unused):
        pl.semaphore_signal(
            barrier, inc=1, device_id=(blk, lax.rem(row + step, nrows)), device_id_type=MESH
        )
        return unused

    lax.fori_loop(1, nrows, greet, 0)
    pl.semaphore_wait(barrier, nblk + nrows - 2)
    out_ref[blk, row] = in_ref[...]

    def over_rows(step):
        other = lax.rem(row + step, nrows)
        return pltpu.make_async_remote_copy(
            src_ref=in_ref,
            dst_ref=out_ref.at[blk, row],
            send_sem=send_r.at[step],
            recv_sem=recv_r.at[step],
            device_id=(blk, other),
            device_id_type=MESH,
        )

    def over_blk(step):
        other = lax.rem(blk + step, nblk)
        return pltpu.make_async_remote_copy(
            src_ref=out_ref.at[blk],
            dst_ref=out_ref.at[blk],
            send_sem=send_b.at[step],
            recv_sem=recv_b.at[step],
            device_id=(other, row),
            device_id_type=MESH,
        )

    def start(step, unused):
        over_rows(step).start()
        return unused

    def finish(step, unused):
        over_rows(step).wait()
        return unused

    lax.fori_loop(1, nrows, start, 0)
    lax.fori_loop(1, nrows, finish, 0)
    for step in range(1, nblk):
        over_blk(step).start()
    for step in range(1, nblk):
        over_blk(step).wait()


def gather_all(vector, nblk, nrows):
    count = vector.shape[0] // LANES
    return pl.pallas_call(
        functools.partial(gather_kernel, nblk, nrows),
        out_shape=jax.ShapeDtypeStruct((nblk, nrows, count, LANES), f32),
        in_specs=[pl.BlockSpec(memory_space=pltpu.VMEM)],
        out_specs=pl.BlockSpec(memory_space=pltpu.VMEM),
        scratch_shapes=[
            pltpu.SemaphoreType.DMA((nrows,)),
            pltpu.SemaphoreType.DMA((nrows,)),
            pltpu.SemaphoreType.DMA((nblk,)),
            pltpu.SemaphoreType.DMA((nblk,)),
        ],
        compiler_params=pltpu.CompilerParams(collective_id=0, has_side_effects=True),
    )(vector.reshape(count, LANES))


def rows_in(pieces, me, nblk):
    rows = pieces.shape[0]
    parts = [lax.dynamic_index_in_dim(pieces, jnp.minimum(me, rows - 1), 0, keepdims=False)]
    for k in range(1, nblk):
        part = lax.dynamic_index_in_dim(pieces, jnp.minimum(me ^ k, rows - 1), 0, keepdims=False)
        pairs = [(s, s ^ k) for s in range(nblk) if s ^ k < rows]
        parts.append(lax.ppermute(part, "blk", pairs))
    stacked = jnp.stack(parts)
    whole = jnp.take(stacked, jnp.arange(nblk) ^ me, axis=0)
    return jnp.where(me < rows, whole, jnp.zeros_like(whole))


def rows_out(whole, rows, me, nblk):
    parts = [lax.dynamic_index_in_dim(whole, me, 0, keepdims=False)]
    for k in range(1, nblk):
        part = lax.dynamic_index_in_dim(whole, me ^ k, 0, keepdims=False)
        pairs = [(s, s ^ k) for s in range(nblk) if s < rows]
        parts.append(lax.ppermute(part, "blk", pairs))
    stacked = jnp.stack(parts)
    return jnp.take(stacked, jnp.arange(rows) ^ me, axis=0)


def pick(array, index, axis=0):
    return lax.dynamic_index_in_dim(array, index, axis, keepdims=False)


def xor_move(array, axis, size, k):
    return lax.ppermute(array, axis, [(s, s ^ k) for s in range(size)])


def halve(array, axis, bit, name, size, k):
    kept = pick(array, bit, axis).astype(f32)
    sent = pick(array, 1 - bit, axis)
    return (kept + xor_move(sent, name, size, k).astype(f32)).astype(bf16)


def reduce_weight(grad, blk, row, nblk, nrows):
    total, cols = grad.shape
    share = total // nrows
    nz = nrows // 2
    core, z = row % 2, row // 2
    x, y = blk % 2, blk // 2
    part = halve(grad.reshape(nz, 2, share, cols), 1, core, "rows", nrows, 1)
    part = part.reshape(nz, 2, share // 2, cols)
    front, back = part[: nz // 2], part[nz // 2 :]
    split = lambda a: jnp.stack([a[..., : cols // 2], a[..., cols // 2 :]])
    front = halve(split(front), 0, x, "blk", nblk, 1)
    back = halve(back, 1, y, "blk", nblk, 2)
    front = halve(front, 1, y, "blk", nblk, 2)
    back = halve(split(back), 0, x, "blk", nblk, 1)
    part = jnp.concatenate([front, back], axis=0)
    if nz <= 4:
        summed = pick(part, z).astype(f32)
        for k in range(1, nz):
            summed = summed + xor_move(pick(part, z ^ k), "rows", nrows, 2 * k).astype(f32)
        part = summed.astype(bf16)
    else:
        k = nz // 2
        while k:
            pairs = part.reshape((2, k) + part.shape[1:])
            part = halve(pairs, 0, (z // k) % 2, "rows", nrows, 2 * k)
            k //= 2
        part = part[0]
    quarters = [part] + [xor_move(part, "blk", nblk, k) for k in range(1, 4)]
    quarters = jnp.take(jnp.stack(quarters), jnp.arange(4) ^ blk, axis=0)
    ordered = quarters.reshape(2, 2, share // 2, cols // 2).transpose(0, 2, 1, 3)
    return ordered.reshape(share, cols).astype(f32)


def per_device(
    tokens, timesteps, lengths, time_table, w_ada, b_ada, gain_attn, w_qkv, w_out, gain_mlp, w_up, b_up,
    w_down, b_down, grad_out
):
    rows_dev, stretch, width = tokens.shape
    nblk, nrows = lax.axis_size("blk"), lax.axis_size("rows")
    blk, row = lax.axis_index("blk"), lax.axis_index("rows")
    seq = stretch * nblk
    head_dim = width // H
    mine = jnp.minimum(blk, rows_dev - 1)

    x_blocks = rows_in(tokens, blk, nblk)
    g_blocks = rows_in(grad_out, blk, nblk)

    slots = jnp.arange(seq, dtype=jnp.int32)
    ends = jnp.cumsum(pick(lengths, mine))
    before = ends[None, :] <= slots[:, None]
    doc = jnp.sum(before.astype(jnp.int32), axis=-1)
    place = slots - jnp.max(jnp.where(before, ends[None, :], 0), axis=-1)
    freqs = 10000.0 ** (-jnp.arange(head_dim // 2, dtype=f32) * 2.0 / head_dim)
    angle = place.astype(f32)[:, None] * freqs
    cosine, sine = jnp.cos(angle), jnp.sin(angle)
    cosine = jnp.concatenate([cosine] * 4, axis=-1)
    sine = jnp.concatenate([-sine, sine] * 2, axis=-1)
    lane = jnp.arange(LANES) % head_dim
    here = lane[None, :] == doc[:, None]
    fq = jnp.where(here, -1e30, 0.0).astype(bf16)
    fk = jnp.where(here | (lane >= NDOC + 3)[None, :], 0.0, 1.0).astype(bf16)

    table = time_table.astype(f32)
    ada_full = w_ada.astype(f32)
    step = pick(timesteps, mine)
    cond = pick(table, step)[None, :]
    modulate = jnp.dot(jax.nn.silu(cond), ada_full, precision=highest) + b_ada.astype(f32)
    shift_a, scale_a, gate_a, shift_m, scale_m, gate_m = jnp.split(modulate, 6, axis=-1)
    gain_a = gain_attn.astype(f32)
    gain_m = gain_mlp.astype(f32)
    factor_a = gain_a * (1.0 + scale_a)
    factor_m = gain_m * (1.0 + scale_m)

    x_row = x_blocks.reshape(seq, width)
    hidden_a, q, k, v = project(x_row, factor_a, shift_a, w_qkv, cosine, sine)
    attended, lse = attend(q, k, v, fq, fk)
    attended_b = attended.astype(bf16)
    branch_a = dot(attended_b, w_out)
    inputs = x_row.astype(f32)
    middle = inputs + gate_a * branch_a
    normed_m, inverse_m = norm_rows(middle)
    hidden_m = (normed_m * factor_m + shift_m).astype(bf16)
    pre = dot(hidden_m, w_up) + b_up.astype(f32)
    gelu_value, gelu_pull = jax.vjp(lambda values: jax.nn.gelu(values, approximate=True), pre)
    active = gelu_value.astype(bf16)
    branch_m = dot(active, w_down) + b_down.astype(f32)
    result = (middle + gate_m * branch_m).astype(bf16)
    out = rows_out(result.reshape(nblk, stretch, width), rows_dev, blk, nblk)

    grad = g_blocks.reshape(seq, width).astype(f32)
    grad_branch = (gate_m * grad).astype(bf16)
    grad_w_down = dot_tn(active, grad_branch).astype(bf16)
    share_w_down = reduce_weight(grad_w_down, blk, row, nblk, nrows)
    grad_b_down = jnp.sum(grad_branch.astype(f32), axis=0)
    dgate_m = jnp.sum(grad * branch_m, axis=0)
    grad_active = dot_nt(grad_branch, w_down)
    grad_pre = gelu_pull(grad_active)[0].astype(bf16)
    grad_w_up = dot_tn(hidden_m, grad_pre).astype(bf16)
    share_w_up = reduce_weight(grad_w_up, blk, row, nblk, nrows)
    grad_b_up = jnp.sum(grad_pre.astype(f32), axis=0)
    grad_hm = dot_nt(grad_pre, w_up)
    dshift_m = jnp.sum(grad_hm, axis=0)
    along_m = jnp.sum(grad_hm * normed_m, axis=0)
    grad_mid = grad + norm_back(grad_hm * factor_m, normed_m, inverse_m)
    dgate_a = jnp.sum(grad_mid * branch_a, axis=0)
    grad_ya = (gate_a * grad_mid).astype(bf16)
    grad_w_out = dot_tn(attended_b, grad_ya).astype(bf16)
    share_w_out = reduce_weight(grad_w_out, blk, row, nblk, nrows)
    grad_att = dot_nt(grad_ya, w_out).astype(bf16)

    dq, dk, dv = attend_back(q, k, v, grad_att, attended, lse, fq, fk, cosine, sine)
    grad_qkv = jnp.concatenate([dq, dk, dv], axis=-1)
    grad_w_qkv = dot_tn(hidden_a, grad_qkv).astype(bf16)
    share_w_qkv = reduce_weight(grad_w_qkv, blk, row, nblk, nrows)
    grad_ha = dot_nt(grad_qkv, w_qkv)
    normed_a, inverse_a = norm_rows(inputs)
    dshift_a = jnp.sum(grad_ha, axis=0)
    along_a = jnp.sum(grad_ha * normed_a, axis=0)
    grad_in = (grad_mid + norm_back(grad_ha * factor_a, normed_a, inverse_a)).astype(bf16)
    grad_tokens = rows_out(grad_in.reshape(nblk, stretch, width), rows_dev, blk, nblk)

    packed = jnp.concatenate(
        [
            dshift_a, along_a * gain_a, dgate_a, dshift_m, along_m * gain_m, dgate_m,
            along_a * (1.0 + scale_a[0]), along_m * (1.0 + scale_m[0]), grad_b_up, grad_b_down,
            jnp.broadcast_to(step.astype(f32), (LANES,)),
        ]
    )
    gathered = gather_all(packed, nblk, nrows).reshape(nblk, nrows, -1)
    gathered = gathered[:rows_dev].reshape(rows_dev * nrows, -1)
    six = 6 * width
    grad_mod = gathered[:, :six]
    smalls = jnp.sum(gathered, axis=0)
    grad_gain_a, grad_gain_m = smalls[six : six + width], smalls[six + width : six + 2 * width]
    rest = six + 2 * width
    ff = b_up.shape[0]
    total_b_up, total_b_down = smalls[rest : rest + ff], smalls[rest + ff : rest + ff + width]
    steps = gathered[:, -1].astype(jnp.int32)
    onehot = (steps[:, None] == jnp.arange(table.shape[0], dtype=jnp.int32)[None, :]).astype(f32)
    conds = jnp.dot(onehot, table, precision=highest)
    share = conds.shape[1] // nrows
    my_conds = lax.dynamic_slice_in_dim(conds, row * share, share, axis=1)
    grad_w_ada = jnp.dot(jax.nn.silu(my_conds).T, grad_mod, precision=highest)
    grad_cond_act = lax.dot_general(
        grad_mod, ada_full, (((1,), (1,)), ((), ())), precision=highest, preferred_element_type=f32
    )
    sigmoid = jax.nn.sigmoid(conds)
    grad_cond = grad_cond_act * sigmoid * (1.0 + conds * (1.0 - sigmoid))
    grad_table = jnp.dot(onehot.T, grad_cond, precision=highest)
    return (
        out,
        grad_tokens,
        grad_table,
        grad_w_ada,
        smalls[:six],
        grad_gain_a,
        share_w_qkv,
        share_w_out,
        grad_gain_m,
        share_w_up,
        total_b_up,
        share_w_down,
        total_b_down,
    )


def solution(mesh):
    whole, split = P(), P("rows", None)
    tokens = P("rows", "blk", None)
    return jax.shard_map(
        per_device,
        mesh=mesh,
        in_specs=(tokens, P("rows"), split) + (whole,) * 11 + (tokens,),
        out_specs=(
            tokens, tokens, whole, split, whole, whole, split, split, whole, split, whole, split, whole
        ),
        check_vma=False,
    )
```

```python
import functools
import math

import jax
import jax.numpy as jnp
from jax import lax
from jax.experimental import pallas as pl
from jax.experimental.pallas import tpu as pltpu
from jax.sharding import PartitionSpec as P

H = 12
NDOC = 8
LANES = 128
CHUNK = 256
MIB = 1 << 20

epsilon = 1e-05
highest = lax.Precision.HIGHEST
bf16 = jnp.bfloat16
f32 = jnp.float32
MESH = pl.DeviceIdType.MESH


def dot(a, b):
    return jnp.dot(a, b, preferred_element_type=f32)


def dot_nt(a, b):
    return lax.dot_general(a, b, (((1,), (1,)), ((), ())), preferred_element_type=f32)


def dot_tn(a, b):
    return lax.dot_general(a, b, (((0,), (0,)), ((), ())), preferred_element_type=f32)


def norm_rows(values):
    centre = jnp.mean(values, axis=-1, keepdims=True)
    centred = values - centre
    spread = jnp.mean(centred * centred, axis=-1, keepdims=True)
    inverse = lax.rsqrt(spread + epsilon)
    return (centred * inverse, inverse)


def norm_back(grad_normed, normed, inverse):
    first = jnp.mean(grad_normed, axis=-1, keepdims=True)
    second = jnp.mean(grad_normed * normed, axis=-1, keepdims=True)
    return inverse * (grad_normed - first - normed * second)


def lane_of(shape):
    return lax.broadcasted_iota(jnp.int32, shape, len(shape) - 1)


def swap_halves(values, half):
    lane = lane_of(values.shape)
    width = values.shape[-1]
    ahead = pltpu.roll(values, width - half, values.ndim - 1)
    behind = pltpu.roll(values, half, values.ndim - 1)
    return jnp.where(lane % (2 * half) < half, ahead, behind)


def in_three(values):
    high = values.astype(bf16)
    rest = values - high.astype(f32)
    middle = rest.astype(bf16)
    low = (rest - middle.astype(f32)).astype(bf16)
    return (high, middle, low)


def partner(blk, k):
    other = blk
    bit = 1
    while bit <= k:
        if k & bit:
            other = other + bit - 2 * bit * (other // bit % 2)
        bit *= 2
    return other


def remote(source, target, send, recv, blk, row):
    return pltpu.make_async_remote_copy(
        src_ref=source, dst_ref=target, send_sem=send, recv_sem=recv, device_id=(blk, row), device_id_type=MESH
    )


def ahead_kernel(
    tok_ref, grad_ref, vec_ref, w_ref, cos_ref, sin_ref, fq_ref, fk_ref,
    x_out, g_out, h_out, ht_out, q_out, k_out, v_out, att_ref, lse_ref, ab_ref,
    x_s, own_s, h_s, ht_s, q_s, k_s, v_s, w_s, zero_s, send_x, recv_x, send_g, recv_g, local
):
    step, last = pl.program_id(0), pl.num_programs(0) - 1
    blk, row = lax.axis_index("blk"), lax.axis_index("rows")
    rows_dev, stretch, width = tok_ref.shape
    nblk = x_s.shape[0]
    half = width // H // 2
    scale = 1.0 / math.sqrt(2 * half)
    has_row = blk < rows_dev
    mine = jnp.minimum(blk, rows_dev - 1)
    kept = ((x_s, x_out), (h_s, h_out), (ht_s, ht_out), (q_s, q_out), (k_s, k_out), (v_s, v_out))

    def move(k, source, target, send, recv, other):
        return remote(source.at[jnp.minimum(other, rows_dev - 1)], target.at[blk], send.at[k], recv.at[k], other, row)

    def each_sent(source, target, send, recv, what):
        for k in range(1, nblk):
            other = partner(blk, k)

            @pl.when(other < rows_dev)
            def sent():
                what(move(k, source, target, send, recv, other))

    def store(i):
        return pltpu.make_async_copy(kept[i][0], kept[i][1], local.at[i])

    def own_grad():
        return pltpu.make_async_copy(grad_ref.at[mine], g_out.at[blk], local.at[8])

    def chunk(source):
        rows = pl.ds(pl.multiple_of(source * stretch, stretch), stretch)
        normed, unused = norm_rows(x_s[source].astype(f32))
        hidden = normed * vec_ref[0:1, :] + vec_ref[1:2, :]
        hidden_b = hidden.astype(bf16)
        h_s[rows, :] = hidden_b
        ht_s[:, rows] = hidden.T.astype(bf16)
        cosine, sine = cos_ref[rows, :], sin_ref[rows, :]
        for part in range(3):
            out = dot(hidden_b, w_s[:, part * width : (part + 1) * width])
            for group in range(width // LANES):
                cols = slice(group * LANES, (group + 1) * LANES)
                piece = out[:, cols]
                if part == 2:
                    v_s[rows, cols] = piece.astype(bf16)
                    continue
                turned = (piece * cosine + swap_halves(piece, half) * sine).astype(bf16)
                if part == 0:
                    q_s[rows, cols] = (turned.astype(f32) * scale).astype(bf16)
                else:
                    k_s[rows, cols] = turned

    @pl.when(step == 0)
    def begin():
        barrier = pltpu.get_barrier_semaphore()
        for k in range(1, nblk):
            pl.semaphore_signal(barrier, inc=1, device_id=(partner(blk, k), row), device_id_type=MESH)
        weights = pltpu.make_async_copy(w_ref, w_s, local.at[6])
        weights.start()
        own = pltpu.make_async_copy(tok_ref.at[mine], own_s, local.at[7])
        own.start()
        pl.semaphore_wait(barrier, nblk - 1)
        each_sent(tok_ref, x_s, send_x, recv_x, lambda copy: copy.start())
        own.wait()

        @pl.when(has_row)
        def mine_first():
            x_s[blk] = own_s[...]

        @pl.when(jnp.logical_not(has_row))
        def nothing():
            x_s[...] = jnp.zeros_like(x_s)

        weights.wait()
        for k in range(nblk):
            source = partner(blk, k)
            if k:
                @pl.when(has_row)
                def arrived():
                    move(k, tok_ref, x_s, send_x, recv_x, source).wait_recv()

            chunk(source)
        each_sent(tok_ref, x_s, send_x, recv_x, lambda copy: copy.wait_send())
        each_sent(grad_ref, g_out, send_g, recv_g, lambda copy: copy.start())
        zero_s[...] = jnp.zeros_like(zero_s)

        @pl.when(has_row)
        def own_part():
            own_grad().start()

        @pl.when(jnp.logical_not(has_row))
        def no_part():
            for i in range(nblk):
                pltpu.make_async_copy(zero_s, g_out.at[i], local.at[9 + i]).start()

        for i in range(len(kept)):
            store(i).start()

    cols = pl.ds(pl.multiple_of(step * LANES, LANES), LANES)
    seq = q_s.shape[0]
    first = lane_of((1, LANES)) < LANES // 2
    one = jnp.ones((), bf16)
    for start in range(0, seq, CHUNK):
        rows = slice(start, start + CHUNK)
        pieces = []
        for head in range(2):
            own = first if head == 0 else jnp.logical_not(first)
            keys = jnp.where(own, k_s[:, cols], fk_ref[...])
            values = jnp.where(own, v_s[:, cols], one)
            queries = jnp.where(own, q_s[rows, cols], fq_ref[rows, :])
            score = dot_nt(queries, keys)
            top = jnp.max(score, axis=-1, keepdims=True)
            weight = jnp.exp(score - top).astype(bf16)
            mixed = dot(weight, values)
            pieces.append((mixed / pltpu.roll(mixed, LANES // 2, 1), top + jnp.log(mixed)))
        attended = jnp.where(first, pieces[0][0], pieces[1][0])
        att_ref[rows, :] = attended
        ab_ref[rows, :] = attended.astype(bf16)
        lse_ref[rows, :] = jnp.where(first, pieces[1][1], pieces[0][1])

    @pl.when(step == last)
    def end():
        for i in range(len(kept)):
            store(i).wait()
        each_sent(grad_ref, g_out, send_g, recv_g, lambda copy: copy.wait_send())

        @pl.when(has_row)
        def received():
            own_grad().wait()
            for k in range(1, nblk):
                move(k, grad_ref, g_out, send_g, recv_g, partner(blk, k)).wait_recv()

        @pl.when(jnp.logical_not(has_row))
        def cleared():
            for i in range(nblk):
                pltpu.make_async_copy(zero_s, g_out.at[i], local.at[9 + i]).wait()


def ahead(tokens, grads, vec, w_qkv, cosine, sine, fq, fk, nblk):
    rows_dev, stretch, width = tokens.shape
    seq = nblk * stretch
    pair = pl.BlockSpec((seq, LANES), lambda i: (0, i))
    fixed = pl.BlockSpec((seq, LANES), lambda i: (0, 0))
    away = pl.BlockSpec(memory_space=pl.ANY)
    blocks, flat = (nblk, stretch, width), (seq, width)
    shape = jax.ShapeDtypeStruct
    return pl.pallas_call(
        ahead_kernel,
        grid=(width // LANES,),
        in_specs=[away, away, pl.BlockSpec(vec.shape, lambda i: (0, 0)), away, fixed, fixed, fixed, fixed],
        out_specs=[away] * 7 + [pair] * 3,
        out_shape=[
            shape(blocks, bf16), shape(blocks, bf16), shape(flat, bf16), shape(flat[::-1], bf16),
            shape(flat, bf16), shape(flat, bf16), shape(flat, bf16),
            shape(flat, f32), shape(flat, f32), shape(flat, bf16),
        ],
        scratch_shapes=[
            pltpu.VMEM(blocks, bf16), pltpu.VMEM((stretch, width), bf16), pltpu.VMEM(flat, bf16),
            pltpu.VMEM(flat[::-1], bf16), pltpu.VMEM(flat, bf16), pltpu.VMEM(flat, bf16), pltpu.VMEM(flat, bf16),
            pltpu.VMEM(w_qkv.shape, bf16), pltpu.VMEM((stretch, width), bf16),
        ] + [pltpu.SemaphoreType.DMA((nblk,))] * 4 + [pltpu.SemaphoreType.DMA((9 + nblk,))],
        compiler_params=pltpu.CompilerParams(
            collective_id=1, has_side_effects=True, vmem_limit_bytes=56 * MIB
        ),
        cost_estimate=pl.CostEstimate(
            flops=22 * seq * seq * width, bytes_accessed=24 * seq * width, transcendentals=H * seq * seq
        ),
    )(tokens, grads, vec, w_qkv, cosine, sine, fq, fk)


def attend_back_kernel(
    q_ref, k_ref, v_ref, d_ref, att_ref, lse_ref, fq_ref, fk_ref, cos_ref, sin_ref,
    dq_ref, dk_ref, dv_ref, qa_ref, da_ref, dq_acc
):
    seq = q_ref.shape[0]
    half = LANES // 4
    scale = 1.0 / math.sqrt(2 * half)
    lane = lane_of((1, LANES))
    first = lane < 2 * half
    place = lane % (2 * half)
    one = jnp.ones((), bf16)
    outs = []
    for head in range(2):
        own = first if head == 0 else jnp.logical_not(first)
        lse = in_three(-lse_ref[...])
        feature = fq_ref[...]
        for i in range(3):
            feature = jnp.where(place == NDOC + i, lse[i], feature)
        qa_ref[...] = jnp.where(own, q_ref[...], feature)
        grads = d_ref[...]
        both = jnp.where(own, grads.astype(f32) * att_ref[...], 0.0)
        delta = in_three(jnp.broadcast_to(-jnp.sum(both, axis=-1, keepdims=True), both.shape))
        feature = jnp.zeros_like(grads)
        for i in range(3):
            feature = jnp.where(place == NDOC + i, delta[i], feature)
        da_ref[...] = jnp.where(own, grads, feature)
        pieces = []
        for begin in range(0, seq, CHUNK):
            rows = slice(begin, begin + CHUNK)
            keys = jnp.where(own, k_ref[rows, :], fk_ref[rows, :])
            values = jnp.where(own, v_ref[rows, :], one)
            prob = jnp.exp(dot_nt(keys, qa_ref[...]))
            grad_v = dot(prob.astype(bf16), d_ref[...])
            grad_s = (prob * dot_nt(values, da_ref[...])).astype(bf16)
            grad_k = dot(grad_s, q_ref[...])
            added = dot_tn(grad_s, k_ref[rows, :])
            if begin == 0:
                dq_acc[head] = added
            else:
                dq_acc[head] += added
            pieces.append((grad_k, grad_v))
        outs.append(pieces)
    for step, begin in enumerate(range(0, seq, CHUNK)):
        rows = slice(begin, begin + CHUNK)
        cosine, sine = cos_ref[rows, :], sin_ref[rows, :]
        grad_k = jnp.where(first, outs[0][step][0], outs[1][step][0])
        dk_ref[rows, :] = (grad_k * cosine - swap_halves(grad_k, half) * sine).astype(bf16)
        dv_ref[rows, :] = jnp.where(first, outs[0][step][1], outs[1][step][1]).astype(bf16)
        grad_q = jnp.where(first, dq_acc[0, rows, :], dq_acc[1, rows, :]) * scale
        dq_ref[rows, :] = (grad_q * cosine - swap_halves(grad_q, half) * sine).astype(bf16)


def attend_back(q, k, v, grads, att, lse, fq, fk, cosine, sine):
    seq, width = q.shape
    pair = pl.BlockSpec((seq, LANES), lambda i: (0, i))
    fixed = pl.BlockSpec((seq, LANES), lambda i: (0, 0))
    return pl.pallas_call(
        attend_back_kernel,
        grid=(width // LANES,),
        in_specs=[pair] * 6 + [fixed] * 4,
        out_specs=[pair] * 3,
        out_shape=[jax.ShapeDtypeStruct((seq, width), bf16)] * 3,
        scratch_shapes=[
            pltpu.VMEM((seq, LANES), bf16),
            pltpu.VMEM((seq, LANES), bf16),
            pltpu.VMEM((2, seq, LANES), f32),
        ],
        compiler_params=pltpu.CompilerParams(vmem_limit_bytes=48 * MIB),
        cost_estimate=pl.CostEstimate(
            flops=40 * seq * seq * width, bytes_accessed=24 * seq * width, transcendentals=H * seq * seq
        ),
    )(q, k, v, grads, att, lse, fq, fk, cosine, sine)


GELU = math.sqrt(2.0 / math.pi)
CUBE = 0.044715


def feed_kernel(
    ab_ref, x_ref, g_ref, vec_ref, w_out_ref, w_up_ref, b_up_ref, w_down_ref, b_down_ref,
    result_ref, dx_ref, datt_ref, g_out_ref, g_up_ref, g_down_ref, gb_up_ref, sums_ref,
    h_s, ht_s, dz_s, dzt_s, y_s, z_s, dh_s, act_s, du_s, dyt_s
):
    step, last = pl.program_id(0), pl.num_programs(0) - 1
    seq, width = x_ref.shape
    gate_a, factor_m, shift_m, gate_m = (vec_ref[i : i + 1, :] for i in range(4))
    chunks = [slice(begin, begin + CHUNK) for begin in range(0, seq, CHUNK)]

    @pl.when(step == 0)
    def before():
        for rows in chunks:
            y = dot(ab_ref[rows, :], w_out_ref[...])
            y_s[rows, :] = y
            normed, unused = norm_rows(x_ref[rows, :].astype(f32) + gate_a * y)
            hidden = normed * factor_m + shift_m
            h_s[rows, :] = hidden.astype(bf16)
            ht_s[:, rows] = hidden.T.astype(bf16)
            grad = gate_m * g_ref[rows, :].astype(f32)
            dz_s[rows, :] = grad.astype(bf16)
            dzt_s[:, rows] = grad.T.astype(bf16)
        z_s[...] = jnp.zeros_like(z_s)
        dh_s[...] = jnp.zeros_like(dh_s)

    bias_sum = jnp.zeros((1, w_up_ref.shape[1]), f32)
    for rows in chunks:
        u = dot(h_s[rows, :], w_up_ref[...]) + b_up_ref[...]
        square = u * u
        turn = jnp.tanh(GELU * u * (1.0 + CUBE * square))
        half = 0.5 * (1.0 + turn)
        act = (u * half).astype(bf16)
        slope = half + (0.5 * GELU) * u * (1.0 - turn * turn) * (1.0 + 3.0 * CUBE * square)
        du = (dot_nt(dz_s[rows, :], w_down_ref[...]) * slope).astype(bf16)
        act_s[rows, :] = act
        du_s[rows, :] = du
        bias_sum = bias_sum + jnp.sum(du.astype(f32), axis=0, keepdims=True)
        z_s[rows, :] += dot(act, w_down_ref[...])
        dh_s[rows, :] += dot_nt(du, w_up_ref[...])
    gb_up_ref[...] = bias_sum
    g_up_ref[...] = dot(ht_s[...], du_s[...]).astype(bf16)
    g_down_ref[...] = dot(dzt_s[...], act_s[...]).astype(bf16)

    @pl.when(step == last)
    def after():
        sums = [jnp.zeros((1, width), f32) for unused in range(5)]
        for rows in chunks:
            y = y_s[rows, :]
            middle = x_ref[rows, :].astype(f32) + gate_a * y
            normed, inverse = norm_rows(middle)
            z = z_s[rows, :] + b_down_ref[...]
            result_ref[rows, :] = (middle + gate_m * z).astype(bf16)
            grad = g_ref[rows, :].astype(f32)
            dh = dh_s[rows, :]
            dx = grad + norm_back(dh * factor_m, normed, inverse)
            dx_ref[rows, :] = dx
            dy = gate_a * dx
            dyb = dy.astype(bf16)
            dyt_s[rows, :] = dyb
            datt_ref[rows, :] = dot_nt(dyb, w_out_ref[...]).astype(bf16)
            terms = (grad * z, dh, dh * normed, dx * y, dz_s[rows, :].astype(f32))
            sums = [a + jnp.sum(b, axis=0, keepdims=True) for a, b in zip(sums, terms)]
        g_out_ref[...] = dot_tn(ab_ref[...], dyt_s[...]).astype(bf16)
        for i in range(5):
            sums_ref[i : i + 1, :] = sums[i]


def feed(ab, x, g, vec, w_out, w_up, b_up, w_down, b_down):
    seq, width = x.shape
    ff = w_up.shape[1]
    wide = width
    fixed = lambda a: pl.BlockSpec(a.shape, lambda i: (0, 0))
    one = lambda shape: pl.BlockSpec(shape, lambda i: (0, 0))
    col = lambda r: pl.BlockSpec((r, wide), lambda i: (0, i))
    shape = jax.ShapeDtypeStruct
    return pl.pallas_call(
        feed_kernel,
        grid=(ff // wide,),
        in_specs=[
            fixed(ab), fixed(x), fixed(g), fixed(vec), fixed(w_out), col(width), col(1),
            pl.BlockSpec((wide, width), lambda i: (i, 0)), fixed(b_down),
        ],
        out_specs=[
            one((seq, width)), one((seq, width)), one((seq, width)), one((width, width)),
            col(width), col(width), col(1), one((8, width)),
        ],
        out_shape=[
            shape((seq, width), bf16), shape((seq, width), f32), shape((seq, width), bf16),
            shape((width, width), bf16), shape((width, ff), bf16), shape((width, ff), bf16),
            shape((1, ff), f32), shape((8, width), f32),
        ],
        scratch_shapes=[
            pltpu.VMEM((seq, width), bf16), pltpu.VMEM((width, seq), bf16),
            pltpu.VMEM((seq, width), bf16), pltpu.VMEM((width, seq), bf16),
            pltpu.VMEM((seq, width), f32), pltpu.VMEM((seq, width), f32), pltpu.VMEM((seq, width), f32),
            pltpu.VMEM((seq, wide), bf16), pltpu.VMEM((seq, wide), bf16), pltpu.VMEM((seq, width), bf16),
        ],
        compiler_params=pltpu.CompilerParams(vmem_limit_bytes=60 * MIB),
        cost_estimate=pl.CostEstimate(
            flops=12 * seq * width * ff, bytes_accessed=30 * seq * width, transcendentals=seq * ff
        ),
    )(ab, x, g, vec, w_out, w_up, b_up, w_down, b_down)


def gather_kernel(nblk, nrows, in_ref, out_ref, send_r, recv_r, send_b, recv_b):
    blk, row = lax.axis_index("blk"), lax.axis_index("rows")
    barrier = pltpu.get_barrier_semaphore()
    for step in range(1, nblk):
        pl.semaphore_signal(
            barrier, inc=1, device_id=(lax.rem(blk + step, nblk), row), device_id_type=MESH
        )

    def greet(step, unused):
        pl.semaphore_signal(
            barrier, inc=1, device_id=(blk, lax.rem(row + step, nrows)), device_id_type=MESH
        )
        return unused

    lax.fori_loop(1, nrows, greet, 0)
    pl.semaphore_wait(barrier, nblk + nrows - 2)
    out_ref[blk, row] = in_ref[...]

    def over_rows(step):
        other = lax.rem(row + step, nrows)
        return pltpu.make_async_remote_copy(
            src_ref=in_ref,
            dst_ref=out_ref.at[blk, row],
            send_sem=send_r.at[step],
            recv_sem=recv_r.at[step],
            device_id=(blk, other),
            device_id_type=MESH,
        )

    def over_blk(step):
        other = lax.rem(blk + step, nblk)
        return pltpu.make_async_remote_copy(
            src_ref=out_ref.at[blk],
            dst_ref=out_ref.at[blk],
            send_sem=send_b.at[step],
            recv_sem=recv_b.at[step],
            device_id=(other, row),
            device_id_type=MESH,
        )

    def start(step, unused):
        over_rows(step).start()
        return unused

    def finish(step, unused):
        over_rows(step).wait()
        return unused

    lax.fori_loop(1, nrows, start, 0)
    lax.fori_loop(1, nrows, finish, 0)
    for step in range(1, nblk):
        over_blk(step).start()
    for step in range(1, nblk):
        over_blk(step).wait()


def gather_all(vector, nblk, nrows):
    count = vector.shape[0] // LANES
    return pl.pallas_call(
        functools.partial(gather_kernel, nblk, nrows),
        out_shape=jax.ShapeDtypeStruct((nblk, nrows, count, LANES), f32),
        in_specs=[pl.BlockSpec(memory_space=pltpu.VMEM)],
        out_specs=pl.BlockSpec(memory_space=pltpu.VMEM),
        scratch_shapes=[
            pltpu.SemaphoreType.DMA((nrows,)),
            pltpu.SemaphoreType.DMA((nrows,)),
            pltpu.SemaphoreType.DMA((nblk,)),
            pltpu.SemaphoreType.DMA((nblk,)),
        ],
        compiler_params=pltpu.CompilerParams(collective_id=0, has_side_effects=True),
    )(vector.reshape(count, LANES))


def rows_out(whole, rows, me, nblk):
    parts = [lax.dynamic_index_in_dim(whole, me, 0, keepdims=False)]
    for k in range(1, nblk):
        part = lax.dynamic_index_in_dim(whole, me ^ k, 0, keepdims=False)
        pairs = [(s, s ^ k) for s in range(nblk) if s < rows]
        parts.append(lax.ppermute(part, "blk", pairs))
    stacked = jnp.stack(parts)
    return jnp.take(stacked, jnp.arange(rows) ^ me, axis=0)


def pick(array, index, axis=0):
    return lax.dynamic_index_in_dim(array, index, axis, keepdims=False)


def xor_move(array, axis, size, k):
    return lax.ppermute(array, axis, [(s, s ^ k) for s in range(size)])


def halve(array, axis, bit, name, size, k):
    kept = pick(array, bit, axis).astype(f32)
    sent = pick(array, 1 - bit, axis)
    return (kept + xor_move(sent, name, size, k).astype(f32)).astype(bf16)


def reduce_weight(grad, blk, row, nblk, nrows):
    total, cols = grad.shape
    share = total // nrows
    nz = nrows // 2
    core, z = row % 2, row // 2
    x, y = blk % 2, blk // 2
    part = halve(grad.reshape(nz, 2, share, cols), 1, core, "rows", nrows, 1)
    part = part.reshape(nz, 2, share // 2, cols)
    front, back = part[: nz // 2], part[nz // 2 :]
    split = lambda a: jnp.stack([a[..., : cols // 2], a[..., cols // 2 :]])
    front = halve(split(front), 0, x, "blk", nblk, 1)
    back = halve(back, 1, y, "blk", nblk, 2)
    front = halve(front, 1, y, "blk", nblk, 2)
    back = halve(split(back), 0, x, "blk", nblk, 1)
    part = jnp.concatenate([front, back], axis=0)
    if nz <= 4:
        summed = pick(part, z).astype(f32)
        for k in range(1, nz):
            summed = summed + xor_move(pick(part, z ^ k), "rows", nrows, 2 * k).astype(f32)
        part = summed.astype(bf16)
    else:
        k = nz // 2
        while k:
            pairs = part.reshape((2, k) + part.shape[1:])
            part = halve(pairs, 0, (z // k) % 2, "rows", nrows, 2 * k)
            k //= 2
        part = part[0]
    quarters = [part] + [xor_move(part, "blk", nblk, k) for k in range(1, 4)]
    quarters = jnp.take(jnp.stack(quarters), jnp.arange(4) ^ blk, axis=0)
    ordered = quarters.reshape(2, 2, share // 2, cols // 2).transpose(0, 2, 1, 3)
    return ordered.reshape(share, cols).astype(f32)


def per_device(
    tokens, timesteps, lengths, time_table, w_ada, b_ada, gain_attn, w_qkv, w_out, gain_mlp, w_up, b_up,
    w_down, b_down, grad_out
):
    rows_dev, stretch, width = tokens.shape
    nblk, nrows = lax.axis_size("blk"), lax.axis_size("rows")
    blk, row = lax.axis_index("blk"), lax.axis_index("rows")
    seq = stretch * nblk
    head_dim = width // H
    mine = jnp.minimum(blk, rows_dev - 1)

    slots = jnp.arange(seq, dtype=jnp.int32)
    ends = jnp.cumsum(pick(lengths, mine))
    before = ends[None, :] <= slots[:, None]
    doc = jnp.sum(before.astype(jnp.int32), axis=-1)
    place = slots - jnp.max(jnp.where(before, ends[None, :], 0), axis=-1)
    freqs = 10000.0 ** (-jnp.arange(head_dim // 2, dtype=f32) * 2.0 / head_dim)
    angle = place.astype(f32)[:, None] * freqs
    cosine, sine = jnp.cos(angle), jnp.sin(angle)
    cosine = jnp.concatenate([cosine] * 4, axis=-1)
    sine = jnp.concatenate([-sine, sine] * 2, axis=-1)
    lane = jnp.arange(LANES) % head_dim
    here = lane[None, :] == doc[:, None]
    fq = jnp.where(here, -1e30, 0.0).astype(bf16)
    fk = jnp.where(here | (lane >= NDOC + 3)[None, :], 0.0, 1.0).astype(bf16)

    table = time_table.astype(f32)
    ada_full = w_ada.astype(f32)
    step = pick(timesteps, mine)
    cond = pick(table, step)[None, :]
    modulate = jnp.dot(jax.nn.silu(cond), ada_full, precision=highest) + b_ada.astype(f32)
    shift_a, scale_a, gate_a, shift_m, scale_m, gate_m = jnp.split(modulate, 6, axis=-1)
    gain_a = gain_attn.astype(f32)
    gain_m = gain_mlp.astype(f32)
    factor_a = gain_a * (1.0 + scale_a)
    factor_m = gain_m * (1.0 + scale_m)

    vec = jnp.concatenate([factor_a, shift_a], axis=0)
    x_blocks, g_blocks, hidden_a, hidden_t, q, k, v, attended, lse, attended_b = ahead(
        tokens, grad_out, vec, w_qkv, cosine, sine, fq, fk, nblk
    )
    x_row = x_blocks.reshape(seq, width)

    g_row = g_blocks.reshape(seq, width)
    vec = jnp.concatenate([gate_a, factor_m, shift_m, gate_m], axis=0)
    result, grad_mid, grad_att, grad_w_out, grad_w_up, grad_w_down, gb_up, sums = feed(
        attended_b, x_row, g_row, vec, w_out, w_up, b_up.astype(f32)[None, :], w_down,
        b_down.astype(f32)[None, :]
    )
    out = rows_out(result.reshape(nblk, stretch, width), rows_dev, blk, nblk)
    dgate_m, dshift_m, along_m, dgate_a, grad_b_down = (sums[i] for i in range(5))
    grad_b_up = gb_up[0]
    share_w_down = reduce_weight(grad_w_down.T, blk, row, nblk, nrows)
    share_w_up = reduce_weight(grad_w_up, blk, row, nblk, nrows)
    share_w_out = reduce_weight(grad_w_out, blk, row, nblk, nrows)

    dq, dk, dv = attend_back(q, k, v, grad_att, attended, lse, fq, fk, cosine, sine)
    grad_qkv = jnp.concatenate([dq, dk, dv], axis=-1)
    grad_w_qkv = dot(hidden_t, grad_qkv).astype(bf16)
    share_w_qkv = reduce_weight(grad_w_qkv, blk, row, nblk, nrows)
    grad_ha = dot_nt(grad_qkv, w_qkv)
    normed_a, inverse_a = norm_rows(x_row.astype(f32))
    dshift_a = jnp.sum(grad_ha, axis=0)
    along_a = jnp.sum(grad_ha * normed_a, axis=0)
    grad_in = (grad_mid + norm_back(grad_ha * factor_a, normed_a, inverse_a)).astype(bf16)
    grad_tokens = rows_out(grad_in.reshape(nblk, stretch, width), rows_dev, blk, nblk)

    packed = jnp.concatenate(
        [
            dshift_a, along_a * gain_a, dgate_a, dshift_m, along_m * gain_m, dgate_m,
            along_a * (1.0 + scale_a[0]), along_m * (1.0 + scale_m[0]), grad_b_up, grad_b_down,
            jnp.broadcast_to(step.astype(f32), (LANES,)),
        ]
    )
    gathered = gather_all(packed, nblk, nrows).reshape(nblk, nrows, -1)
    gathered = gathered[:rows_dev].reshape(rows_dev * nrows, -1)
    six = 6 * width
    grad_mod = gathered[:, :six]
    smalls = jnp.sum(gathered, axis=0)
    grad_gain_a, grad_gain_m = smalls[six : six + width], smalls[six + width : six + 2 * width]
    rest = six + 2 * width
    ff = b_up.shape[0]
    total_b_up, total_b_down = smalls[rest : rest + ff], smalls[rest + ff : rest + ff + width]
    steps = gathered[:, -1].astype(jnp.int32)
    onehot = (steps[:, None] == jnp.arange(table.shape[0], dtype=jnp.int32)[None, :]).astype(f32)
    conds = jnp.dot(onehot, table, precision=highest)
    share = conds.shape[1] // nrows
    my_conds = lax.dynamic_slice_in_dim(conds, row * share, share, axis=1)
    grad_w_ada = jnp.dot(jax.nn.silu(my_conds).T, grad_mod, precision=highest)
    grad_cond_act = lax.dot_general(
        grad_mod, ada_full, (((1,), (1,)), ((), ())), precision=highest, preferred_element_type=f32
    )
    sigmoid = jax.nn.sigmoid(conds)
    grad_cond = grad_cond_act * sigmoid * (1.0 + conds * (1.0 - sigmoid))
    grad_table = jnp.dot(onehot.T, grad_cond, precision=highest)
    return (
        out,
        grad_tokens,
        grad_table,
        grad_w_ada,
        smalls[:six],
        grad_gain_a,
        share_w_qkv,
        share_w_out,
        grad_gain_m,
        share_w_up,
        total_b_up,
        share_w_down,
        total_b_down,
    )


def solution(mesh):
    whole, split = P(), P("rows", None)
    tokens = P("rows", "blk", None)
    return jax.shard_map(
        per_device,
        mesh=mesh,
        in_specs=(tokens, P("rows"), split) + (whole,) * 11 + (tokens,),
        out_specs=(
            tokens, tokens, whole, split, whole, whole, split, split, whole, split, whole, split, whole
        ),
        check_vma=False,
    )
```

```python
import functools
import math

import jax
import jax.numpy as jnp
from jax import lax
from jax.experimental import pallas as pl
from jax.experimental.pallas import tpu as pltpu
from jax.sharding import PartitionSpec as P

H = 12
NDOC = 8
LANES = 128
CHUNK = 256
MIB = 1 << 20

epsilon = 1e-05
highest = lax.Precision.HIGHEST
bf16 = jnp.bfloat16
f32 = jnp.float32
MESH = pl.DeviceIdType.MESH


def dot(a, b):
    return jnp.dot(a, b, preferred_element_type=f32)


def dot_nt(a, b):
    return lax.dot_general(a, b, (((1,), (1,)), ((), ())), preferred_element_type=f32)


def dot_tn(a, b):
    return lax.dot_general(a, b, (((0,), (0,)), ((), ())), preferred_element_type=f32)


def norm_rows(values):
    centre = jnp.mean(values, axis=-1, keepdims=True)
    centred = values - centre
    spread = jnp.mean(centred * centred, axis=-1, keepdims=True)
    inverse = lax.rsqrt(spread + epsilon)
    return (centred * inverse, inverse)


def norm_back(grad_normed, normed, inverse):
    first = jnp.mean(grad_normed, axis=-1, keepdims=True)
    second = jnp.mean(grad_normed * normed, axis=-1, keepdims=True)
    return inverse * (grad_normed - first - normed * second)


def lane_of(shape):
    return lax.broadcasted_iota(jnp.int32, shape, len(shape) - 1)


def swap_halves(values, half):
    lane = lane_of(values.shape)
    width = values.shape[-1]
    ahead = pltpu.roll(values, width - half, values.ndim - 1)
    behind = pltpu.roll(values, half, values.ndim - 1)
    return jnp.where(lane % (2 * half) < half, ahead, behind)


def in_three(values):
    high = values.astype(bf16)
    rest = values - high.astype(f32)
    middle = rest.astype(bf16)
    low = (rest - middle.astype(f32)).astype(bf16)
    return (high, middle, low)


def partner(blk, k):
    other = blk
    bit = 1
    while bit <= k:
        if k & bit:
            other = other + bit - 2 * bit * (other // bit % 2)
        bit *= 2
    return other


def remote(source, target, send, recv, blk, row):
    return pltpu.make_async_remote_copy(
        src_ref=source, dst_ref=target, send_sem=send, recv_sem=recv, device_id=(blk, row), device_id_type=MESH
    )


def ahead_kernel(
    tok_ref, grad_ref, vec_ref, w_ref, cos_ref, sin_ref, fq_ref, fk_ref,
    x_out, g_out, h_out, ht_out, q_out, k_out, v_out, att_ref, lse_ref, ab_ref,
    x_s, own_s, h_s, ht_s, q_s, k_s, v_s, w_s, zero_s, send_x, recv_x, send_g, recv_g, local
):
    step, last = pl.program_id(0), pl.num_programs(0) - 1
    blk, row = lax.axis_index("blk"), lax.axis_index("rows")
    rows_dev, stretch, width = tok_ref.shape
    nblk = x_s.shape[0]
    half = width // H // 2
    scale = 1.0 / math.sqrt(2 * half)
    has_row = blk < rows_dev
    mine = jnp.minimum(blk, rows_dev - 1)
    kept = ((x_s, x_out), (h_s, h_out), (ht_s, ht_out), (q_s, q_out), (k_s, k_out), (v_s, v_out))

    def move(k, source, target, send, recv, other):
        return remote(source.at[jnp.minimum(other, rows_dev - 1)], target.at[blk], send.at[k], recv.at[k], other, row)

    def each_sent(source, target, send, recv, what):
        for k in range(1, nblk):
            other = partner(blk, k)

            @pl.when(other < rows_dev)
            def sent():
                what(move(k, source, target, send, recv, other))

    def store(i):
        return pltpu.make_async_copy(kept[i][0], kept[i][1], local.at[i])

    def own_grad():
        return pltpu.make_async_copy(grad_ref.at[mine], g_out.at[blk], local.at[8])

    def chunk(source):
        rows = pl.ds(pl.multiple_of(source * stretch, stretch), stretch)
        normed, unused = norm_rows(x_s[source].astype(f32))
        hidden = normed * vec_ref[0:1, :] + vec_ref[1:2, :]
        hidden_b = hidden.astype(bf16)
        h_s[rows, :] = hidden_b
        ht_s[:, rows] = hidden.T.astype(bf16)
        cosine, sine = cos_ref[rows, :], sin_ref[rows, :]
        for part in range(3):
            out = dot(hidden_b, w_s[:, part * width : (part + 1) * width])
            for group in range(width // LANES):
                cols = slice(group * LANES, (group + 1) * LANES)
                piece = out[:, cols]
                if part == 2:
                    v_s[rows, cols] = piece.astype(bf16)
                    continue
                turned = (piece * cosine + swap_halves(piece, half) * sine).astype(bf16)
                if part == 0:
                    q_s[rows, cols] = (turned.astype(f32) * scale).astype(bf16)
                else:
                    k_s[rows, cols] = turned

    @pl.when(step == 0)
    def begin():
        barrier = pltpu.get_barrier_semaphore()
        for k in range(1, nblk):
            pl.semaphore_signal(barrier, inc=1, device_id=(partner(blk, k), row), device_id_type=MESH)
        weights = pltpu.make_async_copy(w_ref, w_s, local.at[6])
        weights.start()
        own = pltpu.make_async_copy(tok_ref.at[mine], own_s, local.at[7])
        own.start()
        pl.semaphore_wait(barrier, nblk - 1)
        each_sent(tok_ref, x_s, send_x, recv_x, lambda copy: copy.start())
        own.wait()

        @pl.when(has_row)
        def mine_first():
            x_s[blk] = own_s[...]

        @pl.when(jnp.logical_not(has_row))
        def nothing():
            x_s[...] = jnp.zeros_like(x_s)

        weights.wait()
        for k in range(nblk):
            source = partner(blk, k)
            if k:
                @pl.when(has_row)
                def arrived():
                    move(k, tok_ref, x_s, send_x, recv_x, source).wait_recv()

            chunk(source)
        each_sent(tok_ref, x_s, send_x, recv_x, lambda copy: copy.wait_send())
        each_sent(grad_ref, g_out, send_g, recv_g, lambda copy: copy.start())
        zero_s[...] = jnp.zeros_like(zero_s)

        @pl.when(has_row)
        def own_part():
            own_grad().start()

        @pl.when(jnp.logical_not(has_row))
        def no_part():
            for i in range(nblk):
                pltpu.make_async_copy(zero_s, g_out.at[i], local.at[9 + i]).start()

        for i in range(len(kept)):
            store(i).start()

    cols = pl.ds(pl.multiple_of(step * LANES, LANES), LANES)
    seq = q_s.shape[0]
    first = lane_of((1, LANES)) < LANES // 2
    one = jnp.ones((), bf16)
    for start in range(0, seq, CHUNK):
        rows = slice(start, start + CHUNK)
        pieces = []
        for head in range(2):
            own = first if head == 0 else jnp.logical_not(first)
            keys = jnp.where(own, k_s[:, cols], fk_ref[...])
            values = jnp.where(own, v_s[:, cols], one)
            queries = jnp.where(own, q_s[rows, cols], fq_ref[rows, :])
            score = dot_nt(queries, keys)
            top = jnp.max(score, axis=-1, keepdims=True)
            weight = jnp.exp(score - top).astype(bf16)
            mixed = dot(weight, values)
            pieces.append((mixed / pltpu.roll(mixed, LANES // 2, 1), top + jnp.log(mixed)))
        attended = jnp.where(first, pieces[0][0], pieces[1][0])
        att_ref[rows, :] = attended
        ab_ref[rows, :] = attended.astype(bf16)
        lse_ref[rows, :] = jnp.where(first, pieces[1][1], pieces[0][1])

    @pl.when(step == last)
    def end():
        for i in range(len(kept)):
            store(i).wait()
        each_sent(grad_ref, g_out, send_g, recv_g, lambda copy: copy.wait_send())

        @pl.when(has_row)
        def received():
            own_grad().wait()
            for k in range(1, nblk):
                move(k, grad_ref, g_out, send_g, recv_g, partner(blk, k)).wait_recv()

        @pl.when(jnp.logical_not(has_row))
        def cleared():
            for i in range(nblk):
                pltpu.make_async_copy(zero_s, g_out.at[i], local.at[9 + i]).wait()


def ahead(tokens, grads, vec, w_qkv, cosine, sine, fq, fk, nblk):
    rows_dev, stretch, width = tokens.shape
    seq = nblk * stretch
    pair = pl.BlockSpec((seq, LANES), lambda i: (0, i))
    fixed = pl.BlockSpec((seq, LANES), lambda i: (0, 0))
    away = pl.BlockSpec(memory_space=pl.ANY)
    blocks, flat = (nblk, stretch, width), (seq, width)
    shape = jax.ShapeDtypeStruct
    return pl.pallas_call(
        ahead_kernel,
        grid=(width // LANES,),
        in_specs=[away, away, pl.BlockSpec(vec.shape, lambda i: (0, 0)), away, fixed, fixed, fixed, fixed],
        out_specs=[away] * 7 + [pair] * 3,
        out_shape=[
            shape(blocks, bf16), shape(blocks, bf16), shape(flat, bf16), shape(flat[::-1], bf16),
            shape(flat, bf16), shape(flat, bf16), shape(flat, bf16),
            shape(flat, f32), shape(flat, f32), shape(flat, bf16),
        ],
        scratch_shapes=[
            pltpu.VMEM(blocks, bf16), pltpu.VMEM((stretch, width), bf16), pltpu.VMEM(flat, bf16),
            pltpu.VMEM(flat[::-1], bf16), pltpu.VMEM(flat, bf16), pltpu.VMEM(flat, bf16), pltpu.VMEM(flat, bf16),
            pltpu.VMEM(w_qkv.shape, bf16), pltpu.VMEM((stretch, width), bf16),
        ] + [pltpu.SemaphoreType.DMA((nblk,))] * 4 + [pltpu.SemaphoreType.DMA((9 + nblk,))],
        compiler_params=pltpu.CompilerParams(
            collective_id=1, has_side_effects=True, vmem_limit_bytes=56 * MIB
        ),
        cost_estimate=pl.CostEstimate(
            flops=22 * seq * seq * width, bytes_accessed=24 * seq * width, transcendentals=H * seq * seq
        ),
    )(tokens, grads, vec, w_qkv, cosine, sine, fq, fk)


def attend_back_kernel(
    q_ref, k_ref, v_ref, d_ref, att_ref, lse_ref, fq_ref, fk_ref, cos_ref, sin_ref,
    dq_ref, dk_ref, dv_ref, qa_ref, da_ref, dq_acc
):
    seq = q_ref.shape[0]
    half = LANES // 4
    scale = 1.0 / math.sqrt(2 * half)
    lane = lane_of((1, LANES))
    first = lane < 2 * half
    place = lane % (2 * half)
    one = jnp.ones((), bf16)
    outs = []
    for head in range(2):
        own = first if head == 0 else jnp.logical_not(first)
        lse = in_three(-lse_ref[...])
        feature = fq_ref[...]
        for i in range(3):
            feature = jnp.where(place == NDOC + i, lse[i], feature)
        qa_ref[...] = jnp.where(own, q_ref[...], feature)
        grads = d_ref[...]
        both = jnp.where(own, grads.astype(f32) * att_ref[...], 0.0)
        delta = in_three(jnp.broadcast_to(-jnp.sum(both, axis=-1, keepdims=True), both.shape))
        feature = jnp.zeros_like(grads)
        for i in range(3):
            feature = jnp.where(place == NDOC + i, delta[i], feature)
        da_ref[...] = jnp.where(own, grads, feature)
        pieces = []
        for begin in range(0, seq, CHUNK):
            rows = slice(begin, begin + CHUNK)
            keys = jnp.where(own, k_ref[rows, :], fk_ref[rows, :])
            values = jnp.where(own, v_ref[rows, :], one)
            prob = jnp.exp(dot_nt(keys, qa_ref[...]))
            grad_v = dot(prob.astype(bf16), d_ref[...])
            grad_s = (prob * dot_nt(values, da_ref[...])).astype(bf16)
            grad_k = dot(grad_s, q_ref[...])
            added = dot_tn(grad_s, k_ref[rows, :])
            if begin == 0:
                dq_acc[head] = added
            else:
                dq_acc[head] += added
            pieces.append((grad_k, grad_v))
        outs.append(pieces)
    for step, begin in enumerate(range(0, seq, CHUNK)):
        rows = slice(begin, begin + CHUNK)
        cosine, sine = cos_ref[rows, :], sin_ref[rows, :]
        grad_k = jnp.where(first, outs[0][step][0], outs[1][step][0])
        dk_ref[rows, :] = (grad_k * cosine - swap_halves(grad_k, half) * sine).astype(bf16)
        dv_ref[rows, :] = jnp.where(first, outs[0][step][1], outs[1][step][1]).astype(bf16)
        grad_q = jnp.where(first, dq_acc[0, rows, :], dq_acc[1, rows, :]) * scale
        dq_ref[rows, :] = (grad_q * cosine - swap_halves(grad_q, half) * sine).astype(bf16)


def attend_back(q, k, v, grads, att, lse, fq, fk, cosine, sine):
    seq, width = q.shape
    pair = pl.BlockSpec((seq, LANES), lambda i: (0, i))
    fixed = pl.BlockSpec((seq, LANES), lambda i: (0, 0))
    return pl.pallas_call(
        attend_back_kernel,
        grid=(width // LANES,),
        in_specs=[pair] * 6 + [fixed] * 4,
        out_specs=[pair] * 3,
        out_shape=[jax.ShapeDtypeStruct((seq, width), bf16)] * 3,
        scratch_shapes=[
            pltpu.VMEM((seq, LANES), bf16),
            pltpu.VMEM((seq, LANES), bf16),
            pltpu.VMEM((2, seq, LANES), f32),
        ],
        compiler_params=pltpu.CompilerParams(vmem_limit_bytes=48 * MIB),
        cost_estimate=pl.CostEstimate(
            flops=40 * seq * seq * width, bytes_accessed=24 * seq * width, transcendentals=H * seq * seq
        ),
    )(q, k, v, grads, att, lse, fq, fk, cosine, sine)


GELU = math.sqrt(2.0 / math.pi)
CUBE = 0.044715


def feed_kernel(
    ab_ref, x_ref, g_ref, vec_ref, w_out_ref, w_up_ref, b_up_ref, w_down_ref, b_down_ref,
    result_ref, dx_ref, datt_ref, g_out_ref, g_up_ref, g_down_ref, gb_up_ref, sums_ref,
    h_s, ht_s, dz_s, dzt_s, y_s, z_s, dh_s, act_s, du_s, dyt_s
):
    step, last = pl.program_id(0), pl.num_programs(0) - 1
    seq, width = x_ref.shape
    wide = w_up_ref.shape[1]
    gate_a, factor_m, shift_m, gate_m = (vec_ref[i : i + 1, :] for i in range(4))
    chunks = [slice(begin, begin + CHUNK) for begin in range(0, seq, CHUNK)]

    @pl.when(step == 0)
    def before():
        for rows in chunks:
            y = dot(ab_ref[rows, :], w_out_ref[...])
            y_s[rows, :] = y
            normed, unused = norm_rows(x_ref[rows, :].astype(f32) + gate_a * y)
            hidden = normed * factor_m + shift_m
            h_s[rows, :] = hidden.astype(bf16)
            ht_s[:, rows] = hidden.T.astype(bf16)
            grad = gate_m * g_ref[rows, :].astype(f32)
            dz_s[rows, :] = grad.astype(bf16)
            dzt_s[:, rows] = grad.T.astype(bf16)
        z_s[...] = jnp.zeros_like(z_s)
        dh_s[...] = jnp.zeros_like(dh_s)

    bias_sum = jnp.zeros((1, w_up_ref.shape[1]), f32)
    for rows in chunks:
        u = dot(h_s[rows, :], w_up_ref[...]) + b_up_ref[...]
        square = u * u
        turn = jnp.tanh(GELU * u * (1.0 + CUBE * square))
        half = 0.5 * (1.0 + turn)
        act = (u * half).astype(bf16)
        slope = half + (0.5 * GELU) * u * (1.0 - turn * turn) * (1.0 + 3.0 * CUBE * square)
        du = (dot_nt(dz_s[rows, :], w_down_ref[...]) * slope).astype(bf16)
        act_s[rows, :] = act
        du_s[rows, :] = du
        bias_sum = bias_sum + jnp.sum(du.astype(f32), axis=0, keepdims=True)
        z_s[rows, :] += dot(act, w_down_ref[...])
        dh_s[rows, :] += dot_nt(du, w_up_ref[...])
    gb_up_ref[...] = bias_sum
    g_up_ref[0] = dot(ht_s[...], du_s[...]).astype(bf16)
    down = dot(dzt_s[...], act_s[...]).astype(bf16)
    g_down_ref[0, 0] = down[:, : wide // 2]
    g_down_ref[0, 1] = down[:, wide // 2 :]

    @pl.when(step == last)
    def after():
        sums = [jnp.zeros((1, width), f32) for unused in range(5)]
        for rows in chunks:
            y = y_s[rows, :]
            middle = x_ref[rows, :].astype(f32) + gate_a * y
            normed, inverse = norm_rows(middle)
            z = z_s[rows, :] + b_down_ref[...]
            result_ref[rows, :] = (middle + gate_m * z).astype(bf16)
            grad = g_ref[rows, :].astype(f32)
            dh = dh_s[rows, :]
            dx = grad + norm_back(dh * factor_m, normed, inverse)
            dx_ref[rows, :] = dx
            dy = gate_a * dx
            dyb = dy.astype(bf16)
            dyt_s[rows, :] = dyb
            datt_ref[rows, :] = dot_nt(dyb, w_out_ref[...]).astype(bf16)
            terms = (grad * z, dh, dh * normed, dx * y, dz_s[rows, :].astype(f32))
            sums = [a + jnp.sum(b, axis=0, keepdims=True) for a, b in zip(sums, terms)]
        g_out_ref[...] = dot_tn(ab_ref[...], dyt_s[...]).astype(bf16)
        for i in range(5):
            sums_ref[i : i + 1, :] = sums[i]


def feed(ab, x, g, vec, w_out, w_up, b_up, w_down, b_down):
    seq, width = x.shape
    ff = w_up.shape[1]
    wide = width
    fixed = lambda a: pl.BlockSpec(a.shape, lambda i: (0, 0))
    one = lambda shape: pl.BlockSpec(shape, lambda i: (0, 0))
    col = lambda r: pl.BlockSpec((r, wide), lambda i: (0, i))
    shape = jax.ShapeDtypeStruct
    return pl.pallas_call(
        feed_kernel,
        grid=(ff // wide,),
        in_specs=[
            fixed(ab), fixed(x), fixed(g), fixed(vec), fixed(w_out), col(width), col(1),
            pl.BlockSpec((wide, width), lambda i: (i, 0)), fixed(b_down),
        ],
        out_specs=[
            one((seq, width)), one((seq, width)), one((seq, width)), one((width, width)),
            pl.BlockSpec((1, width, wide), lambda i: (i, 0, 0)),
            pl.BlockSpec((1, 2, width, wide // 2), lambda i: (i, 0, 0, 0)), col(1), one((8, width)),
        ],
        out_shape=[
            shape((seq, width), bf16), shape((seq, width), f32), shape((seq, width), bf16),
            shape((width, width), bf16), shape((ff // wide, width, wide), bf16),
            shape((ff // wide, 2, width, wide // 2), bf16),
            shape((1, ff), f32), shape((8, width), f32),
        ],
        scratch_shapes=[
            pltpu.VMEM((seq, width), bf16), pltpu.VMEM((width, seq), bf16),
            pltpu.VMEM((seq, width), bf16), pltpu.VMEM((width, seq), bf16),
            pltpu.VMEM((seq, width), f32), pltpu.VMEM((seq, width), f32), pltpu.VMEM((seq, width), f32),
            pltpu.VMEM((seq, wide), bf16), pltpu.VMEM((seq, wide), bf16), pltpu.VMEM((seq, width), bf16),
        ],
        compiler_params=pltpu.CompilerParams(vmem_limit_bytes=60 * MIB),
        cost_estimate=pl.CostEstimate(
            flops=12 * seq * width * ff, bytes_accessed=30 * seq * width, transcendentals=seq * ff
        ),
    )(ab, x, g, vec, w_out, w_up, b_up, w_down, b_down)


def gather_kernel(nblk, nrows, in_ref, out_ref, send_r, recv_r, send_b, recv_b):
    blk, row = lax.axis_index("blk"), lax.axis_index("rows")
    barrier = pltpu.get_barrier_semaphore()
    for step in range(1, nblk):
        pl.semaphore_signal(
            barrier, inc=1, device_id=(lax.rem(blk + step, nblk), row), device_id_type=MESH
        )

    def greet(step, unused):
        pl.semaphore_signal(
            barrier, inc=1, device_id=(blk, lax.rem(row + step, nrows)), device_id_type=MESH
        )
        return unused

    lax.fori_loop(1, nrows, greet, 0)
    pl.semaphore_wait(barrier, nblk + nrows - 2)
    out_ref[blk, row] = in_ref[...]

    def over_rows(step):
        other = lax.rem(row + step, nrows)
        return pltpu.make_async_remote_copy(
            src_ref=in_ref,
            dst_ref=out_ref.at[blk, row],
            send_sem=send_r.at[step],
            recv_sem=recv_r.at[step],
            device_id=(blk, other),
            device_id_type=MESH,
        )

    def over_blk(step):
        other = lax.rem(blk + step, nblk)
        return pltpu.make_async_remote_copy(
            src_ref=out_ref.at[blk],
            dst_ref=out_ref.at[blk],
            send_sem=send_b.at[step],
            recv_sem=recv_b.at[step],
            device_id=(other, row),
            device_id_type=MESH,
        )

    def start(step, unused):
        over_rows(step).start()
        return unused

    def finish(step, unused):
        over_rows(step).wait()
        return unused

    lax.fori_loop(1, nrows, start, 0)
    lax.fori_loop(1, nrows, finish, 0)
    for step in range(1, nblk):
        over_blk(step).start()
    for step in range(1, nblk):
        over_blk(step).wait()


def gather_all(vector, nblk, nrows):
    count = vector.shape[0] // LANES
    return pl.pallas_call(
        functools.partial(gather_kernel, nblk, nrows),
        out_shape=jax.ShapeDtypeStruct((nblk, nrows, count, LANES), f32),
        in_specs=[pl.BlockSpec(memory_space=pltpu.VMEM)],
        out_specs=pl.BlockSpec(memory_space=pltpu.VMEM),
        scratch_shapes=[
            pltpu.SemaphoreType.DMA((nrows,)),
            pltpu.SemaphoreType.DMA((nrows,)),
            pltpu.SemaphoreType.DMA((nblk,)),
            pltpu.SemaphoreType.DMA((nblk,)),
        ],
        compiler_params=pltpu.CompilerParams(collective_id=0, has_side_effects=True),
    )(vector.reshape(count, LANES))


class Place:
    def __init__(self):
        self.blk, self.row = lax.axis_index("blk"), lax.axis_index("rows")
        self.x, self.y = self.blk % 2, self.blk // 2
        self.core, self.z = self.row % 2, self.row // 2

    def along_blk(self, k):
        return (partner(self.blk, k), self.row)

    def along_rows(self, k):
        return (self.blk, partner(self.row, k))


class Sems:
    def __init__(self, send, recv):
        self.send, self.recv, self.used = send, recv, 0

    def take(self, count):
        self.used += count
        return self.used - count

    def copy(self, index, source, target, device):
        return remote(source, target, self.send.at[index], self.recv.at[index], *device)


def part(index, size, step):
    return pl.ds(pl.multiple_of(index * size, step), size)


class RowPiece:
    SEMS = 11

    @staticmethod
    def scratch(nz, share, cols):
        hs, hc = share // 2, cols // 2
        shapes = [
            (nz, share, cols), (nz // 2, share, hc), (nz // 2, hs, cols), (nz // 2, hs, hc), (nz // 2, hs, hc),
            (nz, hs, hc), (nz, hs, hc), (4, hs, hc),
        ]
        return [pltpu.VMEM(shape, bf16) for shape in shapes]

    def __init__(self, place, sems, whole, own, bufs, store):
        self.p, self.sems, self.base = place, sems, sems.take(self.SEMS)
        self.whole, self.own, self.store = whole, own, store
        self.core, self.a1, self.b1, self.a2, self.b2, self.r3, self.zr, self.ag = bufs
        self.nz, share, cols = self.core.shape
        self.hs, self.hc, self.hz = share // 2, cols // 2, self.nz // 2

    def copies(self, stage):
        p, at = self.p, self.base
        low, high = slice(0, self.hz), slice(self.hz, self.nz)
        row = lambda y: part(y, self.hs, 16)
        col = lambda x: part(x, self.hc, LANES)
        if stage == 0:
            return [self.sems.copy(at, self.whole.at[:, 1 - p.core], self.core, p.along_rows(1))]
        if stage == 1:
            return [
                self.sems.copy(at + 1, self.core.at[low, :, col(1 - p.x)], self.a1, p.along_blk(1)),
                self.sems.copy(at + 2, self.core.at[high, row(1 - p.y), :], self.b1, p.along_blk(2)),
            ]
        if stage == 2:
            return [
                self.sems.copy(at + 3, self.a1.at[:, row(1 - p.y), :], self.a2, p.along_blk(2)),
                self.sems.copy(at + 4, self.b1.at[:, :, col(1 - p.x)], self.b2, p.along_blk(1)),
            ]
        if stage == 3:
            return [
                self.sems.copy(at + 4 + k, self.r3.at[partner(p.z, k)], self.zr.at[p.z], p.along_rows(2 * k))
                for k in range(1, self.nz)
            ]
        return [
            self.sems.copy(at + 7 + k, self.ag.at[p.blk], self.ag.at[p.blk], p.along_blk(k)) for k in range(1, 4)
        ]

    def wait(self, stage):
        for copy in self.copies(stage):
            copy.wait()

    def run(self, stage):
        p = self.p
        if stage:
            self.wait(stage - 1)
        mine_row, mine_col = part(p.y, self.hs, 16), part(p.x, self.hc, LANES)
        if stage == 1:
            self.core[...] = self.core[...] + self.own()
        if stage == 2:
            self.a1[...] = self.a1[...] + self.core[: self.hz, :, mine_col]
            self.b1[...] = self.b1[...] + self.core[self.hz :, mine_row, :]
        if stage == 3:
            self.r3[: self.hz] = self.a1[:, mine_row, :] + self.a2[...]
            self.r3[self.hz :] = self.b1[:, :, mine_col] + self.b2[...]
        if stage == 4:
            total = self.r3[p.z].astype(f32)
            for k in range(1, self.nz):
                total = total + self.zr[partner(p.z, k)].astype(f32)
            self.ag[p.blk] = total.astype(bf16)
        if stage == 5:
            for q in range(4):
                rows = slice(q // 2 * self.hs, (q // 2 + 1) * self.hs)
                self.store(rows, q % 2 * self.hc, self.ag[q].astype(f32))
            return
        for copy in self.copies(stage):
            copy.start()


class ColPiece:
    SEMS = 12

    @staticmethod
    def scratch(nz, depth, cols):
        shapes = [
            (2, 2, 2, depth, cols), (2, depth, cols), (2, depth, cols), (depth, cols), (depth, cols),
            (2, depth, cols), (nz, 2, depth, cols),
        ]
        return [pltpu.VMEM(shape, bf16) for shape in shapes]

    def __init__(self, place, sems, whole, own, bufs, gathered, store, owner):
        self.p, self.sems, self.base = place, sems, sems.take(self.SEMS)
        self.whole, self.own, self.store, self.owner = whole, own, store, owner
        self.core, self.a1, self.b1, self.a2, self.b2, self.r3, self.zr = bufs
        self.ag = gathered
        self.nz = self.zr.shape[0]

    def copies(self, stage):
        p, at = self.p, self.base
        if stage == 0:
            return [self.sems.copy(at, self.whole.at[1 - p.core], self.core, p.along_rows(1))]
        if stage == 1:
            return [
                self.sems.copy(at + 1, self.core.at[:, 1 - p.x, 0], self.a1, p.along_blk(1)),
                self.sems.copy(at + 2, self.core.at[1 - p.y, :, 1], self.b1, p.along_blk(2)),
            ]
        if stage == 2:
            return [
                self.sems.copy(at + 3, self.a1.at[1 - p.y], self.a2, p.along_blk(2)),
                self.sems.copy(at + 4, self.b1.at[1 - p.x], self.b2, p.along_blk(1)),
            ]
        return [
            self.sems.copy(at + 8 + k, self.ag.at[p.blk], self.ag.at[p.blk], p.along_blk(k)) for k in range(1, 4)
        ]

    def over_z(self, k):
        p = self.p
        device = (p.blk, 2 * self.owner + p.core)
        return self.sems.copy(self.base + 5 + k, self.r3, self.zr.at[p.z], device)

    def run(self, stage):
        p, is_owner = self.p, self.p.z == self.owner
        if stage in (1, 2, 3):
            for copy in self.copies(stage - 1):
                copy.wait()
        if stage == 1:
            self.core[...] = self.core[...] + self.own()
        if stage == 2:
            self.a1[...] = self.a1[...] + self.core[:, p.x, 0]
            self.b1[...] = self.b1[...] + self.core[p.y, :, 1]
        if stage == 3:
            self.r3[0] = self.a1[p.y] + self.a2[...]
            self.r3[1] = self.b1[p.x] + self.b2[...]
            for k in range(1, self.nz):
                @pl.when(p.z == self.owner ^ k)
                def sent():
                    self.over_z(k).start()
            return
        if stage == 4:
            for k in range(1, self.nz):
                @pl.when(p.z == self.owner ^ k)
                def left():
                    self.over_z(k).wait_send()

            @pl.when(is_owner)
            def summed():
                total = self.r3[...].astype(f32)
                for k in range(1, self.nz):
                    self.over_z(k).wait_recv()
                    total = total + self.zr[self.owner ^ k].astype(f32)
                self.ag[p.blk] = total.astype(bf16)
                for copy in self.copies(4):
                    copy.start()
            return
        if stage == 5:
            @pl.when(is_owner)
            def whole():
                for copy in self.copies(4):
                    copy.wait()
                depth = self.r3.shape[1]
                for q in range(8):
                    self.store(slice(q * depth, (q + 1) * depth), self.ag[q // 2, q % 2].astype(f32))
            return
        for copy in self.copies(stage):
            copy.start()


class Gather:
    def __init__(self, place, sems, source, target):
        self.p, self.sems, self.source, self.target = place, sems, source, target
        self.nblk, self.nrows = target.shape[:2]
        self.base = sems.take(self.nblk + self.nrows)

    def copies(self, stage):
        p = self.p
        if stage == 0:
            return [
                self.sems.copy(self.base + k, self.source, self.target.at[p.blk, p.row], p.along_rows(k))
                for k in range(1, self.nrows)
            ]
        return [
            self.sems.copy(self.base + self.nrows + k, self.target.at[p.blk], self.target.at[p.blk], p.along_blk(k))
            for k in range(1, self.nblk)
        ]

    def run(self, stage):
        if stage:
            for copy in self.copies(stage - 1):
                copy.wait()
        else:
            self.target[self.p.blk, self.p.row] = self.source[...]
        if stage < 2:
            for copy in self.copies(stage):
                copy.start()


class Return:
    def __init__(self, place, sems, source, target, local):
        self.p, self.sems, self.source, self.target, self.local = place, sems, source, target, local
        self.rows, self.nblk = target.shape[0], source.shape[0]
        self.base = sems.take(self.nblk)
        self.mine = jnp.minimum(place.blk, self.rows - 1)

    def copy(self, k):
        device = self.p.along_blk(k)
        return self.sems.copy(self.base + k, self.source.at[device[0]], self.target.at[self.mine], device)

    def own(self):
        return pltpu.make_async_copy(self.source.at[self.p.blk], self.target.at[self.mine], self.local)

    def start(self, ks):
        @pl.when(self.p.blk < self.rows)
        def sent():
            for k in ks:
                (self.copy(k) if k else self.own()).start()

    def finish(self):
        @pl.when(self.p.blk < self.rows)
        def left():
            self.own().wait()
            for k in range(1, self.nblk):
                self.copy(k).wait_send()

        for k in range(1, self.nblk):
            @pl.when(partner(self.p.blk, k) < self.rows)
            def arrived():
                self.copy(k).wait_recv()


def greet(place, nblk, nrows):
    barrier = pltpu.get_barrier_semaphore()
    for k in range(1, nblk):
        pl.semaphore_signal(barrier, inc=1, device_id=place.along_blk(k), device_id_type=MESH)
    for k in range(1, nrows):
        pl.semaphore_signal(barrier, inc=1, device_id=place.along_rows(k), device_id_type=MESH)
    pl.semaphore_wait(barrier, nblk + nrows - 2)


def behind_kernel(
    n_up, owners,
    q_ref, k_ref, v_ref, d_ref, att_ref, lse_ref, fq_ref, fk_ref, cos_ref, sin_ref, wq_ref, wk_ref, wv_ref,
    ht_ref, x_ref, dx_ref, vec_ref, early_ref, up_ref, down_ref, out_ref, result_ref,
    tok_out, grad_out, share_qkv, share_out, share_up, share_down, early_out, late_out,
    qa_ref, da_ref, dq_acc, dqkv_s, dh_s, gq_s, gt_s, early_s, late_s, late_b, early_g, late_g, down_ag,
    own_up, own_down, own_out, send, recv, local, *bufs
):
    step, last = pl.program_id(0), pl.num_programs(0) - 1
    place = Place()
    sems = Sems(send, recv)
    nblk, stretch, width = x_ref.shape
    nrows = early_g.shape[1]
    seq = nblk * stretch
    n_down = len(owners)
    bufs = list(bufs)

    def taken(count):
        out = bufs[:count]
        del bufs[:count]
        return out

    def store_at(ref, begin):
        def store(rows, col, value):
            ref[rows, begin + col : begin + col + value.shape[1]] = value
        return store

    def store_qkv(j):
        def store(rows, col, value):
            for group in range(value.shape[1] // LANES):
                lane = col + group * LANES
                at = lane // (2 * LANES) * width + j * 2 * LANES + lane % (2 * LANES)
                share_qkv[rows, at : at + LANES] = value[:, group * LANES : (group + 1) * LANES]
        return store

    def store_down(rows, value):
        share_down[rows, :] = value

    pieces = []
    loads = []
    for i in range(n_up):
        pieces.append(RowPiece(place, sems, up_ref.at[i], lambda i=i: own_up[i], taken(8), store_at(share_up, i * width)))
        loads.append((up_ref.at[i, :, place.core], own_up.at[i]))
    for i in range(n_down):
        pieces.append(
            ColPiece(place, sems, down_ref.at[i], lambda i=i: own_down[i], taken(7), down_ag, store_down, owners[i])
        )
        loads.append((down_ref.at[i, place.core], own_down.at[i]))
    pieces.append(RowPiece(place, sems, out_ref, lambda: own_out[...], taken(8), store_at(share_out, 0)))
    loads.append((out_ref.at[:, place.core], own_out))
    loads = [pltpu.make_async_copy(a, b, local.at[2 + i]) for i, (a, b) in enumerate(loads)]
    late_pieces = [
        RowPiece(place, sems, gq_s.at[j], lambda j=j: gq_s[j, :, place.core], taken(8), store_qkv(j)) for j in range(3)
    ]
    results = Return(place, sems, result_ref, tok_out, local.at[0])
    grads = Return(place, sems, gt_s, grad_out, local.at[1])
    early = Gather(place, sems, early_s, early_g)
    late = Gather(place, sems, late_b, late_g)

    plan = {}

    def at(slot, *actions):
        plan.setdefault(slot, []).extend(actions)

    def stage(piece, number):
        return lambda: piece.run(number)

    def loaded():
        for load in loads:
            load.wait()

    half_way = len(pieces)
    at(0, lambda: greet(place, nblk, nrows))
    at(0, *[load.start for load in loads])
    at(0, *[stage(piece, 0) for piece in pieces])
    at(0, lambda: results.start(range(nblk)))
    at(1, loaded)
    for e, piece in enumerate(pieces):
        begin = 1 + e * 5 // half_way
        for number in range(1, 6):
            at(min(begin + 2 * number - 2, 20), stage(piece, number))
    at(2, lambda: early_start(), lambda: early.run(0))
    at(4, lambda: early.run(1))
    at(8, lambda: early.run(2))
    for number in range(1, 6):
        at(3 + 2 * number, stage(late_pieces[0], number))
    for number in (1, 2):
        at(7 + 2 * number, stage(late_pieces[1], number))

    def early_start():
        early_s[...] = early_ref[...]

    def slot(number):
        if number in plan:
            @pl.when(step == number // 2)
            def actions():
                for action in plan[number]:
                    action()

    half = LANES // 4
    scale = 1.0 / math.sqrt(2 * half)
    lane = lane_of((1, LANES))
    first = lane < 2 * half
    where = lane % (2 * half)
    one = jnp.ones((), bf16)
    outs = []
    for head in range(2):
        for i in range(6):
            slot(2 * i + head)
        own = first if head == 0 else jnp.logical_not(first)
        lse = in_three(-lse_ref[...])
        feature = fq_ref[...]
        for i in range(3):
            feature = jnp.where(where == NDOC + i, lse[i], feature)
        qa_ref[...] = jnp.where(own, q_ref[...], feature)
        datt = d_ref[...]
        both = jnp.where(own, datt.astype(f32) * att_ref[...], 0.0)
        delta = in_three(jnp.broadcast_to(-jnp.sum(both, axis=-1, keepdims=True), both.shape))
        feature = jnp.zeros_like(datt)
        for i in range(3):
            feature = jnp.where(where == NDOC + i, delta[i], feature)
        da_ref[...] = jnp.where(own, datt, feature)
        blocks = []
        for begin in range(0, seq, CHUNK):
            rows = slice(begin, begin + CHUNK)
            keys = jnp.where(own, k_ref[rows, :], fk_ref[rows, :])
            values = jnp.where(own, v_ref[rows, :], one)
            prob = jnp.exp(dot_nt(keys, qa_ref[...]))
            grad_v = dot(prob.astype(bf16), d_ref[...])
            grad_s = (prob * dot_nt(values, da_ref[...])).astype(bf16)
            grad_k = dot(grad_s, q_ref[...])
            added = dot_tn(grad_s, k_ref[rows, :])
            if begin == 0:
                dq_acc[head] = added
            else:
                dq_acc[head] += added
            blocks.append((grad_k, grad_v))
        outs.append(blocks)
    side = step % 2 * LANES
    for number, begin in enumerate(range(0, seq, CHUNK)):
        rows = slice(begin, begin + CHUNK)
        cosine, sine = cos_ref[rows, :], sin_ref[rows, :]
        grad_k = jnp.where(first, outs[0][number][0], outs[1][number][0])
        grad_k = (grad_k * cosine - swap_halves(grad_k, half) * sine).astype(bf16)
        grad_v = jnp.where(first, outs[0][number][1], outs[1][number][1]).astype(bf16)
        grad_q = jnp.where(first, dq_acc[0, rows, :], dq_acc[1, rows, :]) * scale
        grad_q = (grad_q * cosine - swap_halves(grad_q, half) * sine).astype(bf16)
        for i, grad in enumerate((grad_q, grad_k, grad_v)):
            dqkv_s[rows, pl.ds(pl.multiple_of(2 * i * LANES + side, LANES), LANES)] = grad

    @pl.when(step % 2 == 1)
    def projections():
        group = step // 2
        grad_w = dot(ht_ref[...], dqkv_s[...]).astype(bf16)
        gq_s[group] = grad_w.reshape(gq_s.shape[1:])
        for rows in (slice(begin, begin + CHUNK) for begin in range(0, seq, CHUNK)):
            added = dot_nt(dqkv_s[rows, : 2 * LANES], wq_ref[...])
            added = added + dot_nt(dqkv_s[rows, 2 * LANES : 4 * LANES], wk_ref[...])
            added = added + dot_nt(dqkv_s[rows, 4 * LANES :], wv_ref[...])

            @pl.when(group == 0)
            def fresh():
                dh_s[rows, :] = added

            @pl.when(group > 0)
            def more():
                dh_s[rows, :] += added

        for j, piece in enumerate(late_pieces):
            @pl.when(group == j)
            def sent():
                piece.run(0)

    @pl.when(step == last)
    def tail():
        factor, gain, scaled = (vec_ref[i : i + 1, :] for i in range(3))
        total = [jnp.zeros((1, width), f32) for unused in range(2)]

        def chunk(k):
            slot = partner(place.blk, k)
            rows = pl.ds(pl.multiple_of(slot * stretch, stretch), stretch)
            normed, inverse = norm_rows(x_ref[slot].astype(f32))
            dh = dh_s[rows, :]
            gt_s[slot] = (dx_ref[rows, :] + norm_back(dh * factor, normed, inverse)).astype(bf16)
            grads.start([k])
            total[0] = total[0] + jnp.sum(dh, axis=0, keepdims=True)
            total[1] = total[1] + jnp.sum(dh * normed, axis=0, keepdims=True)

        before, middle, after = late_pieces
        chunk(1)
        chunk(2)
        middle.run(3)
        after.run(1)
        chunk(3)
        chunk(0)
        late_s[...] = jnp.zeros_like(late_s)
        for i, row in enumerate((total[0], total[1] * gain, total[1] * scaled)):
            for group in range(width // LANES):
                at_row = i * (width // LANES) + group
                late_s[at_row : at_row + 1, :] = row[:, group * LANES : (group + 1) * LANES]
        late_b[...] = late_s[...].astype(bf16)
        late.run(0)
        after.run(2)
        late.run(1)
        middle.run(4)
        after.run(3)
        for number in range(12, 21):
            for action in plan.get(number, []):
                action()
        late.run(2)
        middle.run(5)
        after.run(4)
        early_out[...] = early_g[...]
        late_out[...] = late_g[...]
        after.run(5)
        results.finish()
        grads.finish()


def behind(q, k, v, grads, att, lse, fq, fk, cosine, sine, w_qkv, hidden_t, x, dx, vec, early, g_up, g_down, g_out,
           result, rows_dev, nrows, owners):
    seq, width = q.shape
    nblk, stretch, unused = x.shape
    n_up, nz, unused, share, cols = g_up.shape
    n_down, depth, dcols = g_down.shape[0], g_down.shape[-2], g_down.shape[-1]
    pair = pl.BlockSpec((seq, LANES), lambda i: (0, i))
    once = pl.Buffered(buffer_count=1)
    fixed = lambda a: pl.BlockSpec(a.shape, lambda i: (0,) * len(a.shape), pipeline_mode=once)
    away = pl.BlockSpec(memory_space=pl.ANY)
    per = width // (2 * LANES)
    weight = lambda n: pl.BlockSpec((width, 2 * LANES), lambda i: (0, n * per + i // 2))
    shape = jax.ShapeDtypeStruct
    back = (rows_dev, stretch, width)
    outs = [
        shape((share, 3 * width), f32), shape((share, cols), f32), shape((share, n_up * cols), f32),
        shape((8 * depth, dcols), f32), shape((nblk, nrows) + early.shape, bf16), shape((nblk, nrows, 32, LANES), bf16),
    ]
    row_bufs = RowPiece.scratch(nz, share, cols)
    col_bufs = ColPiece.scratch(nz, depth, dcols)
    sems = (n_up + 4) * RowPiece.SEMS + n_down * ColPiece.SEMS + 2 * nblk + 2 * (nblk + nrows)
    scratch = [
        pltpu.VMEM((seq, LANES), bf16), pltpu.VMEM((seq, LANES), bf16), pltpu.VMEM((2, seq, LANES), f32),
        pltpu.VMEM((seq, 6 * LANES), bf16), pltpu.VMEM((seq, width), f32),
        pltpu.VMEM((3, nz, 2, share, cols), bf16), pltpu.VMEM((nblk, stretch, width), bf16),
        pltpu.VMEM(early.shape, bf16), pltpu.VMEM((32, LANES), f32), pltpu.VMEM((32, LANES), bf16),
        pltpu.VMEM((nblk, nrows) + early.shape, bf16), pltpu.VMEM((nblk, nrows, 32, LANES), bf16),
        pltpu.VMEM((4, 2, depth, dcols), bf16),
        pltpu.VMEM((n_up, nz, share, cols), bf16), pltpu.VMEM((n_down, 2, 2, 2, depth, dcols), bf16),
        pltpu.VMEM((nz, share, cols), bf16),
        pltpu.SemaphoreType.DMA((sems,)), pltpu.SemaphoreType.DMA((sems,)),
        pltpu.SemaphoreType.DMA((3 + n_up + n_down,)),
    ] + row_bufs * n_up + col_bufs * n_down + row_bufs * 4
    return pl.pallas_call(
        functools.partial(behind_kernel, n_up, owners),
        grid=(width // LANES,),
        in_specs=[pair] * 6 + [fixed(fq), fixed(fk), fixed(cosine), fixed(sine), weight(0), weight(1), weight(2)]
        + [fixed(hidden_t), fixed(x), fixed(dx), fixed(vec), fixed(early)] + [away] * 4,
        out_specs=[away, away] + [pl.BlockSpec(o.shape, lambda i, n=len(o.shape): (0,) * n) for o in outs],
        out_shape=[shape(back, bf16), shape(back, bf16)] + outs,
        scratch_shapes=scratch,
        compiler_params=pltpu.CompilerParams(collective_id=2, has_side_effects=True, vmem_limit_bytes=62 * MIB),
        cost_estimate=pl.CostEstimate(
            flops=52 * seq * seq * width, bytes_accessed=40 * seq * width, transcendentals=H * seq * seq
        ),
    )(q, k, v, grads, att, lse, fq, fk, cosine, sine, w_qkv, w_qkv, w_qkv, hidden_t, x, dx, vec, early, g_up, g_down,
      g_out, result)


def rows_out(whole, rows, me, nblk):
    parts = [lax.dynamic_index_in_dim(whole, me, 0, keepdims=False)]
    for k in range(1, nblk):
        part = lax.dynamic_index_in_dim(whole, me ^ k, 0, keepdims=False)
        pairs = [(s, s ^ k) for s in range(nblk) if s < rows]
        parts.append(lax.ppermute(part, "blk", pairs))
    stacked = jnp.stack(parts)
    return jnp.take(stacked, jnp.arange(rows) ^ me, axis=0)


def pick(array, index, axis=0):
    return lax.dynamic_index_in_dim(array, index, axis, keepdims=False)


def xor_move(array, axis, size, k):
    return lax.ppermute(array, axis, [(s, s ^ k) for s in range(size)])


def halve(array, axis, bit, name, size, k):
    kept = pick(array, bit, axis).astype(f32)
    sent = pick(array, 1 - bit, axis)
    return (kept + xor_move(sent, name, size, k).astype(f32)).astype(bf16)


def reduce_weight(grad, blk, row, nblk, nrows):
    total, cols = grad.shape
    share = total // nrows
    nz = nrows // 2
    core, z = row % 2, row // 2
    x, y = blk % 2, blk // 2
    part = halve(grad.reshape(nz, 2, share, cols), 1, core, "rows", nrows, 1)
    part = part.reshape(nz, 2, share // 2, cols)
    front, back = part[: nz // 2], part[nz // 2 :]
    split = lambda a: jnp.stack([a[..., : cols // 2], a[..., cols // 2 :]])
    front = halve(split(front), 0, x, "blk", nblk, 1)
    back = halve(back, 1, y, "blk", nblk, 2)
    front = halve(front, 1, y, "blk", nblk, 2)
    back = halve(split(back), 0, x, "blk", nblk, 1)
    part = jnp.concatenate([front, back], axis=0)
    if nz <= 4:
        summed = pick(part, z).astype(f32)
        for k in range(1, nz):
            summed = summed + xor_move(pick(part, z ^ k), "rows", nrows, 2 * k).astype(f32)
        part = summed.astype(bf16)
    else:
        k = nz // 2
        while k:
            pairs = part.reshape((2, k) + part.shape[1:])
            part = halve(pairs, 0, (z // k) % 2, "rows", nrows, 2 * k)
            k //= 2
        part = part[0]
    quarters = [part] + [xor_move(part, "blk", nblk, k) for k in range(1, 4)]
    quarters = jnp.take(jnp.stack(quarters), jnp.arange(4) ^ blk, axis=0)
    ordered = quarters.reshape(2, 2, share // 2, cols // 2).transpose(0, 2, 1, 3)
    return ordered.reshape(share, cols).astype(f32)


def per_device(
    tokens, timesteps, lengths, time_table, w_ada, b_ada, gain_attn, w_qkv, w_out, gain_mlp, w_up, b_up,
    w_down, b_down, grad_out
):
    rows_dev, stretch, width = tokens.shape
    nblk, nrows = lax.axis_size("blk"), lax.axis_size("rows")
    blk, row = lax.axis_index("blk"), lax.axis_index("rows")
    seq = stretch * nblk
    head_dim = width // H
    mine = jnp.minimum(blk, rows_dev - 1)

    slots = jnp.arange(seq, dtype=jnp.int32)
    ends = jnp.cumsum(pick(lengths, mine))
    before = ends[None, :] <= slots[:, None]
    doc = jnp.sum(before.astype(jnp.int32), axis=-1)
    place = slots - jnp.max(jnp.where(before, ends[None, :], 0), axis=-1)
    freqs = 10000.0 ** (-jnp.arange(head_dim // 2, dtype=f32) * 2.0 / head_dim)
    angle = place.astype(f32)[:, None] * freqs
    cosine, sine = jnp.cos(angle), jnp.sin(angle)
    cosine = jnp.concatenate([cosine] * 4, axis=-1)
    sine = jnp.concatenate([-sine, sine] * 2, axis=-1)
    lane = jnp.arange(LANES) % head_dim
    here = lane[None, :] == doc[:, None]
    fq = jnp.where(here, -1e30, 0.0).astype(bf16)
    fk = jnp.where(here | (lane >= NDOC + 3)[None, :], 0.0, 1.0).astype(bf16)

    table = time_table.astype(f32)
    ada_full = w_ada.astype(f32)
    step = pick(timesteps, mine)
    cond = pick(table, step)[None, :]
    modulate = jnp.dot(jax.nn.silu(cond), ada_full, precision=highest) + b_ada.astype(f32)
    shift_a, scale_a, gate_a, shift_m, scale_m, gate_m = jnp.split(modulate, 6, axis=-1)
    gain_a = gain_attn.astype(f32)
    gain_m = gain_mlp.astype(f32)
    factor_a = gain_a * (1.0 + scale_a)
    factor_m = gain_m * (1.0 + scale_m)

    vec = jnp.concatenate([factor_a, shift_a], axis=0)
    x_blocks, g_blocks, hidden_a, hidden_t, q, k, v, attended, lse, attended_b = ahead(
        tokens, grad_out, vec, w_qkv, cosine, sine, fq, fk, nblk
    )
    x_row = x_blocks.reshape(seq, width)

    g_row = g_blocks.reshape(seq, width)
    vec = jnp.concatenate([gate_a, factor_m, shift_m, gate_m], axis=0)
    result, grad_mid, grad_att, grad_w_out, grad_w_up, grad_w_down, gb_up, sums = feed(
        attended_b, x_row, g_row, vec, w_out, w_up, b_up.astype(f32)[None, :], w_down,
        b_down.astype(f32)[None, :]
    )
    result = result.reshape(nblk, stretch, width)
    dgate_m, dshift_m, along_m, dgate_a, grad_b_down = (sums[i] for i in range(5))
    ff = b_up.shape[0]
    early = jnp.concatenate(
        [
            dgate_a, dshift_m, along_m * gain_m, dgate_m, along_m * (1.0 + scale_m[0]), grad_b_down, gb_up[0],
            jnp.broadcast_to(step.astype(f32), (LANES,)),
        ]
    )
    count = early.shape[0]

    if (nblk, nrows) == (4, 8):
        rows_early = -(-count // (16 * LANES)) * 16
        early = jnp.pad(early, (0, rows_early * LANES - count)).reshape(rows_early, LANES).astype(bf16)
        vec = jnp.concatenate([factor_a, gain_a[None, :], 1.0 + scale_a], axis=0)
        nf, nz, share = grad_w_up.shape[0], nrows // 2, width // nrows
        out, grad_tokens, share_w_qkv, share_w_out, share_w_up, share_w_down, early, late = behind(
            q, k, v, grad_att, attended, lse, fq, fk, cosine, sine, w_qkv, hidden_t, x_blocks, grad_mid, vec, early,
            grad_w_up.reshape(nf, nz, 2, share, -1), grad_w_down.reshape(nf, 2, 2, 2, 2, width // 8, -1),
            grad_w_out.reshape(nz, 2, share, width), result, rows_dev, nrows, tuple(range(nf)),
        )
        share_w_down = share_w_down.T
        early = early.reshape(nblk, nrows, -1)[:rows_dev].reshape(rows_dev * nrows, -1).astype(f32)
        late = late.reshape(nblk, nrows, -1)[:rows_dev].reshape(rows_dev * nrows, -1).astype(f32)
        dshift_a, dscale_a, part_gain_a = (late[:, i * width : (i + 1) * width] for i in range(3))
    else:
        out = rows_out(result, rows_dev, blk, nblk)
        share_w_down = reduce_weight(grad_w_down.transpose(2, 0, 1, 3).reshape(width, ff).T, blk, row, nblk, nrows)
        share_w_up = reduce_weight(grad_w_up.transpose(1, 0, 2).reshape(width, ff), blk, row, nblk, nrows)
        share_w_out = reduce_weight(grad_w_out, blk, row, nblk, nrows)
        dq, dk, dv = attend_back(q, k, v, grad_att, attended, lse, fq, fk, cosine, sine)
        grad_qkv = jnp.concatenate([dq, dk, dv], axis=-1)
        grad_w_qkv = dot(hidden_t, grad_qkv).astype(bf16)
        share_w_qkv = reduce_weight(grad_w_qkv, blk, row, nblk, nrows)
        grad_ha = dot_nt(grad_qkv, w_qkv)
        normed_a, inverse_a = norm_rows(x_row.astype(f32))
        along_a = jnp.sum(grad_ha * normed_a, axis=0)
        grad_in = (grad_mid + norm_back(grad_ha * factor_a, normed_a, inverse_a)).astype(bf16)
        grad_tokens = rows_out(grad_in.reshape(nblk, stretch, width), rows_dev, blk, nblk)
        packed = jnp.concatenate(
            [early, jnp.sum(grad_ha, axis=0), along_a * gain_a, along_a * (1.0 + scale_a[0])]
        )
        gathered = gather_all(packed, nblk, nrows).reshape(nblk, nrows, -1)
        early = gathered[:rows_dev].reshape(rows_dev * nrows, -1)
        dshift_a, dscale_a, part_gain_a = (early[:, count + i * width : count + (i + 1) * width] for i in range(3))

    grad_mod = jnp.concatenate([dshift_a, dscale_a, early[:, : 4 * width]], axis=-1)
    smalls = jnp.sum(early, axis=0)
    grad_gain_m, total_b_down = smalls[4 * width : 5 * width], smalls[5 * width : 6 * width]
    total_b_up = smalls[6 * width : 6 * width + ff]
    steps = early[:, 6 * width + ff].astype(jnp.int32)
    onehot = (steps[:, None] == jnp.arange(table.shape[0], dtype=jnp.int32)[None, :]).astype(f32)
    conds = jnp.dot(onehot, table, precision=highest)
    share = conds.shape[1] // nrows
    my_conds = lax.dynamic_slice_in_dim(conds, row * share, share, axis=1)
    grad_w_ada = jnp.dot(jax.nn.silu(my_conds).T, grad_mod, precision=highest)
    grad_cond_act = lax.dot_general(
        grad_mod, ada_full, (((1,), (1,)), ((), ())), precision=highest, preferred_element_type=f32
    )
    sigmoid = jax.nn.sigmoid(conds)
    grad_cond = grad_cond_act * sigmoid * (1.0 + conds * (1.0 - sigmoid))
    grad_table = jnp.dot(onehot.T, grad_cond, precision=highest)
    return (
        out,
        grad_tokens,
        grad_table,
        grad_w_ada,
        jnp.sum(grad_mod, axis=0),
        jnp.sum(part_gain_a, axis=0),
        share_w_qkv,
        share_w_out,
        grad_gain_m,
        share_w_up,
        total_b_up,
        share_w_down,
        total_b_down,
    )


def solution(mesh):
    whole, split = P(), P("rows", None)
    tokens = P("rows", "blk", None)
    return jax.shard_map(
        per_device,
        mesh=mesh,
        in_specs=(tokens, P("rows"), split) + (whole,) * 11 + (tokens,),
        out_specs=(
            tokens, tokens, whole, split, whole, whole, split, split, whole, split, whole, split, whole
        ),
        check_vma=False,
    )
```

```python
import functools
import math
import types

import jax
import jax.numpy as jnp
import numpy as np
from jax import lax
from jax.experimental import pallas as pl
from jax.experimental.pallas import tpu as pltpu
from jax.sharding import PartitionSpec as P

H = 12
NDOC = 8
LANES = 128
CHUNK = 256
MIB = 1 << 20

epsilon = 1e-05
highest = lax.Precision.HIGHEST
bf16 = jnp.bfloat16
f32 = jnp.float32
MESH = pl.DeviceIdType.MESH


def dot(a, b):
    return jnp.dot(a, b, preferred_element_type=f32)


def dot_nt(a, b):
    return lax.dot_general(a, b, (((1,), (1,)), ((), ())), preferred_element_type=f32)


def dot_tn(a, b):
    return lax.dot_general(a, b, (((0,), (0,)), ((), ())), preferred_element_type=f32)


def norm_rows(values):
    centre = jnp.mean(values, axis=-1, keepdims=True)
    centred = values - centre
    spread = jnp.mean(centred * centred, axis=-1, keepdims=True)
    inverse = lax.rsqrt(spread + epsilon)
    return (centred * inverse, inverse)


def norm_back(grad_normed, normed, inverse):
    first = jnp.mean(grad_normed, axis=-1, keepdims=True)
    second = jnp.mean(grad_normed * normed, axis=-1, keepdims=True)
    return inverse * (grad_normed - first - normed * second)


def lane_of(shape):
    return lax.broadcasted_iota(jnp.int32, shape, len(shape) - 1)


def swap_halves(values, half):
    lane = lane_of(values.shape)
    width = values.shape[-1]
    ahead = pltpu.roll(values, width - half, values.ndim - 1)
    behind = pltpu.roll(values, half, values.ndim - 1)
    return jnp.where(lane % (2 * half) < half, ahead, behind)


def in_three(values):
    high = values.astype(bf16)
    rest = values - high.astype(f32)
    middle = rest.astype(bf16)
    low = (rest - middle.astype(f32)).astype(bf16)
    return (high, middle, low)


def partner(blk, k):
    other = blk
    bit = 1
    while bit <= k:
        if k & bit:
            other = other + bit - 2 * bit * (other // bit % 2)
        bit *= 2
    return other


def remote(source, target, send, recv, blk, row):
    return pltpu.make_async_remote_copy(
        src_ref=source, dst_ref=target, send_sem=send, recv_sem=recv, device_id=(blk, row), device_id_type=MESH
    )


class Vec:
    shift_a, scale_a, gate_a, shift_m, scale_m, gate_m, factor_a, factor_m, gain_a, gain_m, step, b_down, b_up = range(13)


def silu(values):
    return values / (1.0 + jnp.exp(-values))


def ahead_kernel(
    tok_ref, grad_ref, w_ref, ada_ref, lengths_ref, steps_ref, table_ref, b_ada_ref, gain_a_ref, gain_m_ref, b_down_ref, b_up_ref, freq_ref,
    x_out, g_out, ht_out, q_out, k_out, v_out, cos_out, sin_out, att_ref, inv_ref, ab_ref, eb_ref, vec_ref,
    x_s, own_s, ht_s, q_s, k_s, v_s, cos_s, sin_s, w_s, ada_s, fq_s, fk_s, zero_s, send_x, recv_x, send_g, recv_g, local
):
    step, last = pl.program_id(0), pl.num_programs(0) - 1
    blk, row = lax.axis_index("blk"), lax.axis_index("rows")
    rows_dev, stretch, width = tok_ref.shape
    nblk = x_s.shape[0]
    half = width // H // 2
    scale = 1.0 / math.sqrt(2 * half)
    has_row = blk < rows_dev
    mine = jnp.minimum(blk, rows_dev - 1)
    kept = (
        (x_s, x_out), (ht_s, ht_out), (q_s, q_out), (k_s, k_out), (v_s, v_out), (cos_s, cos_out), (sin_s, sin_out)
    )
    free = len(kept)

    def move(k, source, target, send, recv, other):
        return remote(source.at[jnp.minimum(other, rows_dev - 1)], target.at[blk], send.at[k], recv.at[k], other, row)

    def each_sent(source, target, send, recv, what):
        for k in range(1, nblk):
            other = partner(blk, k)

            @pl.when(other < rows_dev)
            def sent():
                what(move(k, source, target, send, recv, other))

    def store(i):
        return pltpu.make_async_copy(kept[i][0], kept[i][1], local.at[i])

    def own_grad():
        return pltpu.make_async_copy(grad_ref.at[mine], g_out.at[blk], local.at[free + 3])

    def chunk(source):
        rows = pl.ds(pl.multiple_of(source * stretch, stretch), stretch)
        normed, unused = norm_rows(x_s[source].astype(f32))
        hidden = normed * vec(Vec.factor_a) + vec(Vec.shift_a)
        hidden_b = hidden.astype(bf16)
        ht_s[:, rows] = hidden.T.astype(bf16)
        cosine, sine = cos_s[rows, :], sin_s[rows, :]
        for part in range(3):
            out = dot(hidden_b, w_s[:, part * width : (part + 1) * width])
            for group in range(width // LANES):
                cols = slice(group * LANES, (group + 1) * LANES)
                piece = out[:, cols]
                if part == 2:
                    v_s[rows, cols] = piece.astype(bf16)
                    continue
                turned = (piece * cosine + swap_halves(piece, half) * sine).astype(bf16)
                if part == 0:
                    q_s[rows, cols] = (turned.astype(f32) * scale).astype(bf16)
                else:
                    k_s[rows, cols] = turned

    def vec(at):
        return vec_ref[at : at + 1, :]

    def prepare():
        wide = table_ref.shape[0]
        time = steps_ref[mine]
        hot = (lane_of((16, wide)) == time).astype(f32).astype(bf16)
        terms = in_three(silu(dot(hot, table_ref[...])))
        line = lax.broadcasted_iota(jnp.int32, (16, 1), 0)
        three = jnp.zeros(terms[0].shape, f32)
        for i, term in enumerate(terms):
            three = jnp.where(line == i, term.astype(f32), three)
        modulate = jnp.sum(dot(three.astype(bf16), ada_s[...]), axis=0, keepdims=True)
        flat = lambda ref: jnp.concatenate([ref[i : i + 1, :] for i in range(ref.shape[0])], axis=1).astype(f32)
        modulate = modulate + flat(b_ada_ref)
        gains = [flat(gain_a_ref), flat(gain_m_ref)]
        rows = [modulate[:, i * width : (i + 1) * width] for i in range(6)]
        rows += [gains[0] * (1.0 + rows[1]), gains[1] * (1.0 + rows[4])] + gains
        rows += [jnp.full((1, width), time, jnp.int32).astype(f32), flat(b_down_ref)]
        b_up = flat(b_up_ref)
        rows += [b_up[:, i * width : (i + 1) * width] for i in range(b_up.shape[1] // width)]
        vec_ref[...] = jnp.zeros_like(vec_ref)
        for i, value in enumerate(rows):
            vec_ref[i : i + 1, :] = value
        shape = fq_s.shape
        slots = lax.broadcasted_iota(jnp.int32, shape, 0)
        feature = lane_of(shape) % (2 * half)
        doc, start = jnp.zeros(shape, jnp.int32), jnp.zeros(shape, jnp.int32)
        last_end = jnp.int32(0)
        for i in range(lengths_ref.shape[1]):
            last_end = last_end + lengths_ref[mine, i]
            past = slots >= last_end
            doc = doc + past.astype(jnp.int32)
            start = jnp.where(past, last_end, start)
        fq_s[...] = jnp.where(feature == doc, -1e30, 0.0).astype(bf16)
        fk_s[...] = jnp.where((feature == doc) | (feature >= NDOC), 0.0, 1.0).astype(bf16)
        angle = (slots - start).astype(f32) * freq_ref[...]
        cos_s[...] = jnp.cos(angle)
        sine = jnp.sin(angle)
        sin_s[...] = jnp.where(feature < half, -sine, sine)

    @pl.when(step == 0)
    def begin():
        barrier = pltpu.get_barrier_semaphore()
        for k in range(1, nblk):
            pl.semaphore_signal(barrier, inc=1, device_id=(partner(blk, k), row), device_id_type=MESH)
        ada = pltpu.make_async_copy(ada_ref, ada_s, local.at[free])
        weights = pltpu.make_async_copy(w_ref, w_s, local.at[free + 1])
        own = pltpu.make_async_copy(tok_ref.at[mine], own_s, local.at[free + 2])
        for copy in (ada, weights, own):
            copy.start()
        pl.semaphore_wait(barrier, nblk - 1)
        each_sent(tok_ref, x_s, send_x, recv_x, lambda copy: copy.start())
        ada.wait()
        prepare()
        own.wait()

        @pl.when(has_row)
        def mine_first():
            x_s[blk] = own_s[...]

        @pl.when(jnp.logical_not(has_row))
        def nothing():
            x_s[...] = jnp.zeros_like(x_s)

        weights.wait()
        for k in range(nblk):
            source = partner(blk, k)
            if k:
                @pl.when(has_row)
                def arrived():
                    move(k, tok_ref, x_s, send_x, recv_x, source).wait_recv()

            chunk(source)
        each_sent(tok_ref, x_s, send_x, recv_x, lambda copy: copy.wait_send())
        each_sent(grad_ref, g_out, send_g, recv_g, lambda copy: copy.start())
        zero_s[...] = jnp.zeros_like(zero_s)

        @pl.when(has_row)
        def own_part():
            own_grad().start()

        @pl.when(jnp.logical_not(has_row))
        def no_part():
            for i in range(nblk):
                pltpu.make_async_copy(zero_s, g_out.at[i], local.at[free + 4 + i]).start()

        for i in range(len(kept)):
            store(i).start()

    cols = pl.ds(pl.multiple_of(step * LANES, LANES), LANES)
    seq = q_s.shape[0]
    first = lane_of((1, LANES)) < LANES // 2
    owns = (first, jnp.logical_not(first))
    one = jnp.ones((), bf16)
    keys = [jnp.where(own, k_s[:, cols], fk_s[...]) for own in owns]
    values = [jnp.where(own, v_s[:, cols], one) for own in owns]

    def score_of(start, head):
        rows = slice(start, start + CHUNK)
        return dot_nt(jnp.where(owns[head], q_s[rows, cols], fq_s[rows, :]), keys[head])

    items = [(start, head) for start in range(0, seq, CHUNK) for head in range(2)]
    ahead_score = score_of(*items[0])
    pieces = [None, None]
    for number, (start, head) in enumerate(items):
        score = ahead_score
        if number + 1 < len(items):
            ahead_score = score_of(*items[number + 1])
        rows = slice(start, start + CHUNK)
        top = jnp.max(score, axis=-1, keepdims=True)
        weight = jnp.exp(score - top).astype(bf16)
        eb_ref[0, head, rows, :] = weight
        mixed = dot(weight, values[head])
        inverse = 1.0 / pltpu.roll(mixed, LANES // 2, 1)
        pieces[head] = (mixed * inverse, inverse)
        if head == 1:
            attended = jnp.where(first, pieces[0][0], pieces[1][0])
            att_ref[rows, :] = attended
            ab_ref[rows, :] = attended.astype(bf16)
            inv_ref[rows, :] = jnp.where(first, pieces[0][1], pieces[1][1])

    @pl.when(step == last)
    def end():
        for i in range(len(kept)):
            store(i).wait()
        each_sent(grad_ref, g_out, send_g, recv_g, lambda copy: copy.wait_send())

        @pl.when(has_row)
        def received():
            own_grad().wait()
            for k in range(1, nblk):
                move(k, grad_ref, g_out, send_g, recv_g, partner(blk, k)).wait_recv()

        @pl.when(jnp.logical_not(has_row))
        def cleared():
            for i in range(nblk):
                pltpu.make_async_copy(zero_s, g_out.at[i], local.at[free + 4 + i]).wait()


def lines_of(vector):
    return vector.reshape(-1, LANES)


def ahead(tokens, grads, w_qkv, w_ada, lengths, timesteps, table, b_ada, gain_a, gain_m, b_down, b_up, nblk):
    rows_dev, stretch, width = tokens.shape
    seq = nblk * stretch
    head_dim = width // H
    freqs = np.float32(10000.0) ** (-np.arange(head_dim // 2, dtype=np.float32) * np.float32(2.0 / head_dim))
    freqs = np.concatenate([freqs] * 4)[None, :]
    small = [table, *(lines_of(a) for a in (b_ada, gain_a, gain_m, b_down, b_up)), freqs]
    pair = pl.BlockSpec((seq, LANES), lambda i: (0, i))
    fixed = lambda a: pl.BlockSpec(a.shape, lambda i: (0, 0), pipeline_mode=pl.Buffered(buffer_count=1))
    away = pl.BlockSpec(memory_space=pl.ANY)
    numbers = pl.BlockSpec(memory_space=pltpu.SMEM)
    blocks, flat, turn = (nblk, stretch, width), (seq, width), (seq, LANES)
    shape = jax.ShapeDtypeStruct
    vec = (16, width)
    return pl.pallas_call(
        ahead_kernel,
        grid=(width // LANES,),
        in_specs=[away] * 4 + [numbers] * 2 + [fixed(a) for a in small],
        out_specs=[away] * 8 + [pair] * 3
        + [pl.BlockSpec((1, 2, seq, seq), lambda i: (i, 0, 0, 0)), pl.BlockSpec(vec, lambda i: (0, 0))],
        out_shape=[
            shape(blocks, bf16), shape(blocks, bf16), shape(flat[::-1], bf16),
            shape(flat, bf16), shape(flat, bf16), shape(flat, bf16), shape(turn, f32), shape(turn, f32),
            shape(flat, f32), shape(flat, f32), shape(flat, bf16), shape((width // LANES, 2, seq, seq), bf16),
            shape(vec, f32),
        ],
        scratch_shapes=[
            pltpu.VMEM(blocks, bf16), pltpu.VMEM((stretch, width), bf16), pltpu.VMEM(flat[::-1], bf16),
            pltpu.VMEM(flat, bf16), pltpu.VMEM(flat, bf16), pltpu.VMEM(flat, bf16),
            pltpu.VMEM(turn, f32), pltpu.VMEM(turn, f32), pltpu.VMEM(w_qkv.shape, bf16), pltpu.VMEM(w_ada.shape, bf16),
            pltpu.VMEM(turn, bf16), pltpu.VMEM(turn, bf16), pltpu.VMEM((stretch, width), bf16),
        ] + [pltpu.SemaphoreType.DMA((nblk,))] * 4 + [pltpu.SemaphoreType.DMA((11 + nblk,))],
        compiler_params=pltpu.CompilerParams(
            collective_id=1, has_side_effects=True, vmem_limit_bytes=60 * MIB
        ),
        cost_estimate=pl.CostEstimate(
            flops=22 * seq * seq * width, bytes_accessed=24 * seq * width, transcendentals=H * seq * seq
        ),
    )(tokens, grads, w_qkv, w_ada, lengths, timesteps, *small)


def attend_back_pair(r, store):
    seq = r.q.shape[0]
    half = LANES // 4
    scale = 1.0 / math.sqrt(2 * half)
    lane = lane_of((1, LANES))
    first = lane < 2 * half
    owns = (first, jnp.logical_not(first))
    where = lane % (2 * half)
    one = jnp.ones((), bf16)
    scaled = r.datt[...].astype(f32) * r.inv[...]
    both = scaled * r.att[...]
    scaled_b = scaled.astype(bf16)
    values = []
    for head, own in enumerate(owns):
        total = -jnp.sum(jnp.where(own, both, 0.0), axis=-1, keepdims=True)
        delta = in_three(jnp.broadcast_to(total, both.shape))
        feature = jnp.zeros_like(scaled_b)
        for i in range(3):
            feature = jnp.where(where == i, delta[i], feature)
        r.da[head] = jnp.where(own, scaled_b, feature)
        values.append(jnp.where(own, r.v[...], one))
    queries_t = r.q[...].astype(f32).T.astype(bf16)
    scaled_t = scaled_b.astype(f32).T.astype(bf16)

    def grad_prob(start, head):
        return dot_nt(r.da[head, start : start + CHUNK, :], values[head])

    items = [(start, head) for start in range(0, seq, CHUNK) for head in range(2)]
    ahead_grad = grad_prob(*items[0])
    grad_q = {}
    for number, (start, head) in enumerate(items):
        grad_p = ahead_grad
        if number + 1 < len(items):
            ahead_grad = grad_prob(*items[number + 1])
        rows = slice(start, start + CHUNK)
        grad_s = (r.eb[0, head, rows, :].astype(f32) * grad_p).astype(bf16)
        r.ds[head, rows, :] = grad_s
        grad_q[start, head] = dot(grad_s, r.k[...])
    upper = lax.broadcasted_iota(jnp.int32, (LANES, 1), 0) < 2 * half
    grad_k = [dot(queries_t, r.ds[head]) for head in range(2)]
    grad_v = [dot(scaled_t, r.eb[0, head]) for head in range(2)]
    grad_k = jnp.where(upper, grad_k[0], grad_k[1]).T
    grad_v = jnp.where(upper, grad_v[0], grad_v[1]).T
    for start in range(0, seq, CHUNK):
        rows = slice(start, start + CHUNK)
        cosine, sine = r.cos[rows, :], r.sin[rows, :]
        turned = []
        for grad in (jnp.where(first, grad_q[start, 0], grad_q[start, 1]) * scale, grad_k[rows, :]):
            turned.append((grad * cosine - swap_halves(grad, half) * sine).astype(bf16))
        store(rows, turned[0], turned[1], grad_v[rows, :].astype(bf16))


def attend_back_kernel(names, *refs):
    r = types.SimpleNamespace(**dict(zip(names, refs)))

    def store(rows, *grads):
        for ref, grad in zip((r.dq, r.dk, r.dv), grads):
            ref[rows, :] = grad

    attend_back_pair(r, store)


def attend_back(q, k, v, grads, att, inv, eb, cosine, sine):
    seq, width = q.shape
    pair = pl.BlockSpec((seq, LANES), lambda i: (0, i))
    fixed = pl.BlockSpec((seq, LANES), lambda i: (0, 0))
    names = list(dict(q=0, k=0, v=0, datt=0, att=0, inv=0, eb=0, cos=0, sin=0, dq=0, dk=0, dv=0, da=0, ds=0))
    return pl.pallas_call(
        functools.partial(attend_back_kernel, names),
        grid=(width // LANES,),
        in_specs=[pair] * 6 + [pl.BlockSpec((1, 2, seq, seq), lambda i: (i, 0, 0, 0)), fixed, fixed],
        out_specs=[pair] * 3,
        out_shape=[jax.ShapeDtypeStruct((seq, width), bf16)] * 3,
        scratch_shapes=[pltpu.VMEM((2, seq, LANES), bf16), pltpu.VMEM((2, seq, seq), bf16)],
        compiler_params=pltpu.CompilerParams(vmem_limit_bytes=56 * MIB),
        cost_estimate=pl.CostEstimate(
            flops=32 * seq * seq * width, bytes_accessed=24 * seq * width + 2 * H * seq * seq, transcendentals=0
        ),
    )(q, k, v, grads, att, inv, eb, cosine, sine)


GELU = math.sqrt(2.0 / math.pi)
CUBE = 0.044715


def vec_rows(ref, *lines):
    return [ref[at : at + 1, :] for at in lines]


def feed_chunk(hidden, grad, w_up_ref, b_up, w_down_ref):
    u = dot(hidden, w_up_ref[...]) + b_up
    square = u * u
    turn = jnp.tanh(GELU * u * (1.0 + CUBE * square))
    half = 0.5 * (1.0 + turn)
    slope = half + (0.5 * GELU) * u * (1.0 - turn * turn) * (1.0 + 3.0 * CUBE * square)
    du = (dot_nt(grad, w_down_ref[...]) * slope).astype(bf16)
    return ((u * half).astype(bf16), du)


def feed_kernel(
    ab_ref, x_ref, g_ref, vec_ref, w_out_ref, w_up_ref, w_down_ref,
    result_ref, dx_ref, datt_ref, g_out_ref, g_up_ref, g_down_ref, gb_up_ref, sums_ref,
    h_s, ht_s, dz_s, dzt_s, y_s, z_s, dh_s, act_s, du_s, dyt_s
):
    step, last = pl.program_id(0), pl.num_programs(0) - 1
    seq, width = x_ref.shape
    wide = w_up_ref.shape[1]
    gate_a, factor_m, shift_m, gate_m, b_down = vec_rows(vec_ref, Vec.gate_a, Vec.factor_m, Vec.shift_m, Vec.gate_m, Vec.b_down)
    chunks = [slice(begin, begin + CHUNK) for begin in range(0, seq, CHUNK)]

    @pl.when(step == 0)
    def before():
        for rows in chunks:
            y = dot(ab_ref[rows, :], w_out_ref[...])
            y_s[rows, :] = y
            normed, unused = norm_rows(x_ref[rows, :].astype(f32) + gate_a * y)
            hidden = normed * factor_m + shift_m
            h_s[rows, :] = hidden.astype(bf16)
            ht_s[:, rows] = hidden.T.astype(bf16)
            grad = gate_m * g_ref[rows, :].astype(f32)
            dz_s[rows, :] = grad.astype(bf16)
            dzt_s[:, rows] = grad.T.astype(bf16)
        z_s[...] = jnp.zeros_like(z_s)
        dh_s[...] = jnp.zeros_like(dh_s)

    b_up = vec_ref[pl.ds(Vec.b_up + step, 1), :]
    bias_sum = jnp.zeros((1, wide), f32)
    for rows in chunks:
        act, du = feed_chunk(h_s[rows, :], dz_s[rows, :], w_up_ref, b_up, w_down_ref)
        act_s[rows, :] = act
        du_s[rows, :] = du
        bias_sum = bias_sum + jnp.sum(du.astype(f32), axis=0, keepdims=True)
        z_s[rows, :] += dot(act, w_down_ref[...])
        dh_s[rows, :] += dot_nt(du, w_up_ref[...])
    gb_up_ref[...] = bias_sum
    g_up_ref[0] = dot(ht_s[...], du_s[...]).astype(bf16)
    down = dot(dzt_s[...], act_s[...]).astype(bf16)
    g_down_ref[0, 0] = down[:, : wide // 2]
    g_down_ref[0, 1] = down[:, wide // 2 :]

    @pl.when(step == last)
    def after():
        sums = [jnp.zeros((1, width), f32) for unused in range(5)]
        for rows in chunks:
            y = y_s[rows, :]
            middle = x_ref[rows, :].astype(f32) + gate_a * y
            normed, inverse = norm_rows(middle)
            z = z_s[rows, :] + b_down
            result_ref[rows, :] = (middle + gate_m * z).astype(bf16)
            grad = g_ref[rows, :].astype(f32)
            dh = dh_s[rows, :]
            dx = grad + norm_back(dh * factor_m, normed, inverse)
            dx_ref[rows, :] = dx
            dy = gate_a * dx
            dyb = dy.astype(bf16)
            dyt_s[rows, :] = dyb
            datt_ref[rows, :] = dot_nt(dyb, w_out_ref[...]).astype(bf16)
            terms = (grad * z, dh, dh * normed, dx * y, dz_s[rows, :].astype(f32))
            sums = [a + jnp.sum(b, axis=0, keepdims=True) for a, b in zip(sums, terms)]
        g_out_ref[...] = dot_tn(ab_ref[...], dyt_s[...]).astype(bf16)
        for i in range(5):
            sums_ref[i : i + 1, :] = sums[i]


def feed(ab, x, g, vec, w_out, w_up, w_down):
    seq, width = x.shape
    ff = w_up.shape[1]
    wide = width
    fixed = lambda a: pl.BlockSpec(a.shape, lambda i: (0, 0))
    one = lambda shape: pl.BlockSpec(shape, lambda i: (0, 0))
    col = lambda r: pl.BlockSpec((r, wide), lambda i: (0, i))
    shape = jax.ShapeDtypeStruct
    return pl.pallas_call(
        feed_kernel,
        grid=(ff // wide,),
        in_specs=[
            fixed(ab), fixed(x), fixed(g), fixed(vec), fixed(w_out), col(width),
            pl.BlockSpec((wide, width), lambda i: (i, 0)),
        ],
        out_specs=[
            one((seq, width)), one((seq, width)), one((seq, width)), one((width, width)),
            pl.BlockSpec((1, width, wide), lambda i: (i, 0, 0)),
            pl.BlockSpec((1, 2, width, wide // 2), lambda i: (i, 0, 0, 0)), col(1), one((8, width)),
        ],
        out_shape=[
            shape((seq, width), bf16), shape((seq, width), f32), shape((seq, width), bf16),
            shape((width, width), bf16), shape((ff // wide, width, wide), bf16),
            shape((ff // wide, 2, width, wide // 2), bf16),
            shape((1, ff), f32), shape((8, width), f32),
        ],
        scratch_shapes=[
            pltpu.VMEM((seq, width), bf16), pltpu.VMEM((width, seq), bf16),
            pltpu.VMEM((seq, width), bf16), pltpu.VMEM((width, seq), bf16),
            pltpu.VMEM((seq, width), f32), pltpu.VMEM((seq, width), f32), pltpu.VMEM((seq, width), f32),
            pltpu.VMEM((seq, wide), bf16), pltpu.VMEM((seq, wide), bf16), pltpu.VMEM((seq, width), bf16),
        ],
        compiler_params=pltpu.CompilerParams(vmem_limit_bytes=60 * MIB),
        cost_estimate=pl.CostEstimate(
            flops=12 * seq * width * ff, bytes_accessed=30 * seq * width, transcendentals=seq * ff
        ),
    )(ab, x, g, vec, w_out, w_up, w_down)


def gather_kernel(nblk, nrows, in_ref, out_ref, send_r, recv_r, send_b, recv_b):
    blk, row = lax.axis_index("blk"), lax.axis_index("rows")
    barrier = pltpu.get_barrier_semaphore()
    for step in range(1, nblk):
        pl.semaphore_signal(
            barrier, inc=1, device_id=(lax.rem(blk + step, nblk), row), device_id_type=MESH
        )

    def greet(step, unused):
        pl.semaphore_signal(
            barrier, inc=1, device_id=(blk, lax.rem(row + step, nrows)), device_id_type=MESH
        )
        return unused

    lax.fori_loop(1, nrows, greet, 0)
    pl.semaphore_wait(barrier, nblk + nrows - 2)
    out_ref[blk, row] = in_ref[...]

    def over_rows(step):
        other = lax.rem(row + step, nrows)
        return pltpu.make_async_remote_copy(
            src_ref=in_ref,
            dst_ref=out_ref.at[blk, row],
            send_sem=send_r.at[step],
            recv_sem=recv_r.at[step],
            device_id=(blk, other),
            device_id_type=MESH,
        )

    def over_blk(step):
        other = lax.rem(blk + step, nblk)
        return pltpu.make_async_remote_copy(
            src_ref=out_ref.at[blk],
            dst_ref=out_ref.at[blk],
            send_sem=send_b.at[step],
            recv_sem=recv_b.at[step],
            device_id=(other, row),
            device_id_type=MESH,
        )

    def start(step, unused):
        over_rows(step).start()
        return unused

    def finish(step, unused):
        over_rows(step).wait()
        return unused

    lax.fori_loop(1, nrows, start, 0)
    lax.fori_loop(1, nrows, finish, 0)
    for step in range(1, nblk):
        over_blk(step).start()
    for step in range(1, nblk):
        over_blk(step).wait()


def gather_all(vector, nblk, nrows):
    count = vector.shape[0] // LANES
    return pl.pallas_call(
        functools.partial(gather_kernel, nblk, nrows),
        out_shape=jax.ShapeDtypeStruct((nblk, nrows, count, LANES), f32),
        in_specs=[pl.BlockSpec(memory_space=pltpu.VMEM)],
        out_specs=pl.BlockSpec(memory_space=pltpu.VMEM),
        scratch_shapes=[
            pltpu.SemaphoreType.DMA((nrows,)),
            pltpu.SemaphoreType.DMA((nrows,)),
            pltpu.SemaphoreType.DMA((nblk,)),
            pltpu.SemaphoreType.DMA((nblk,)),
        ],
        compiler_params=pltpu.CompilerParams(collective_id=0, has_side_effects=True),
    )(vector.reshape(count, LANES))


class Place:
    def __init__(self):
        self.blk, self.row = lax.axis_index("blk"), lax.axis_index("rows")
        self.x, self.y = self.blk % 2, self.blk // 2
        self.core, self.z = self.row % 2, self.row // 2

    def along_blk(self, k):
        return (partner(self.blk, k), self.row)

    def along_rows(self, k):
        return (self.blk, partner(self.row, k))


class Sems:
    def __init__(self, send, recv):
        self.send, self.recv, self.used = send, recv, 0

    def take(self, count):
        self.used += count
        return self.used - count

    def copy(self, index, source, target, device):
        return remote(source, target, self.send.at[index], self.recv.at[index], *device)


def part(index, size, step):
    return pl.ds(pl.multiple_of(index * size, step), size)


class Piece:
    def __init__(self, place, sems, dims, bufs, whole=None, own=None, store=None):
        self.p, self.sems, self.base = place, sems, sems.take(self.SEMS)
        self.whole, self.own, self.store = whole, own, store
        self.b = types.SimpleNamespace(**bufs)
        self.nz, share, cols = dims
        self.hs, self.hc, self.hz = share // 2, cols // 2, self.nz // 2

    def start(self, stage):
        for copy in self.copies(stage):
            copy.start()

    def wait(self, stage):
        for copy in self.copies(stage):
            copy.wait()

    def run(self, stage, go_on=True):
        if stage:
            self.wait(stage - 1)
            self.add(stage)
        if stage < 5 and go_on:
            self.start(stage)


ROW_BUFS = ("core", "a1", "b1", "a2", "b2", "r3", "zr", "ag")
FAR_BUFS = ("core", "z1", "z2", "pr", "ag")


def shapes_of(names, shapes):
    return {name: pltpu.VMEM(shape, bf16) for name, shape in zip(names, shapes)}


class RowPiece(Piece):
    SEMS = 11

    @staticmethod
    def scratch(nz, share, cols):
        hs, hc = share // 2, cols // 2
        return shapes_of(
            ROW_BUFS,
            [
                (nz, share, cols), (nz // 2, share, hc), (nz // 2, hs, cols), (nz // 2, hs, hc), (nz // 2, hs, hc),
                (nz, hs, hc), (nz, hs, hc), (4, hs, hc),
            ],
        )

    def row(self, y):
        return part(y, self.hs, 16)

    def col(self, x):
        return part(x, self.hc, LANES)

    def copies(self, stage):
        p, at, b, copy = self.p, self.base, self.b, self.sems.copy
        low, high = slice(0, self.hz), slice(self.hz, self.nz)
        if stage == 0:
            return [copy(at, self.whole.at[:, 1 - p.core], b.core, p.along_rows(1))]
        if stage == 1:
            return [
                copy(at + 1, b.core.at[low, :, self.col(1 - p.x)], b.a1, p.along_blk(1)),
                copy(at + 2, b.core.at[high, self.row(1 - p.y), :], b.b1, p.along_blk(2)),
            ]
        if stage == 2:
            return [
                copy(at + 3, b.a1.at[:, self.row(1 - p.y), :], b.a2, p.along_blk(2)),
                copy(at + 4, b.b1.at[:, :, self.col(1 - p.x)], b.b2, p.along_blk(1)),
            ]
        if stage == 3:
            return [
                copy(at + 4 + k, b.r3.at[partner(p.z, k)], b.zr.at[p.z], p.along_rows(2 * k))
                for k in range(1, self.nz)
            ]
        return [copy(at + 7 + k, b.ag.at[p.blk], b.ag.at[p.blk], p.along_blk(k)) for k in range(1, 4)]

    def add(self, stage):
        p, b = self.p, self.b
        row, col = self.row(p.y), self.col(p.x)
        if stage == 1:
            b.core[...] = b.core[...] + self.own()
        if stage == 2:
            b.a1[...] = b.a1[...] + b.core[: self.hz, :, col]
            b.b1[...] = b.b1[...] + b.core[self.hz :, row, :]
        if stage == 3:
            b.r3[: self.hz] = b.a1[:, row, :] + b.a2[...]
            b.r3[self.hz :] = b.b1[:, :, col] + b.b2[...]
        if stage == 4:
            total = b.r3[p.z].astype(f32)
            for k in range(1, self.nz):
                total = total + b.zr[partner(p.z, k)].astype(f32)
            b.ag[p.blk] = total.astype(bf16)
        if stage == 5:
            for q in range(4):
                rows = slice(q // 2 * self.hs, (q // 2 + 1) * self.hs)
                self.store(rows, q % 2 * self.hc, b.ag[q])


class FarPiece(Piece):
    SEMS = 9

    @staticmethod
    def scratch(nz, share, cols):
        hs, hc = share // 2, cols // 2
        return shapes_of(
            FAR_BUFS,
            [(nz, share, cols), (nz // 2, share, cols), (share, cols), (4, hs, hc), (4, hs, hc)],
        )

    def quarter(self, blk):
        return (part(blk // 2, self.hs, 16), part(blk % 2, self.hc, LANES))

    def copies(self, stage):
        p, at, b, copy = self.p, self.base, self.b, self.sems.copy
        low, high = p.z % 2, p.z // 2
        if stage == 0:
            return [copy(at, self.whole.at[:, 1 - p.core], b.core, p.along_rows(1))]
        if stage == 1:
            return [
                copy(at + 1, b.core.at[1 - low], b.z1.at[0], p.along_rows(2)),
                copy(at + 2, b.core.at[3 - low], b.z1.at[1], p.along_rows(2)),
            ]
        if stage == 2:
            return [copy(at + 3, b.z1.at[1 - high], b.z2, p.along_rows(4))]
        if stage == 3:
            return [
                copy(at + 3 + k, b.z2.at[self.quarter(partner(p.blk, k))], b.pr.at[p.blk], p.along_blk(k))
                for k in range(1, 4)
            ]
        return [copy(at + 3 + k, b.ag.at[p.blk], b.ag.at[p.blk], p.along_blk(k)) for k in range(1, 4)]

    def add(self, stage):
        p, b = self.p, self.b
        low, high = p.z % 2, p.z // 2
        if stage == 1:
            b.core[...] = b.core[...] + self.own()
        if stage == 2:
            for i in range(2):
                b.z1[i] = b.z1[i] + b.core[2 * i + low]
        if stage == 3:
            b.z2[...] = b.z2[...] + b.z1[high]
        if stage == 4:
            rows, cols = self.quarter(p.blk)
            total = b.z2[rows, cols].astype(f32)
            for k in range(1, 4):
                total = total + b.pr[partner(p.blk, k)].astype(f32)
            b.ag[p.blk] = total.astype(bf16)
        if stage == 5:
            for q in range(4):
                rows = slice(q // 2 * self.hs, (q // 2 + 1) * self.hs)
                self.store(rows, q % 2 * self.hc, b.ag[q])


class ColPiece(Piece):
    SEMS = 12

    @staticmethod
    def scratch(nz, depth, cols):
        return shapes_of(
            ROW_BUFS[:6],
            [
                (2, 2, 2, depth, cols), (2, depth, cols), (2, depth, cols), (depth, cols), (depth, cols),
                (2, depth, cols),
            ],
        )

    @staticmethod
    def shared(nz, depth, cols):
        return shapes_of(("zr", "ag"), [(nz, 2, depth, cols), (4, 2, depth, cols)])

    def __init__(self, place, sems, dims, bufs, owner, **kinds):
        super().__init__(place, sems, dims, bufs, **kinds)
        self.owner = owner
        self.depth = dims[1]

    def copies(self, stage):
        p, at, b, copy = self.p, self.base, self.b, self.sems.copy
        if stage == 0:
            return [copy(at, self.whole.at[1 - p.core], b.core, p.along_rows(1))]
        if stage == 1:
            return [
                copy(at + 1, b.core.at[:, 1 - p.x, 0], b.a1, p.along_blk(1)),
                copy(at + 2, b.core.at[1 - p.y, :, 1], b.b1, p.along_blk(2)),
            ]
        if stage == 2:
            return [
                copy(at + 3, b.a1.at[1 - p.y], b.a2, p.along_blk(2)),
                copy(at + 4, b.b1.at[1 - p.x], b.b2, p.along_blk(1)),
            ]
        return [copy(at + 8 + k, b.ag.at[p.blk], b.ag.at[p.blk], p.along_blk(k)) for k in range(1, 4)]

    def over_z(self, k):
        device = (self.p.blk, 2 * self.owner + self.p.core)
        return self.sems.copy(self.base + 5 + k, self.b.r3, self.b.zr.at[self.p.z], device)

    def from_afar(self, k, what):
        @pl.when(self.p.z == self.owner ^ k)
        def far():
            what(self.over_z(k))

    def here(self, what):
        @pl.when(self.p.z == self.owner)
        def at_owner():
            what()

    def start(self, stage):
        if stage == 3:
            for k in range(1, 4):
                self.from_afar(k, lambda copy: copy.start())
        elif stage == 4:
            self.here(lambda: [copy.start() for copy in self.copies(4)] and None)
        else:
            super().start(stage)

    def wait(self, stage):
        if stage == 3:
            for k in range(1, 4):
                self.from_afar(k, lambda copy: copy.wait_send())
            self.here(lambda: [self.over_z(k).wait_recv() for k in range(1, 4)] and None)
        elif stage == 4:
            self.here(lambda: [copy.wait() for copy in self.copies(4)] and None)
        else:
            super().wait(stage)

    def add(self, stage):
        p, b = self.p, self.b
        if stage == 1:
            b.core[...] = b.core[...] + self.own()
        if stage == 2:
            b.a1[...] = b.a1[...] + b.core[:, p.x, 0]
            b.b1[...] = b.b1[...] + b.core[p.y, :, 1]
        if stage == 3:
            b.r3[0] = b.a1[p.y] + b.a2[...]
            b.r3[1] = b.b1[p.x] + b.b2[...]
        if stage == 4:
            def summed():
                total = b.r3[...].astype(f32)
                for k in range(1, 4):
                    total = total + b.zr[self.owner ^ k].astype(f32)
                b.ag[p.blk] = total.astype(bf16)
            self.here(summed)
        if stage == 5:
            def stored():
                for q in range(8):
                    self.store(slice(q * self.depth, (q + 1) * self.depth), b.ag[q // 2, q % 2])
            self.here(stored)


class Bag:
    def __init__(self):
        self.names, self.items = [], []

    def add(self, name, item):
        if isinstance(item, dict):
            for key, value in item.items():
                self.add(f"{name}.{key}", value)
        else:
            self.names.append(name)
            self.items.append(item)


def group(refs, name):
    return {key[len(name) + 1 :]: ref for key, ref in vars(refs).items() if key.startswith(name + ".")}


def only(shapes, names):
    return {name: shapes[name] for name in names if name in shapes}


class Plan:
    def __init__(self):
        self.actions = {}

    def at(self, point, *actions):
        self.actions.setdefault(point, []).extend(actions)

    def stages(self, piece, first, points):
        for number, point in enumerate(points):
            self.at(point, lambda number=first + number: piece.run(number))

    def run(self, point):
        for action in self.actions.get(point, []):
            action()

    def under(self, step, number, point):
        if point in self.actions:
            @pl.when(step == number)
            def actions():
                self.run(point)


EARLY, LATE = 64, 32


def write_lines(target, lines):
    target[...] = jnp.zeros_like(target)
    at = 0
    for line in lines:
        for k in range(line.shape[1] // LANES):
            target[at : at + 1, :] = line[:, k * LANES : (k + 1) * LANES]
            at += 1


FEED_POINTS = ((7, 11), (11, 16), (16,), ())
HANDED = {1: ("core",), 2: ("a1", "b1"), 3: ("r3",)}


def feed_move_kernel(names, *refs):
    r = types.SimpleNamespace(**dict(zip(names, refs)))
    step, last = pl.program_id(0), pl.num_programs(0) - 1
    place = Place()
    sems = Sems(r.send, r.recv)
    seq, width = r.x.shape
    wide = r.w_up.shape[1]
    nz, unused, share, cols = r.gu.shape[1:]
    depth, dcols = r.gd.shape[-2:]
    nrows = 2 * nz
    plan = Plan()

    ups, downs = [], []
    for i in range(4):
        side = i % 2
        ups.append(
            RowPiece(
                place, sems, (nz, share, cols), group(r, f"u{i}"), r.gu.at[side],
                lambda side=side: r.gu[side, :, place.core],
            )
        )
        bufs = group(r, f"d{i}")
        downs.append(
            ColPiece(
                place, sems, (nz, depth, dcols), bufs, i, whole=r.gd.at[side],
                own=lambda side=side: r.gd[side, place.core],
            )
        )
    for i, points in enumerate(FEED_POINTS):
        for kind, piece in (("up", ups[i]), ("down", downs[i])):
            plan.stages(piece, 1, points)
            if len(points) < 5:
                plan.at(20, lambda kind=kind, piece=piece, i=i, stage=len(points) + 1: hand_over(piece, stage, f"{kind}{i}"))

    def hand_over(piece, stage, name):
        piece.run(stage, False)
        for key in HANDED[stage]:
            getattr(r, f"{name}.{key}")[...] = getattr(piece.b, key)[...]

    gate_a, factor_m, shift_m, gate_m, b_down = vec_rows(r.vec, Vec.gate_a, Vec.factor_m, Vec.shift_m, Vec.gate_m, Vec.b_down)
    chunks = [slice(begin, begin + CHUNK) for begin in range(0, seq, CHUNK)]

    @pl.when(step == 0)
    def before():
        greet(place, 4, nrows)

        def enter(number, unused):
            rows = part(number, CHUNK, CHUNK)
            y = dot(r.ab[rows, :], r.w_out[...])
            r.y[rows, :] = y
            normed, unused = norm_rows(r.x[rows, :].astype(f32) + gate_a * y)
            hidden = normed * factor_m + shift_m
            r.h[rows, :] = hidden.astype(bf16)
            r.ht[:, rows] = hidden.T.astype(bf16)
            grad = gate_m * r.g[rows, :].astype(f32)
            r.dz[rows, :] = grad.astype(bf16)
            r.dzt[:, rows] = grad.T.astype(bf16)
            return 0

        lax.fori_loop(0, len(chunks), enter, 0)
        r.z[...] = jnp.zeros_like(r.z)
        r.dh[...] = jnp.zeros_like(r.dh)

    b_up = r.vec[pl.ds(Vec.b_up + step, 1), :]
    bias_sum = jnp.zeros((1, wide), f32)
    for number, rows in enumerate(chunks):
        for i in range(4):
            plan.under(step, i, 4 * i + number)
        act, du = feed_chunk(r.h[rows, :], r.dz[rows, :], r.w_up, b_up, r.w_down)
        r.act[rows, :] = act
        r.du[rows, :] = du
        bias_sum = bias_sum + jnp.sum(du.astype(f32), axis=0, keepdims=True)
        r.z[rows, :] += dot(act, r.w_down[...])
        r.dh[rows, :] += dot_nt(du, r.w_up[...])
    r.gb[pl.ds(step, 1), :] = bias_sum
    side = step % 2
    r.gu[side] = dot(r.ht[...], r.du[...]).astype(bf16).reshape(r.gu.shape[1:])
    down = dot(r.dzt[...], r.act[...]).astype(bf16)
    for core in range(2):
        half = down[:, core * dcols : (core + 1) * dcols]
        r.gd[side, core] = half.reshape(r.gd.shape[2:])
    for i in range(4):
        @pl.when(step == i)
        def sent():
            ups[i].run(0)
            downs[i].run(0)

    @pl.when(step == last)
    def after():
        plan.run(16)

        def leave(number, sums):
            rows = part(number, CHUNK, CHUNK)
            y = r.y[rows, :]
            middle = r.x[rows, :].astype(f32) + gate_a * y
            normed, inverse = norm_rows(middle)
            z = r.z[rows, :] + b_down
            r.result[rows, :] = (middle + gate_m * z).astype(bf16)
            grad = r.g[rows, :].astype(f32)
            dh = r.dh[rows, :]
            dx = grad + norm_back(dh * factor_m, normed, inverse)
            r.dx[rows, :] = dx
            dyb = (gate_a * dx).astype(bf16)
            r.dy[rows, :] = dyb
            r.datt[rows, :] = dot_nt(dyb, r.w_out[...]).astype(bf16)
            terms = (grad * z, dh, dh * normed, dx * y, r.dz[rows, :].astype(f32))
            return tuple(a + jnp.sum(b, axis=0, keepdims=True) for a, b in zip(sums, terms))

        sums = lax.fori_loop(0, len(chunks), leave, tuple(jnp.zeros((1, width), f32) for unused in range(5)))
        plan.run(18)
        r.g_out[...] = dot_tn(r.ab[...], r.dy[...]).astype(bf16)
        gain_m, scale_m, time = vec_rows(r.vec, Vec.gain_m, Vec.scale_m, Vec.step)
        dgate_m, dshift_m, along_m, dgate_a, grad_b_down = sums
        lines = [dgate_a, dshift_m, along_m * gain_m, dgate_m, along_m * (1.0 + scale_m), grad_b_down]
        lines += [r.gb[i : i + 1, :] for i in range(4)] + [time[:, :LANES]]
        write_lines(r.pack, lines)
        r.early[...] = r.pack[...].astype(bf16)
        plan.run(20)


def feed_move(ab, x, g, vec, w_out, w_up, w_down, nrows):
    seq, width = x.shape
    ff = w_up.shape[1]
    wide = width
    nz, share, depth, dcols = nrows // 2, width // nrows, width // 8, wide // 2
    once = pl.Buffered(buffer_count=1)
    fixed = lambda a: pl.BlockSpec(a.shape, lambda i: (0, 0), pipeline_mode=once)
    col = lambda r: pl.BlockSpec((r, wide), lambda i: (0, i))
    shape = jax.ShapeDtypeStruct
    ins, outs, scratch = Bag(), Bag(), Bag()
    for name, spec in (
        ("ab", fixed(ab)), ("x", fixed(x)), ("g", fixed(g)), ("vec", fixed(vec)), ("w_out", fixed(w_out)),
        ("w_up", col(width)), ("w_down", pl.BlockSpec((wide, width), lambda i: (i, 0))),
    ):
        ins.add(name, spec)
    for name, dims, kind in (
        ("result", (seq, width), bf16), ("dx", (seq, width), f32), ("datt", (seq, width), bf16),
        ("g_out", (width, width), bf16), ("early", (EARLY, LANES), bf16),
    ):
        outs.add(name, shape(dims, kind))
    row_bufs, col_bufs = RowPiece.scratch(nz, share, wide), ColPiece.scratch(nz, depth, dcols)
    for i, points in enumerate(FEED_POINTS):
        if len(points) < 5:
            for kind, bufs in (("up", row_bufs), ("down", col_bufs)):
                for key in HANDED[len(points) + 1]:
                    outs.add(f"{kind}{i}.{key}", shape(bufs[key].shape, bf16))
    for name in ("h", "dz", "act", "du", "dy"):
        scratch.add(name, pltpu.VMEM((seq, width), bf16))
    for name in ("ht", "dzt"):
        scratch.add(name, pltpu.VMEM((width, seq), bf16))
    for name in ("y", "z", "dh"):
        scratch.add(name, pltpu.VMEM((seq, width), f32))
    scratch.add("gb", pltpu.VMEM((8, wide), f32))
    scratch.add("pack", pltpu.VMEM((EARLY, LANES), f32))
    scratch.add("gu", pltpu.VMEM((2, nz, 2, share, wide), bf16))
    scratch.add("gd", pltpu.VMEM((2, 2, 2, 2, 2, depth, dcols), bf16))
    for i, points in enumerate(FEED_POINTS):
        kept = ROW_BUFS[: (1, 3, 6)[len(points)]]
        scratch.add(f"u{i}", only(row_bufs, kept))
        scratch.add(f"d{i}", only(col_bufs, kept))
    count = 4 * (RowPiece.SEMS + ColPiece.SEMS)
    scratch.add("send", pltpu.SemaphoreType.DMA((count,)))
    scratch.add("recv", pltpu.SemaphoreType.DMA((count,)))
    results = pl.pallas_call(
        functools.partial(feed_move_kernel, ins.names + outs.names + scratch.names),
        grid=(ff // wide,),
        in_specs=ins.items,
        out_specs=[pl.BlockSpec(o.shape, lambda i, n=len(o.shape): (0,) * n) for o in outs.items],
        out_shape=outs.items,
        scratch_shapes=scratch.items,
        compiler_params=pltpu.CompilerParams(collective_id=3, has_side_effects=True, vmem_limit_bytes=62 * MIB),
        cost_estimate=pl.CostEstimate(
            flops=12 * seq * width * ff, bytes_accessed=30 * seq * width, transcendentals=seq * ff
        ),
    )(ab, x, g, vec, w_out, w_up, w_down)
    return dict(zip(outs.names, results))


class Gather:
    def __init__(self, place, sems, source, target):
        self.p, self.sems, self.source, self.target = place, sems, source, target
        self.nblk, self.nrows = target.shape[:2]
        self.base = sems.take(self.nblk + self.nrows)

    def copies(self, stage):
        p = self.p
        if stage == 0:
            return [
                self.sems.copy(self.base + k, self.source, self.target.at[p.blk, p.row], p.along_rows(k))
                for k in range(1, self.nrows)
            ]
        return [
            self.sems.copy(self.base + self.nrows + k, self.target.at[p.blk], self.target.at[p.blk], p.along_blk(k))
            for k in range(1, self.nblk)
        ]

    def run(self, stage):
        if stage:
            for copy in self.copies(stage - 1):
                copy.wait()
        else:
            self.target[self.p.blk, self.p.row] = self.source[...]
        if stage < 2:
            for copy in self.copies(stage):
                copy.start()


class Return:
    def __init__(self, place, sems, source, target, local):
        self.p, self.sems, self.source, self.target, self.local = place, sems, source, target, local
        self.rows, self.nblk = target.shape[0], source.shape[0]
        self.base = sems.take(self.nblk)
        self.mine = jnp.minimum(place.blk, self.rows - 1)

    def copy(self, k):
        device = self.p.along_blk(k)
        return self.sems.copy(self.base + k, self.source.at[device[0]], self.target.at[self.mine], device)

    def own(self):
        return pltpu.make_async_copy(self.source.at[self.p.blk], self.target.at[self.mine], self.local)

    def start(self, ks):
        @pl.when(self.p.blk < self.rows)
        def sent():
            for k in ks:
                (self.copy(k) if k else self.own()).start()

    def finish(self):
        @pl.when(self.p.blk < self.rows)
        def left():
            self.own().wait()
            for k in range(1, self.nblk):
                self.copy(k).wait_send()

        for k in range(1, self.nblk):
            @pl.when(partner(self.p.blk, k) < self.rows)
            def arrived():
                self.copy(k).wait_recv()


def greet(place, nblk, nrows):
    barrier = pltpu.get_barrier_semaphore()
    for k in range(1, nblk):
        pl.semaphore_signal(barrier, inc=1, device_id=place.along_blk(k), device_id_type=MESH)
    for k in range(1, nrows):
        pl.semaphore_signal(barrier, inc=1, device_id=place.along_rows(k), device_id_type=MESH)
    pl.semaphore_wait(barrier, nblk + nrows - 2)


BEHIND_POINTS = ((8, 11), (8, 11), (6, 10, 13), (7, 10, 12, 15))
OUTER_POINTS = (5, 9, 11, 13, 15)
EARLY_POINTS = (8, 16)
RESULT_POINTS = (0, 0, 0, 0)
LATE_POINTS = ((9, 11, 13, 15, 16), (12, 13, 15, 17, 18), (12, 13, 15, 17, 19))


def behind_kernel(names, *refs):
    r = types.SimpleNamespace(**dict(zip(names, refs)))
    step, last = pl.program_id(0), pl.num_programs(0) - 1
    place = Place()
    sems = Sems(r.send, r.recv)
    nblk, stretch, width = r.x.shape
    nrows = r.early_g.shape[1]
    nz, unused, share, cols = r.gq.shape[1:]
    depth, dcols = getattr(r, "d.ag").shape[-2:]
    seq = nblk * stretch
    dims, ddims = (nz, share, cols), (nz, depth, dcols)

    def store_at(ref, begin):
        def store(rows, col, value):
            ref[rows, begin + col : begin + col + value.shape[1]] = value
        return store

    def store_qkv(j):
        def store(rows, col, value):
            for k in range(value.shape[1] // LANES):
                lane = col + k * LANES
                at = lane // (2 * LANES) * width + j * 2 * LANES + lane % (2 * LANES)
                r.share_qkv[rows, at : at + LANES] = value[:, k * LANES : (k + 1) * LANES]
        return store

    def store_down(rows, value):
        r.share_down[rows, :] = value

    shared = group(r, "d")
    carried = []
    for i, points in enumerate(FEED_POINTS):
        if len(points) < 5:
            up = RowPiece(
                place, sems, dims, dict(group(r, f"u{i}"), **group(r, f"up{i}")), store=store_at(r.share_up, i * cols)
            )
            down = ColPiece(
                place, sems, ddims, dict(shared, **group(r, f"d{i}"), **group(r, f"down{i}")), i, store=store_down
            )
            carried.append((len(points) + 1, up, down))
    outer = RowPiece(
        place, sems, dims, group(r, "o"), r.g_out, lambda: r.own_out[...], store_at(r.share_out, 0)
    )
    load = pltpu.make_async_copy(r.g_out.at[:, place.core], r.own_out, r.local.at[2])
    late_pieces = [
        kind(
            place, sems, dims, group(r, f"q{j}"), r.gq.at[j], lambda j=j: r.gq[j, :, place.core], store_qkv(j)
        )
        for j, kind in enumerate((RowPiece, RowPiece, RowPiece))
    ]
    results = Return(place, sems, r.result, r.tok_out, r.local.at[0])
    grads = Return(place, sems, r.gt, r.grad_out, r.local.at[1])
    early = Gather(place, sems, r.early_s, r.early_g)
    late = Gather(place, sems, r.late_b, r.late_g)

    def open_up():
        greet(place, nblk, nrows)
        load.start()
        for stage, up, down in carried:
            up.start(stage)
            down.start(stage)
        outer.run(0)
        r.share_down[...] = jnp.zeros_like(r.share_down)

    def start_early():
        r.early_s[...] = r.early[...]
        early.run(0)

    plan = Plan()
    plan.at(0, open_up)
    plan.at(1, start_early, load.wait)
    for (stage, up, down), points in zip(carried, BEHIND_POINTS):
        for piece in (up, down):
            plan.stages(piece, stage + 1, points)
    plan.stages(outer, 1, OUTER_POINTS)
    plan.stages(early, 1, EARLY_POINTS)
    for k, point in zip((3, 1, 2, 0), RESULT_POINTS):
        plan.at(point, lambda k=k: results.start([k]))
    for piece, points in zip(late_pieces, LATE_POINTS):
        plan.stages(piece, 1, points)

    for i in range(6):
        plan.under(step, i, 2 * i)
    side = step % 2 * LANES

    def store(rows, *grads):
        for i, grad in enumerate(grads):
            r.dqkv[rows, pl.ds(pl.multiple_of(2 * i * LANES + side, LANES), LANES)] = grad

    attend_back_pair(r, store)
    for i in range(6):
        plan.under(step, i, 2 * i + 1)

    @pl.when(step % 2 == 1)
    def projections():
        number = step // 2
        grad_w = dot(r.ht[...], r.dqkv[...]).astype(bf16)
        r.gq[number] = grad_w.reshape(r.gq.shape[1:])
        for j, piece in enumerate(late_pieces):
            @pl.when(number == j)
            def sent():
                piece.run(0)

        for rows in (slice(begin, begin + CHUNK) for begin in range(0, seq, CHUNK)):
            added = dot_nt(r.dqkv[rows, : 2 * LANES], r.wq[...])
            added = added + dot_nt(r.dqkv[rows, 2 * LANES : 4 * LANES], r.wk[...])
            added = added + dot_nt(r.dqkv[rows, 4 * LANES :], r.wv[...])

            @pl.when(number == 0)
            def fresh():
                r.dh[rows, :] = added

            @pl.when(number > 0)
            def more():
                r.dh[rows, :] += added

    @pl.when(step == last)
    def tail():
        factor, gain, scale = vec_rows(r.vec, Vec.factor_a, Vec.gain_a, Vec.scale_a)
        total = [jnp.zeros((1, width), f32) for unused in range(2)]

        def chunk(k):
            slot = partner(place.blk, k)
            rows = pl.ds(pl.multiple_of(slot * stretch, stretch), stretch)
            normed, inverse = norm_rows(r.x[slot].astype(f32))
            dh = r.dh[rows, :]
            r.gt[slot] = (r.dx[rows, :] + norm_back(dh * factor, normed, inverse)).astype(bf16)
            grads.start([k])
            total[0] = total[0] + jnp.sum(dh, axis=0, keepdims=True)
            total[1] = total[1] + jnp.sum(dh * normed, axis=0, keepdims=True)

        plan.run(12)
        chunk(3)
        plan.run(13)
        chunk(1)
        plan.run(14)
        chunk(2)
        chunk(0)
        write_lines(r.late_s, (total[0], total[1] * gain, total[1] * (1.0 + scale)))
        r.late_b[...] = r.late_s[...].astype(bf16)
        late.run(0)
        plan.run(15)
        plan.run(16)
        r.early_out[...] = r.early_g[...]
        late.run(1)
        plan.run(17)
        late.run(2)
        r.late_out[...] = r.late_g[...]
        plan.run(18)
        plan.run(19)
        results.finish()
        grads.finish()


def behind(q, k, v, grads, att, inv, eb, cosine, sine, w_qkv, hidden_t, x, dx, vec, early, handed, g_out, result,
           rows_dev, nrows):
    seq, width = q.shape
    nblk, stretch, unused = x.shape
    nz, share, cols, depth, dcols = nrows // 2, width // nrows, width, width // 8, width // 2
    pair = pl.BlockSpec((seq, LANES), lambda i: (0, i))
    once = pl.Buffered(buffer_count=1)
    fixed = lambda a: pl.BlockSpec(a.shape, lambda i: (0,) * len(a.shape), pipeline_mode=once)
    away = pl.BlockSpec(memory_space=pl.ANY)
    per = width // (2 * LANES)
    weight = lambda n: pl.BlockSpec((width, 2 * LANES), lambda i: (0, n * per + i // 2))
    shape = jax.ShapeDtypeStruct
    ins, args, outs, scratch = Bag(), [], Bag(), Bag()
    for name, spec, value in (
        ("q", pair, q), ("k", pair, k), ("v", pair, v), ("datt", pair, grads), ("att", pair, att), ("inv", pair, inv),
        ("eb", pl.BlockSpec((1, 2, seq, seq), lambda i: (i, 0, 0, 0)), eb), ("cos", fixed(cosine), cosine), ("sin", fixed(sine), sine),
        ("wq", weight(0), w_qkv), ("wk", weight(1), w_qkv), ("wv", weight(2), w_qkv),
        ("ht", fixed(hidden_t), hidden_t), ("x", fixed(x), x), ("dx", fixed(dx), dx), ("vec", fixed(vec), vec),
        ("early", fixed(early), early), *((name, fixed(value), value) for name, value in handed.items()),
        ("g_out", away, g_out), ("result", away, result),
    ):
        ins.add(name, spec)
        args.append(value)
    back = shape((rows_dev, stretch, width), bf16)
    late = (LATE, LANES)
    for name, value in (
        ("tok_out", back), ("grad_out", back), ("share_qkv", shape((share, 3 * width), bf16)),
        ("share_out", shape((share, cols), bf16)), ("share_up", shape((share, 4 * cols), bf16)),
        ("share_down", shape((8 * depth, dcols), bf16)),
        ("early_out", shape((nblk, nrows) + early.shape, bf16)), ("late_out", shape((nblk, nrows) + late, bf16)),
    ):
        outs.add(name, value)
    for name, dims, kind in (
        ("da", (2, seq, LANES), bf16), ("ds", (2, seq, seq), bf16),
        ("dqkv", (seq, 6 * LANES), bf16), ("dh", (seq, width), f32), ("gq", (3, nz, 2, share, cols), bf16),
        ("gt", (nblk, stretch, width), bf16), ("early_s", early.shape, bf16), ("late_s", late, f32),
        ("late_b", late, bf16), ("early_g", (nblk, nrows) + early.shape, bf16),
        ("late_g", (nblk, nrows) + late, bf16), ("own_out", (nz, share, cols), bf16),
    ):
        scratch.add(name, pltpu.VMEM(dims, kind))
    near, cross = RowPiece.scratch(nz, share, cols), ColPiece.scratch(nz, depth, dcols)
    for i, points in enumerate(FEED_POINTS):
        if len(points) < 5:
            kept = ROW_BUFS[(1, 3, 6)[len(points)] :]
            scratch.add(f"u{i}", only(near, kept))
            scratch.add(f"d{i}", only(cross, kept))
    scratch.add("d", ColPiece.shared(nz, depth, dcols))
    scratch.add("o", near)
    for j in range(3):
        scratch.add(f"q{j}", near)
    count = 8 * RowPiece.SEMS + 4 * ColPiece.SEMS + 2 * nblk + 2 * (nblk + nrows)
    scratch.add("send", pltpu.SemaphoreType.DMA((count,)))
    scratch.add("recv", pltpu.SemaphoreType.DMA((count,)))
    scratch.add("local", pltpu.SemaphoreType.DMA((3,)))
    results = pl.pallas_call(
        functools.partial(behind_kernel, ins.names + outs.names + scratch.names),
        grid=(width // LANES,),
        in_specs=ins.items,
        out_specs=[away, away] + [pl.BlockSpec(o.shape, lambda i, n=len(o.shape): (0,) * n) for o in outs.items[2:]],
        out_shape=outs.items,
        scratch_shapes=scratch.items,
        compiler_params=pltpu.CompilerParams(collective_id=2, has_side_effects=True, vmem_limit_bytes=62 * MIB),
        cost_estimate=pl.CostEstimate(
            flops=52 * seq * seq * width, bytes_accessed=40 * seq * width, transcendentals=H * seq * seq
        ),
    )(*args)
    return dict(zip(outs.names, results))


FETCH = ("tok", "grad", "early", "late", "table", "ada", "up", "qkv", "outer", "down")


def finish_kernel(names, *refs):
    r = types.SimpleNamespace(**dict(zip(names, refs)))
    row = lax.axis_index("rows")
    loads = {name: pltpu.make_async_copy(getattr(r, name + "_in"), getattr(r, name), r.local.at[i]) for i, name in enumerate(FETCH)}
    for load in loads.values():
        load.start()
    moves = []
    for i, (name, target) in enumerate((("tok", r.out), ("grad", r.grad_tokens))):
        loads[name].wait()
        moves.append(pltpu.make_async_copy(getattr(r, name), target, r.local.at[len(FETCH) + i]))
        moves[-1].start()
    for name in ("early", "late", "table", "ada"):
        loads[name].wait()
    rows_dev = r.out.shape[0]
    nblk, nrows = r.early.shape[:2]
    count = rows_dev * nrows
    width = r.out.shape[-1]
    per = width // LANES
    for b in range(rows_dev):
        r.early_s[b] = r.early[b].astype(f32)
        r.late_s[b] = r.late[b].astype(f32)
    r.mod[...] = jnp.zeros_like(r.mod)

    def of_all(ref, line):
        return [ref[b, :, line, :] for b in range(rows_dev)]

    for i in range(6 * per):
        blocks = of_all(r.late_s, i) if i < 2 * per else of_all(r.early_s, i - 2 * per)
        for b, block in enumerate(blocks):
            r.mod[b * nrows : (b + 1) * nrows, i * LANES : (i + 1) * LANES] = block
    total = jnp.sum(r.early_s[...], axis=(0, 1))
    late_total = jnp.sum(r.late_s[...], axis=(0, 1))

    ff = r.b_up.shape[0]
    r.gain_m[...] = total[4 * per : 5 * per]
    r.b_down[...] = total[5 * per : 6 * per]
    r.b_up[...] = total[6 * per : 6 * per + ff]
    r.gain_a[...] = late_total[2 * per : 3 * per]
    r.b_ada[: 2 * per, :] = late_total[: 2 * per]
    r.b_ada[2 * per :, :] = total[: 4 * per]
    mod = r.mod[...]
    mod_b = mod.astype(bf16)
    steps = r.steps
    steps[...] = jnp.full(steps.shape, -1.0, f32)
    for b, block in enumerate(of_all(r.early_s, 6 * per + ff)):
        steps[b * nrows : (b + 1) * nrows, :] = block
    entries = r.table.shape[0]
    hot = (steps[:, :entries] == lane_of((1, entries)).astype(f32)).astype(f32).astype(bf16)
    conds = dot(hot, r.table[...])
    r.act_t[...] = jnp.concatenate([silu(conds), jnp.zeros((LANES - conds.shape[0], conds.shape[1]), f32)]).T
    share = r.w_ada.shape[0]
    mine = r.act_t[pl.ds(pl.multiple_of(row * share, share), share), : conds.shape[0]]
    r.w_ada[...] = sum(dot(term, mod_b) for term in in_three(mine))
    grad_act = dot_nt(mod_b, r.ada[...])
    sigmoid = 1.0 / (1.0 + jnp.exp(-conds))
    grad_cond = grad_act * sigmoid * (1.0 + conds * (1.0 - sigmoid))
    r.grad_table[...] = sum(dot_tn(hot, term) for term in in_three(grad_cond))
    for name in ("up", "qkv", "outer", "down"):
        loads[name].wait()
    r.w_up[...] = r.up[...].astype(f32)
    r.w_qkv[...] = r.qkv[...].astype(f32)
    r.w_out[...] = r.outer[...].astype(f32)

    r.w_down[...] = r.down[...].astype(f32).T
    for move in moves:
        move.wait()


def finish(o, table, w_ada):
    rows_dev, stretch, width = o["tok_out"].shape
    nblk, nrows = o["early_out"].shape[:2]
    shape = jax.ShapeDtypeStruct
    away, near = pl.BlockSpec(memory_space=pl.ANY), pl.BlockSpec(memory_space=pltpu.VMEM)
    args, outs, scratch = [], Bag(), Bag()
    fetched = dict(
        tok=o["tok_out"], grad=o["grad_out"], early=o["early_out"], late=o["late_out"], table=table, ada=w_ada,
        up=o["share_up"], qkv=o["share_qkv"], outer=o["share_out"], down=o["share_down"],
    )
    for name in FETCH:
        args.append(fetched[name])
        scratch.add(name, pltpu.VMEM(fetched[name].shape, fetched[name].dtype))
    names = [name + "_in" for name in FETCH] + ["out", "grad_tokens"]
    six, share, per = 6 * width, width // nrows, width // LANES
    ff = o["share_up"].shape[1]
    for name, dims in (
        ("grad_table", table.shape), ("w_ada", (w_ada.shape[0] // nrows, six)), ("b_ada", (6 * per, LANES)),
        ("gain_a", (per, LANES)), ("w_qkv", (share, 3 * width)), ("w_out", (share, width)), ("gain_m", (per, LANES)),
        ("w_up", (share, ff)), ("b_up", (ff // LANES, LANES)), ("w_down", (ff // nrows, width)),
        ("b_down", (per, LANES)),
    ):
        outs.add(name, shape(dims, f32))
    lines = 32
    for name, dims in (
        ("early_s", (rows_dev, nrows, EARLY, LANES)), ("late_s", (rows_dev, nrows, LATE, LANES)), ("mod", (lines, six)),
        ("steps", (lines, LANES)), ("act_t", (LANES, LANES)),
    ):
        scratch.add(name, pltpu.VMEM(dims, f32))
    scratch.add("local", pltpu.SemaphoreType.DMA((2 + len(FETCH),)))
    moved = shape((rows_dev, stretch, width), bf16)
    return pl.pallas_call(
        functools.partial(finish_kernel, names + outs.names + scratch.names),
        in_specs=[away] * len(args),
        out_specs=[away, away] + [near] * len(outs.items),
        out_shape=[moved, moved] + outs.items,
        scratch_shapes=scratch.items,
        compiler_params=pltpu.CompilerParams(vmem_limit_bytes=62 * MIB),
    )(*args)


def rows_out(whole, rows, me, nblk):
    parts = [lax.dynamic_index_in_dim(whole, me, 0, keepdims=False)]
    for k in range(1, nblk):
        part = lax.dynamic_index_in_dim(whole, me ^ k, 0, keepdims=False)
        pairs = [(s, s ^ k) for s in range(nblk) if s < rows]
        parts.append(lax.ppermute(part, "blk", pairs))
    stacked = jnp.stack(parts)
    return jnp.take(stacked, jnp.arange(rows) ^ me, axis=0)


def pick(array, index, axis=0):
    return lax.dynamic_index_in_dim(array, index, axis, keepdims=False)


def xor_move(array, axis, size, k):
    return lax.ppermute(array, axis, [(s, s ^ k) for s in range(size)])


def halve(array, axis, bit, name, size, k):
    kept = pick(array, bit, axis).astype(f32)
    sent = pick(array, 1 - bit, axis)
    return (kept + xor_move(sent, name, size, k).astype(f32)).astype(bf16)


def reduce_weight(grad, blk, row, nblk, nrows):
    total, cols = grad.shape
    share = total // nrows
    nz = nrows // 2
    core, z = row % 2, row // 2
    x, y = blk % 2, blk // 2
    part = halve(grad.reshape(nz, 2, share, cols), 1, core, "rows", nrows, 1)
    part = part.reshape(nz, 2, share // 2, cols)
    front, back = part[: nz // 2], part[nz // 2 :]
    split = lambda a: jnp.stack([a[..., : cols // 2], a[..., cols // 2 :]])
    front = halve(split(front), 0, x, "blk", nblk, 1)
    back = halve(back, 1, y, "blk", nblk, 2)
    front = halve(front, 1, y, "blk", nblk, 2)
    back = halve(split(back), 0, x, "blk", nblk, 1)
    part = jnp.concatenate([front, back], axis=0)
    if nz <= 4:
        summed = pick(part, z).astype(f32)
        for k in range(1, nz):
            summed = summed + xor_move(pick(part, z ^ k), "rows", nrows, 2 * k).astype(f32)
        part = summed.astype(bf16)
    else:
        k = nz // 2
        while k:
            pairs = part.reshape((2, k) + part.shape[1:])
            part = halve(pairs, 0, (z // k) % 2, "rows", nrows, 2 * k)
            k //= 2
        part = part[0]
    quarters = [part] + [xor_move(part, "blk", nblk, k) for k in range(1, 4)]
    quarters = jnp.take(jnp.stack(quarters), jnp.arange(4) ^ blk, axis=0)
    ordered = quarters.reshape(2, 2, share // 2, cols // 2).transpose(0, 2, 1, 3)
    return ordered.reshape(share, cols).astype(f32)


def per_device(
    tokens, timesteps, lengths, time_table, w_ada, b_ada, gain_attn, w_qkv, w_out, gain_mlp, w_up, b_up,
    w_down, b_down, grad_out
):
    rows_dev, stretch, width = tokens.shape
    nblk, nrows = lax.axis_size("blk"), lax.axis_size("rows")
    blk, row = lax.axis_index("blk"), lax.axis_index("rows")
    seq = stretch * nblk

    x_blocks, g_blocks, hidden_t, q, k, v, cosine, sine, attended, inv, attended_b, eb, vec = ahead(
        tokens, grad_out, w_qkv, w_ada, lengths, timesteps, time_table, b_ada, gain_attn, gain_mlp, b_down, b_up, nblk
    )
    x_row = x_blocks.reshape(seq, width)

    ff = b_up.shape[0]
    fed = (attended_b, x_row, g_blocks.reshape(seq, width), vec, w_out, w_up, w_down)

    if (nblk, nrows) == (4, 8):
        f = feed_move(*fed, nrows)
        nz, share = nrows // 2, width // nrows
        o = behind(
            q, k, v, f["datt"], attended, inv, eb, cosine, sine, w_qkv, hidden_t, x_blocks, f["dx"], vec, f["early"],
            {name: value for name, value in f.items() if "." in name}, f["g_out"].reshape(nz, 2, share, width),
            f["result"].reshape(nblk, stretch, width), rows_dev, nrows,
        )
        out, grad_tokens, *rest = finish(o, time_table, w_ada)
        flat = (2, 3, 6, 8, 10)
        return (out, grad_tokens, *(value.reshape(-1) if i in flat else value for i, value in enumerate(rest)))

    shift_a, scale_a, gate_a, shift_m, scale_m, gate_m, factor_a, factor_m, gain_a, gain_m, step = vec[:11]
    result, grad_mid, grad_att, grad_w_out, grad_w_up, grad_w_down, gb_up, sums = feed(*fed)
    dgate_m, dshift_m, along_m, dgate_a, grad_b_down = (sums[i] for i in range(5))
    out = rows_out(result.reshape(nblk, stretch, width), rows_dev, blk, nblk)
    share_w_down = reduce_weight(grad_w_down.transpose(2, 0, 1, 3).reshape(width, ff).T, blk, row, nblk, nrows)
    share_w_up = reduce_weight(grad_w_up.transpose(1, 0, 2).reshape(width, ff), blk, row, nblk, nrows)
    share_w_out = reduce_weight(grad_w_out, blk, row, nblk, nrows)
    dq, dk, dv = attend_back(q, k, v, grad_att, attended, inv, eb, cosine, sine)
    grad_qkv = jnp.concatenate([dq, dk, dv], axis=-1)
    grad_w_qkv = dot(hidden_t, grad_qkv).astype(bf16)
    share_w_qkv = reduce_weight(grad_w_qkv, blk, row, nblk, nrows)
    grad_ha = dot_nt(grad_qkv, w_qkv)
    normed_a, inverse_a = norm_rows(x_row.astype(f32))
    along_a = jnp.sum(grad_ha * normed_a, axis=0)
    grad_in = (grad_mid + norm_back(grad_ha * factor_a, normed_a, inverse_a)).astype(bf16)
    grad_tokens = rows_out(grad_in.reshape(nblk, stretch, width), rows_dev, blk, nblk)
    count = 6 * width + ff + LANES
    packed = jnp.concatenate(
        [
            dgate_a, dshift_m, along_m * gain_m, dgate_m, along_m * (1.0 + scale_m), grad_b_down, gb_up[0],
            step[:LANES], jnp.sum(grad_ha, axis=0), along_a * gain_a, along_a * (1.0 + scale_a),
        ]
    )
    gathered = gather_all(packed, nblk, nrows).reshape(nblk, nrows, -1)
    early = gathered[:rows_dev].reshape(rows_dev * nrows, -1)
    dshift_a, dscale_a, part_gain_a = (early[:, count + i * width : count + (i + 1) * width] for i in range(3))

    table, ada_full = time_table.astype(f32), w_ada.astype(f32)
    grad_mod = jnp.concatenate([dshift_a, dscale_a, early[:, : 4 * width]], axis=-1)
    smalls = jnp.sum(early, axis=0)
    grad_gain_m, total_b_down = smalls[4 * width : 5 * width], smalls[5 * width : 6 * width]
    total_b_up = smalls[6 * width : 6 * width + ff]
    steps = early[:, 6 * width + ff].astype(jnp.int32)
    onehot = (steps[:, None] == jnp.arange(table.shape[0], dtype=jnp.int32)[None, :]).astype(f32)
    conds = jnp.dot(onehot, table, precision=highest)
    share = conds.shape[1] // nrows
    my_conds = lax.dynamic_slice_in_dim(conds, row * share, share, axis=1)
    grad_w_ada = jnp.dot(jax.nn.silu(my_conds).T, grad_mod, precision=highest)
    grad_cond_act = lax.dot_general(
        grad_mod, ada_full, (((1,), (1,)), ((), ())), precision=highest, preferred_element_type=f32
    )
    sigmoid = jax.nn.sigmoid(conds)
    grad_cond = grad_cond_act * sigmoid * (1.0 + conds * (1.0 - sigmoid))
    grad_table = jnp.dot(onehot.T, grad_cond, precision=highest)
    return (
        out,
        grad_tokens,
        grad_table,
        grad_w_ada,
        jnp.sum(grad_mod, axis=0),
        jnp.sum(part_gain_a, axis=0),
        share_w_qkv,
        share_w_out,
        grad_gain_m,
        share_w_up,
        total_b_up,
        share_w_down,
        total_b_down,
    )


def solution(mesh):
    whole, split = P(), P("rows", None)
    tokens = P("rows", "blk", None)
    return jax.shard_map(
        per_device,
        mesh=mesh,
        in_specs=(tokens, P("rows"), split) + (whole,) * 11 + (tokens,),
        out_specs=(
            tokens, tokens, whole, split, whole, whole, split, split, whole, split, whole, split, whole
        ),
        check_vma=False,
    )
```

```python
import functools
import math
import types

import jax
import jax.numpy as jnp
import numpy as np
from jax import lax
from jax.experimental import pallas as pl
from jax.experimental.pallas import tpu as pltpu
from jax.sharding import PartitionSpec as P

H = 12
NDOC = 8
LANES = 128
CHUNK = 256
MIB = 1 << 20

epsilon = 1e-05
highest = lax.Precision.HIGHEST
bf16 = jnp.bfloat16
f32 = jnp.float32
MESH = pl.DeviceIdType.MESH


def dot(a, b):
    return jnp.dot(a, b, preferred_element_type=f32)


def dot_nt(a, b):
    return lax.dot_general(a, b, (((1,), (1,)), ((), ())), preferred_element_type=f32)


def dot_tn(a, b):
    return lax.dot_general(a, b, (((0,), (0,)), ((), ())), preferred_element_type=f32)


def norm_rows(values):
    centre = jnp.mean(values, axis=-1, keepdims=True)
    centred = values - centre
    spread = jnp.mean(centred * centred, axis=-1, keepdims=True)
    inverse = lax.rsqrt(spread + epsilon)
    return (centred * inverse, inverse)


def norm_back(grad_normed, normed, inverse):
    first = jnp.mean(grad_normed, axis=-1, keepdims=True)
    second = jnp.mean(grad_normed * normed, axis=-1, keepdims=True)
    return inverse * (grad_normed - first - normed * second)


def lane_of(shape):
    return lax.broadcasted_iota(jnp.int32, shape, len(shape) - 1)


def swap_halves(values, half):
    lane = lane_of(values.shape)
    width = values.shape[-1]
    ahead = pltpu.roll(values, width - half, values.ndim - 1)
    behind = pltpu.roll(values, half, values.ndim - 1)
    return jnp.where(lane % (2 * half) < half, ahead, behind)


def in_three(values):
    high = values.astype(bf16)
    rest = values - high.astype(f32)
    middle = rest.astype(bf16)
    low = (rest - middle.astype(f32)).astype(bf16)
    return (high, middle, low)


def partner(blk, k):
    other = blk
    bit = 1
    while bit <= k:
        if k & bit:
            other = other + bit - 2 * bit * (other // bit % 2)
        bit *= 2
    return other


def remote(source, target, send, recv, blk, row):
    return pltpu.make_async_remote_copy(
        src_ref=source, dst_ref=target, send_sem=send, recv_sem=recv, device_id=(blk, row), device_id_type=MESH
    )


class Vec:
    shift_a, scale_a, gate_a, shift_m, scale_m, gate_m, factor_a, factor_m, gain_a, gain_m, step, b_down, b_up = range(13)


def silu(values):
    return values / (1.0 + jnp.exp(-values))


def ahead_kernel(
    tok_ref, grad_ref, w_ref, ada_ref, lengths_ref, steps_ref, table_ref, b_ada_ref, gain_a_ref, gain_m_ref, b_down_ref, b_up_ref, freq_ref,
    x_out, g_out, ht_out, q_out, k_out, v_out, cos_out, sin_out, att_ref, inv_ref, ab_ref, eb_ref, vec_ref,
    x_s, own_s, ht_s, q_s, k_s, v_s, cos_s, sin_s, w_s, ada_s, fq_s, fk_s, zero_s, send_x, recv_x, send_g, recv_g, local
):
    step, last = pl.program_id(0), pl.num_programs(0) - 1
    blk, row = lax.axis_index("blk"), lax.axis_index("rows")
    rows_dev, stretch, width = tok_ref.shape
    nblk = x_s.shape[0]
    half = width // H // 2
    scale = 1.0 / math.sqrt(2 * half)
    has_row = blk < rows_dev
    mine = jnp.minimum(blk, rows_dev - 1)
    kept = (
        (x_s, x_out), (ht_s, ht_out), (q_s, q_out), (k_s, k_out), (v_s, v_out), (cos_s, cos_out), (sin_s, sin_out)
    )
    free = len(kept)

    def move(k, source, target, send, recv, other):
        return remote(source.at[jnp.minimum(other, rows_dev - 1)], target.at[blk], send.at[k], recv.at[k], other, row)

    def each_sent(source, target, send, recv, what):
        for k in range(1, nblk):
            other = partner(blk, k)

            @pl.when(other < rows_dev)
            def sent():
                what(move(k, source, target, send, recv, other))

    def store(i):
        return pltpu.make_async_copy(kept[i][0], kept[i][1], local.at[i])

    def own_grad():
        return pltpu.make_async_copy(grad_ref.at[mine], g_out.at[blk], local.at[free + 3])

    def chunk(source):
        rows = pl.ds(pl.multiple_of(source * stretch, stretch), stretch)
        normed, unused = norm_rows(x_s[source].astype(f32))
        hidden = normed * vec(Vec.factor_a) + vec(Vec.shift_a)
        hidden_b = hidden.astype(bf16)
        ht_s[:, rows] = hidden.T.astype(bf16)
        cosine, sine = cos_s[rows, :], sin_s[rows, :]
        for part in range(3):
            out = dot(hidden_b, w_s[:, part * width : (part + 1) * width])
            for group in range(width // LANES):
                cols = slice(group * LANES, (group + 1) * LANES)
                piece = out[:, cols]
                if part == 2:
                    v_s[rows, cols] = piece.astype(bf16)
                    continue
                turned = (piece * cosine + swap_halves(piece, half) * sine).astype(bf16)
                if part == 0:
                    q_s[rows, cols] = (turned.astype(f32) * scale).astype(bf16)
                else:
                    k_s[rows, cols] = turned

    def vec(at):
        return vec_ref[at : at + 1, :]

    def prepare():
        wide = table_ref.shape[0]
        time = steps_ref[mine]
        hot = (lane_of((16, wide)) == time).astype(f32).astype(bf16)
        terms = in_three(silu(dot(hot, table_ref[...])))
        line = lax.broadcasted_iota(jnp.int32, (16, 1), 0)
        three = jnp.zeros(terms[0].shape, f32)
        for i, term in enumerate(terms):
            three = jnp.where(line == i, term.astype(f32), three)
        modulate = jnp.sum(dot(three.astype(bf16), ada_s[...]), axis=0, keepdims=True)
        flat = lambda ref: jnp.concatenate([ref[i : i + 1, :] for i in range(ref.shape[0])], axis=1).astype(f32)
        modulate = modulate + flat(b_ada_ref)
        gains = [flat(gain_a_ref), flat(gain_m_ref)]
        rows = [modulate[:, i * width : (i + 1) * width] for i in range(6)]
        rows += [gains[0] * (1.0 + rows[1]), gains[1] * (1.0 + rows[4])] + gains
        rows += [jnp.full((1, width), time, jnp.int32).astype(f32), flat(b_down_ref)]
        b_up = flat(b_up_ref)
        rows += [b_up[:, i * width : (i + 1) * width] for i in range(b_up.shape[1] // width)]
        vec_ref[...] = jnp.zeros_like(vec_ref)
        for i, value in enumerate(rows):
            vec_ref[i : i + 1, :] = value
        shape = fq_s.shape
        slots = lax.broadcasted_iota(jnp.int32, shape, 0)
        feature = lane_of(shape) % (2 * half)
        doc, start = jnp.zeros(shape, jnp.int32), jnp.zeros(shape, jnp.int32)
        last_end = jnp.int32(0)
        for i in range(lengths_ref.shape[1]):
            last_end = last_end + lengths_ref[mine, i]
            past = slots >= last_end
            doc = doc + past.astype(jnp.int32)
            start = jnp.where(past, last_end, start)
        fq_s[...] = jnp.where(feature == doc, -1e30, 0.0).astype(bf16)
        fk_s[...] = jnp.where((feature == doc) | (feature >= NDOC), 0.0, 1.0).astype(bf16)
        angle = (slots - start).astype(f32) * freq_ref[...]
        cos_s[...] = jnp.cos(angle)
        sine = jnp.sin(angle)
        sin_s[...] = jnp.where(feature < half, -sine, sine)

    @pl.when(step == 0)
    def begin():
        barrier = pltpu.get_barrier_semaphore()
        for k in range(1, nblk):
            pl.semaphore_signal(barrier, inc=1, device_id=(partner(blk, k), row), device_id_type=MESH)
        ada = pltpu.make_async_copy(ada_ref, ada_s, local.at[free])
        weights = pltpu.make_async_copy(w_ref, w_s, local.at[free + 1])
        own = pltpu.make_async_copy(tok_ref.at[mine], own_s, local.at[free + 2])
        for copy in (ada, weights, own):
            copy.start()
        pl.semaphore_wait(barrier, nblk - 1)
        each_sent(tok_ref, x_s, send_x, recv_x, lambda copy: copy.start())
        ada.wait()
        prepare()
        own.wait()

        @pl.when(has_row)
        def mine_first():
            x_s[blk] = own_s[...]

        @pl.when(jnp.logical_not(has_row))
        def nothing():
            x_s[...] = jnp.zeros_like(x_s)

        weights.wait()
        for k in range(nblk):
            source = partner(blk, k)
            if k:
                @pl.when(has_row)
                def arrived():
                    move(k, tok_ref, x_s, send_x, recv_x, source).wait_recv()

            chunk(source)
        each_sent(tok_ref, x_s, send_x, recv_x, lambda copy: copy.wait_send())
        each_sent(grad_ref, g_out, send_g, recv_g, lambda copy: copy.start())
        zero_s[...] = jnp.zeros_like(zero_s)

        @pl.when(has_row)
        def own_part():
            own_grad().start()

        @pl.when(jnp.logical_not(has_row))
        def no_part():
            for i in range(nblk):
                pltpu.make_async_copy(zero_s, g_out.at[i], local.at[free + 4 + i]).start()

        for i in range(len(kept)):
            store(i).start()

    cols = pl.ds(pl.multiple_of(step * LANES, LANES), LANES)
    seq = q_s.shape[0]
    first = lane_of((1, LANES)) < LANES // 2
    owns = (first, jnp.logical_not(first))
    one = jnp.ones((), bf16)
    keys = [jnp.where(own, k_s[:, cols], fk_s[...]) for own in owns]
    values = [jnp.where(own, v_s[:, cols], one) for own in owns]

    def score_of(start, head):
        rows = slice(start, start + CHUNK)
        return dot_nt(jnp.where(owns[head], q_s[rows, cols], fq_s[rows, :]), keys[head])

    items = [(start, head) for start in range(0, seq, CHUNK) for head in range(2)]
    ahead_score = score_of(*items[0])
    pieces = [None, None]
    for number, (start, head) in enumerate(items):
        score = ahead_score
        if number + 1 < len(items):
            ahead_score = score_of(*items[number + 1])
        rows = slice(start, start + CHUNK)
        top = jnp.max(score, axis=-1, keepdims=True)
        weight = jnp.exp(score - top).astype(bf16)
        eb_ref[0, head, rows, :] = weight
        mixed = dot(weight, values[head])
        inverse = 1.0 / pltpu.roll(mixed, LANES // 2, 1)
        pieces[head] = (mixed * inverse, inverse)
        if head == 1:
            attended = jnp.where(first, pieces[0][0], pieces[1][0])
            att_ref[rows, :] = attended
            ab_ref[rows, :] = attended.astype(bf16)
            inv_ref[rows, :] = jnp.where(first, pieces[0][1], pieces[1][1])

    @pl.when(step == last)
    def end():
        for i in range(len(kept)):
            store(i).wait()
        each_sent(grad_ref, g_out, send_g, recv_g, lambda copy: copy.wait_send())

        @pl.when(has_row)
        def received():
            own_grad().wait()
            for k in range(1, nblk):
                move(k, grad_ref, g_out, send_g, recv_g, partner(blk, k)).wait_recv()

        @pl.when(jnp.logical_not(has_row))
        def cleared():
            for i in range(nblk):
                pltpu.make_async_copy(zero_s, g_out.at[i], local.at[free + 4 + i]).wait()


def lines_of(vector):
    return vector.reshape(-1, LANES)


def ahead(tokens, grads, w_qkv, w_ada, lengths, timesteps, table, b_ada, gain_a, gain_m, b_down, b_up, nblk):
    rows_dev, stretch, width = tokens.shape
    seq = nblk * stretch
    head_dim = width // H
    freqs = np.float32(10000.0) ** (-np.arange(head_dim // 2, dtype=np.float32) * np.float32(2.0 / head_dim))
    freqs = np.concatenate([freqs] * 4)[None, :]
    small = [table, *(lines_of(a) for a in (b_ada, gain_a, gain_m, b_down, b_up)), freqs]
    pair = pl.BlockSpec((seq, LANES), lambda i: (0, i))
    fixed = lambda a: pl.BlockSpec(a.shape, lambda i: (0, 0), pipeline_mode=pl.Buffered(buffer_count=1))
    away = pl.BlockSpec(memory_space=pl.ANY)
    numbers = pl.BlockSpec(memory_space=pltpu.SMEM)
    blocks, flat, turn = (nblk, stretch, width), (seq, width), (seq, LANES)
    shape = jax.ShapeDtypeStruct
    vec = (16, width)
    return pl.pallas_call(
        ahead_kernel,
        grid=(width // LANES,),
        in_specs=[away] * 4 + [numbers] * 2 + [fixed(a) for a in small],
        out_specs=[away] * 8 + [pair] * 3
        + [pl.BlockSpec((1, 2, seq, seq), lambda i: (i, 0, 0, 0)), pl.BlockSpec(vec, lambda i: (0, 0))],
        out_shape=[
            shape(blocks, bf16), shape(blocks, bf16), shape(flat[::-1], bf16),
            shape(flat, bf16), shape(flat, bf16), shape(flat, bf16), shape(turn, f32), shape(turn, f32),
            shape(flat, f32), shape(flat, f32), shape(flat, bf16), shape((width // LANES, 2, seq, seq), bf16),
            shape(vec, f32),
        ],
        scratch_shapes=[
            pltpu.VMEM(blocks, bf16), pltpu.VMEM((stretch, width), bf16), pltpu.VMEM(flat[::-1], bf16),
            pltpu.VMEM(flat, bf16), pltpu.VMEM(flat, bf16), pltpu.VMEM(flat, bf16),
            pltpu.VMEM(turn, f32), pltpu.VMEM(turn, f32), pltpu.VMEM(w_qkv.shape, bf16), pltpu.VMEM(w_ada.shape, bf16),
            pltpu.VMEM(turn, bf16), pltpu.VMEM(turn, bf16), pltpu.VMEM((stretch, width), bf16),
        ] + [pltpu.SemaphoreType.DMA((nblk,))] * 4 + [pltpu.SemaphoreType.DMA((11 + nblk,))],
        compiler_params=pltpu.CompilerParams(
            collective_id=1, has_side_effects=True, vmem_limit_bytes=60 * MIB
        ),
        cost_estimate=pl.CostEstimate(
            flops=22 * seq * seq * width, bytes_accessed=24 * seq * width, transcendentals=H * seq * seq
        ),
    )(tokens, grads, w_qkv, w_ada, lengths, timesteps, *small)


def attend_back_pair(r, store):
    seq = r.q.shape[0]
    half = LANES // 4
    scale = 1.0 / math.sqrt(2 * half)
    lane = lane_of((1, LANES))
    first = lane < 2 * half
    owns = (first, jnp.logical_not(first))
    where = lane % (2 * half)
    one = jnp.ones((), bf16)
    scaled = r.datt[...].astype(f32) * r.inv[...]
    both = scaled * r.att[...]
    scaled_b = scaled.astype(bf16)
    values = []
    for head, own in enumerate(owns):
        total = -jnp.sum(jnp.where(own, both, 0.0), axis=-1, keepdims=True)
        delta = in_three(jnp.broadcast_to(total, both.shape))
        feature = jnp.zeros_like(scaled_b)
        for i in range(3):
            feature = jnp.where(where == i, delta[i], feature)
        r.da[head] = jnp.where(own, scaled_b, feature)
        values.append(jnp.where(own, r.v[...], one))
    queries_t = r.q[...].astype(f32).T.astype(bf16)
    scaled_t = scaled_b.astype(f32).T.astype(bf16)

    def grad_prob(start, head):
        return dot_nt(r.da[head, start : start + CHUNK, :], values[head])

    items = [(start, head) for start in range(0, seq, CHUNK) for head in range(2)]
    ahead_grad = grad_prob(*items[0])
    grad_q = {}
    for number, (start, head) in enumerate(items):
        grad_p = ahead_grad
        if number + 1 < len(items):
            ahead_grad = grad_prob(*items[number + 1])
        rows = slice(start, start + CHUNK)
        grad_s = (r.eb[0, head, rows, :].astype(f32) * grad_p).astype(bf16)
        r.ds[head, rows, :] = grad_s
        grad_q[start, head] = dot(grad_s, r.k[...])
    upper = lax.broadcasted_iota(jnp.int32, (LANES, 1), 0) < 2 * half
    grad_k = [dot(queries_t, r.ds[head]) for head in range(2)]
    grad_v = [dot(scaled_t, r.eb[0, head]) for head in range(2)]
    grad_k = jnp.where(upper, grad_k[0], grad_k[1]).T
    grad_v = jnp.where(upper, grad_v[0], grad_v[1]).T
    for start in range(0, seq, CHUNK):
        rows = slice(start, start + CHUNK)
        cosine, sine = r.cos[rows, :], r.sin[rows, :]
        turned = []
        for grad in (jnp.where(first, grad_q[start, 0], grad_q[start, 1]) * scale, grad_k[rows, :]):
            turned.append((grad * cosine - swap_halves(grad, half) * sine).astype(bf16))
        store(rows, turned[0], turned[1], grad_v[rows, :].astype(bf16))


def attend_back_kernel(names, *refs):
    r = types.SimpleNamespace(**dict(zip(names, refs)))

    def store(rows, *grads):
        for ref, grad in zip((r.dq, r.dk, r.dv), grads):
            ref[rows, :] = grad

    attend_back_pair(r, store)


def attend_back(q, k, v, grads, att, inv, eb, cosine, sine):
    seq, width = q.shape
    pair = pl.BlockSpec((seq, LANES), lambda i: (0, i))
    fixed = pl.BlockSpec((seq, LANES), lambda i: (0, 0))
    names = list(dict(q=0, k=0, v=0, datt=0, att=0, inv=0, eb=0, cos=0, sin=0, dq=0, dk=0, dv=0, da=0, ds=0))
    return pl.pallas_call(
        functools.partial(attend_back_kernel, names),
        grid=(width // LANES,),
        in_specs=[pair] * 6 + [pl.BlockSpec((1, 2, seq, seq), lambda i: (i, 0, 0, 0)), fixed, fixed],
        out_specs=[pair] * 3,
        out_shape=[jax.ShapeDtypeStruct((seq, width), bf16)] * 3,
        scratch_shapes=[pltpu.VMEM((2, seq, LANES), bf16), pltpu.VMEM((2, seq, seq), bf16)],
        compiler_params=pltpu.CompilerParams(vmem_limit_bytes=56 * MIB),
        cost_estimate=pl.CostEstimate(
            flops=32 * seq * seq * width, bytes_accessed=24 * seq * width + 2 * H * seq * seq, transcendentals=0
        ),
    )(q, k, v, grads, att, inv, eb, cosine, sine)


GELU = math.sqrt(2.0 / math.pi)
CUBE = 0.044715


def vec_rows(ref, *lines):
    return [ref[at : at + 1, :] for at in lines]


def feed_chunk(hidden, grad, w_up_ref, b_up, w_down_ref):
    u = dot(hidden, w_up_ref[...]) + b_up
    square = u * u
    turn = jnp.tanh(GELU * u * (1.0 + CUBE * square))
    half = 0.5 * (1.0 + turn)
    slope = half + (0.5 * GELU) * u * (1.0 - turn * turn) * (1.0 + 3.0 * CUBE * square)
    du = (dot_nt(grad, w_down_ref[...]) * slope).astype(bf16)
    return ((u * half).astype(bf16), du)


def feed_kernel(
    ab_ref, x_ref, g_ref, vec_ref, w_out_ref, w_up_ref, w_down_ref,
    result_ref, dx_ref, datt_ref, g_out_ref, g_up_ref, g_down_ref, gb_up_ref, sums_ref,
    h_s, ht_s, dz_s, dzt_s, y_s, z_s, dh_s, act_s, du_s, dyt_s
):
    step, last = pl.program_id(0), pl.num_programs(0) - 1
    seq, width = x_ref.shape
    wide = w_up_ref.shape[1]
    gate_a, factor_m, shift_m, gate_m, b_down = vec_rows(vec_ref, Vec.gate_a, Vec.factor_m, Vec.shift_m, Vec.gate_m, Vec.b_down)
    chunks = [slice(begin, begin + CHUNK) for begin in range(0, seq, CHUNK)]

    @pl.when(step == 0)
    def before():
        for rows in chunks:
            y = dot(ab_ref[rows, :], w_out_ref[...])
            y_s[rows, :] = y
            normed, unused = norm_rows(x_ref[rows, :].astype(f32) + gate_a * y)
            hidden = normed * factor_m + shift_m
            h_s[rows, :] = hidden.astype(bf16)
            ht_s[:, rows] = hidden.T.astype(bf16)
            grad = gate_m * g_ref[rows, :].astype(f32)
            dz_s[rows, :] = grad.astype(bf16)
            dzt_s[:, rows] = grad.T.astype(bf16)
        z_s[...] = jnp.zeros_like(z_s)
        dh_s[...] = jnp.zeros_like(dh_s)

    b_up = vec_ref[pl.ds(Vec.b_up + step, 1), :]
    bias_sum = jnp.zeros((1, wide), f32)
    for rows in chunks:
        act, du = feed_chunk(h_s[rows, :], dz_s[rows, :], w_up_ref, b_up, w_down_ref)
        act_s[rows, :] = act
        du_s[rows, :] = du
        bias_sum = bias_sum + jnp.sum(du.astype(f32), axis=0, keepdims=True)
        z_s[rows, :] += dot(act, w_down_ref[...])
        dh_s[rows, :] += dot_nt(du, w_up_ref[...])
    gb_up_ref[...] = bias_sum
    g_up_ref[0] = dot(ht_s[...], du_s[...]).astype(bf16)
    down = dot(dzt_s[...], act_s[...]).astype(bf16)
    g_down_ref[0, 0] = down[:, : wide // 2]
    g_down_ref[0, 1] = down[:, wide // 2 :]

    @pl.when(step == last)
    def after():
        sums = [jnp.zeros((1, width), f32) for unused in range(5)]
        for rows in chunks:
            y = y_s[rows, :]
            middle = x_ref[rows, :].astype(f32) + gate_a * y
            normed, inverse = norm_rows(middle)
            z = z_s[rows, :] + b_down
            result_ref[rows, :] = (middle + gate_m * z).astype(bf16)
            grad = g_ref[rows, :].astype(f32)
            dh = dh_s[rows, :]
            dx = grad + norm_back(dh * factor_m, normed, inverse)
            dx_ref[rows, :] = dx
            dy = gate_a * dx
            dyb = dy.astype(bf16)
            dyt_s[rows, :] = dyb
            datt_ref[rows, :] = dot_nt(dyb, w_out_ref[...]).astype(bf16)
            terms = (grad * z, dh, dh * normed, dx * y, dz_s[rows, :].astype(f32))
            sums = [a + jnp.sum(b, axis=0, keepdims=True) for a, b in zip(sums, terms)]
        g_out_ref[...] = dot_tn(ab_ref[...], dyt_s[...]).astype(bf16)
        for i in range(5):
            sums_ref[i : i + 1, :] = sums[i]


def feed(ab, x, g, vec, w_out, w_up, w_down):
    seq, width = x.shape
    ff = w_up.shape[1]
    wide = width
    fixed = lambda a: pl.BlockSpec(a.shape, lambda i: (0, 0))
    one = lambda shape: pl.BlockSpec(shape, lambda i: (0, 0))
    col = lambda r: pl.BlockSpec((r, wide), lambda i: (0, i))
    shape = jax.ShapeDtypeStruct
    return pl.pallas_call(
        feed_kernel,
        grid=(ff // wide,),
        in_specs=[
            fixed(ab), fixed(x), fixed(g), fixed(vec), fixed(w_out), col(width),
            pl.BlockSpec((wide, width), lambda i: (i, 0)),
        ],
        out_specs=[
            one((seq, width)), one((seq, width)), one((seq, width)), one((width, width)),
            pl.BlockSpec((1, width, wide), lambda i: (i, 0, 0)),
            pl.BlockSpec((1, 2, width, wide // 2), lambda i: (i, 0, 0, 0)), col(1), one((8, width)),
        ],
        out_shape=[
            shape((seq, width), bf16), shape((seq, width), f32), shape((seq, width), bf16),
            shape((width, width), bf16), shape((ff // wide, width, wide), bf16),
            shape((ff // wide, 2, width, wide // 2), bf16),
            shape((1, ff), f32), shape((8, width), f32),
        ],
        scratch_shapes=[
            pltpu.VMEM((seq, width), bf16), pltpu.VMEM((width, seq), bf16),
            pltpu.VMEM((seq, width), bf16), pltpu.VMEM((width, seq), bf16),
            pltpu.VMEM((seq, width), f32), pltpu.VMEM((seq, width), f32), pltpu.VMEM((seq, width), f32),
            pltpu.VMEM((seq, wide), bf16), pltpu.VMEM((seq, wide), bf16), pltpu.VMEM((seq, width), bf16),
        ],
        compiler_params=pltpu.CompilerParams(vmem_limit_bytes=60 * MIB),
        cost_estimate=pl.CostEstimate(
            flops=12 * seq * width * ff, bytes_accessed=30 * seq * width, transcendentals=seq * ff
        ),
    )(ab, x, g, vec, w_out, w_up, w_down)


def gather_kernel(nblk, nrows, in_ref, out_ref, send_r, recv_r, send_b, recv_b):
    blk, row = lax.axis_index("blk"), lax.axis_index("rows")
    barrier = pltpu.get_barrier_semaphore()
    for step in range(1, nblk):
        pl.semaphore_signal(
            barrier, inc=1, device_id=(lax.rem(blk + step, nblk), row), device_id_type=MESH
        )

    def greet(step, unused):
        pl.semaphore_signal(
            barrier, inc=1, device_id=(blk, lax.rem(row + step, nrows)), device_id_type=MESH
        )
        return unused

    lax.fori_loop(1, nrows, greet, 0)
    pl.semaphore_wait(barrier, nblk + nrows - 2)
    out_ref[blk, row] = in_ref[...]

    def over_rows(step):
        other = lax.rem(row + step, nrows)
        return pltpu.make_async_remote_copy(
            src_ref=in_ref,
            dst_ref=out_ref.at[blk, row],
            send_sem=send_r.at[step],
            recv_sem=recv_r.at[step],
            device_id=(blk, other),
            device_id_type=MESH,
        )

    def over_blk(step):
        other = lax.rem(blk + step, nblk)
        return pltpu.make_async_remote_copy(
            src_ref=out_ref.at[blk],
            dst_ref=out_ref.at[blk],
            send_sem=send_b.at[step],
            recv_sem=recv_b.at[step],
            device_id=(other, row),
            device_id_type=MESH,
        )

    def start(step, unused):
        over_rows(step).start()
        return unused

    def finish(step, unused):
        over_rows(step).wait()
        return unused

    lax.fori_loop(1, nrows, start, 0)
    lax.fori_loop(1, nrows, finish, 0)
    for step in range(1, nblk):
        over_blk(step).start()
    for step in range(1, nblk):
        over_blk(step).wait()


def gather_all(vector, nblk, nrows):
    count = vector.shape[0] // LANES
    return pl.pallas_call(
        functools.partial(gather_kernel, nblk, nrows),
        out_shape=jax.ShapeDtypeStruct((nblk, nrows, count, LANES), f32),
        in_specs=[pl.BlockSpec(memory_space=pltpu.VMEM)],
        out_specs=pl.BlockSpec(memory_space=pltpu.VMEM),
        scratch_shapes=[
            pltpu.SemaphoreType.DMA((nrows,)),
            pltpu.SemaphoreType.DMA((nrows,)),
            pltpu.SemaphoreType.DMA((nblk,)),
            pltpu.SemaphoreType.DMA((nblk,)),
        ],
        compiler_params=pltpu.CompilerParams(collective_id=0, has_side_effects=True),
    )(vector.reshape(count, LANES))


class Place:
    def __init__(self):
        self.blk, self.row = lax.axis_index("blk"), lax.axis_index("rows")
        self.x, self.y = self.blk % 2, self.blk // 2
        self.core, self.z = self.row % 2, self.row // 2

    def along_blk(self, k):
        return (partner(self.blk, k), self.row)

    def along_rows(self, k):
        return (self.blk, partner(self.row, k))


class Sems:
    def __init__(self, send, recv):
        self.send, self.recv, self.used = send, recv, 0

    def take(self, count):
        self.used += count
        return self.used - count

    def copy(self, index, source, target, device):
        return remote(source, target, self.send.at[index], self.recv.at[index], *device)


def part(index, size, step):
    return pl.ds(pl.multiple_of(index * size, step), size)


class Piece:
    def __init__(self, place, sems, dims, bufs, whole=None, own=None, store=None):
        self.p, self.sems, self.base = place, sems, sems.take(self.SEMS)
        self.whole, self.own, self.store = whole, own, store
        self.b = types.SimpleNamespace(**bufs)
        self.nz, share, cols = dims
        self.hs, self.hc, self.hz = share // 2, cols // 2, self.nz // 2

    def start(self, stage):
        for copy in self.copies(stage):
            copy.start()

    def wait(self, stage):
        for copy in self.copies(stage):
            copy.wait()

    def run(self, stage, go_on=True):
        if stage:
            self.wait(stage - 1)
            self.add(stage)
        if stage < 5 and go_on:
            self.start(stage)


ROW_BUFS = ("core", "a1", "b1", "a2", "b2", "r3", "zr", "ag")
FAR_BUFS = ("core", "z1", "z2", "pr", "ag")


def shapes_of(names, shapes):
    return {name: pltpu.VMEM(shape, bf16) for name, shape in zip(names, shapes)}


class RowPiece(Piece):
    SEMS = 11

    @staticmethod
    def scratch(nz, share, cols):
        hs, hc = share // 2, cols // 2
        return shapes_of(
            ROW_BUFS,
            [
                (nz, share, cols), (nz // 2, share, hc), (nz // 2, hs, cols), (nz // 2, hs, hc), (nz // 2, hs, hc),
                (nz, hs, hc), (nz, hs, hc), (4, hs, hc),
            ],
        )

    def row(self, y):
        return part(y, self.hs, 16)

    def col(self, x):
        return part(x, self.hc, LANES)

    def copies(self, stage):
        p, at, b, copy = self.p, self.base, self.b, self.sems.copy
        low, high = slice(0, self.hz), slice(self.hz, self.nz)
        if stage == 0:
            return [copy(at, self.whole.at[:, 1 - p.core], b.core, p.along_rows(1))]
        if stage == 1:
            return [
                copy(at + 1, b.core.at[low, :, self.col(1 - p.x)], b.a1, p.along_blk(1)),
                copy(at + 2, b.core.at[high, self.row(1 - p.y), :], b.b1, p.along_blk(2)),
            ]
        if stage == 2:
            return [
                copy(at + 3, b.a1.at[:, self.row(1 - p.y), :], b.a2, p.along_blk(2)),
                copy(at + 4, b.b1.at[:, :, self.col(1 - p.x)], b.b2, p.along_blk(1)),
            ]
        if stage == 3:
            return [
                copy(at + 4 + k, b.r3.at[partner(p.z, k)], b.zr.at[p.z], p.along_rows(2 * k))
                for k in range(1, self.nz)
            ]
        return [copy(at + 7 + k, b.ag.at[p.blk], b.ag.at[p.blk], p.along_blk(k)) for k in range(1, 4)]

    def add(self, stage):
        p, b = self.p, self.b
        row, col = self.row(p.y), self.col(p.x)
        if stage == 1:
            b.core[...] = b.core[...] + self.own()
        if stage == 2:
            b.a1[...] = b.a1[...] + b.core[: self.hz, :, col]
            b.b1[...] = b.b1[...] + b.core[self.hz :, row, :]
        if stage == 3:
            b.r3[: self.hz] = b.a1[:, row, :] + b.a2[...]
            b.r3[self.hz :] = b.b1[:, :, col] + b.b2[...]
        if stage == 4:
            total = b.r3[p.z].astype(f32)
            for k in range(1, self.nz):
                total = total + b.zr[partner(p.z, k)].astype(f32)
            b.ag[p.blk] = total.astype(bf16)
        if stage == 5:
            for q in range(4):
                rows = slice(q // 2 * self.hs, (q // 2 + 1) * self.hs)
                self.store(rows, q % 2 * self.hc, b.ag[q])


class FarPiece(Piece):
    SEMS = 9

    @staticmethod
    def scratch(nz, share, cols):
        hs, hc = share // 2, cols // 2
        return shapes_of(
            FAR_BUFS,
            [(nz, share, cols), (nz // 2, share, cols), (share, cols), (4, hs, hc), (4, hs, hc)],
        )

    def quarter(self, blk):
        return (part(blk // 2, self.hs, 16), part(blk % 2, self.hc, LANES))

    def copies(self, stage):
        p, at, b, copy = self.p, self.base, self.b, self.sems.copy
        low, high = p.z % 2, p.z // 2
        if stage == 0:
            return [copy(at, self.whole.at[:, 1 - p.core], b.core, p.along_rows(1))]
        if stage == 1:
            return [
                copy(at + 1, b.core.at[1 - low], b.z1.at[0], p.along_rows(2)),
                copy(at + 2, b.core.at[3 - low], b.z1.at[1], p.along_rows(2)),
            ]
        if stage == 2:
            return [copy(at + 3, b.z1.at[1 - high], b.z2, p.along_rows(4))]
        if stage == 3:
            return [
                copy(at + 3 + k, b.z2.at[self.quarter(partner(p.blk, k))], b.pr.at[p.blk], p.along_blk(k))
                for k in range(1, 4)
            ]
        return [copy(at + 3 + k, b.ag.at[p.blk], b.ag.at[p.blk], p.along_blk(k)) for k in range(1, 4)]

    def add(self, stage):
        p, b = self.p, self.b
        low, high = p.z % 2, p.z // 2
        if stage == 1:
            b.core[...] = b.core[...] + self.own()
        if stage == 2:
            for i in range(2):
                b.z1[i] = b.z1[i] + b.core[2 * i + low]
        if stage == 3:
            b.z2[...] = b.z2[...] + b.z1[high]
        if stage == 4:
            rows, cols = self.quarter(p.blk)
            total = b.z2[rows, cols].astype(f32)
            for k in range(1, 4):
                total = total + b.pr[partner(p.blk, k)].astype(f32)
            b.ag[p.blk] = total.astype(bf16)
        if stage == 5:
            for q in range(4):
                rows = slice(q // 2 * self.hs, (q // 2 + 1) * self.hs)
                self.store(rows, q % 2 * self.hc, b.ag[q])


class ColPiece(Piece):
    SEMS = 12

    @staticmethod
    def scratch(nz, depth, cols):
        return shapes_of(
            ROW_BUFS[:6],
            [
                (2, 2, 2, depth, cols), (2, depth, cols), (2, depth, cols), (depth, cols), (depth, cols),
                (2, depth, cols),
            ],
        )

    @staticmethod
    def shared(nz, depth, cols):
        return shapes_of(("zr", "ag"), [(nz, 2, depth, cols), (4, 2, depth, cols)])

    def __init__(self, place, sems, dims, bufs, owner, **kinds):
        super().__init__(place, sems, dims, bufs, **kinds)
        self.owner = owner
        self.depth = dims[1]

    def copies(self, stage):
        p, at, b, copy = self.p, self.base, self.b, self.sems.copy
        if stage == 0:
            return [copy(at, self.whole.at[1 - p.core], b.core, p.along_rows(1))]
        if stage == 1:
            return [
                copy(at + 1, b.core.at[:, 1 - p.x, 0], b.a1, p.along_blk(1)),
                copy(at + 2, b.core.at[1 - p.y, :, 1], b.b1, p.along_blk(2)),
            ]
        if stage == 2:
            return [
                copy(at + 3, b.a1.at[1 - p.y], b.a2, p.along_blk(2)),
                copy(at + 4, b.b1.at[1 - p.x], b.b2, p.along_blk(1)),
            ]
        return [copy(at + 8 + k, b.ag.at[p.blk], b.ag.at[p.blk], p.along_blk(k)) for k in range(1, 4)]

    def over_z(self, k):
        device = (self.p.blk, 2 * self.owner + self.p.core)
        return self.sems.copy(self.base + 5 + k, self.b.r3, self.b.zr.at[self.p.z], device)

    def from_afar(self, k, what):
        @pl.when(self.p.z == self.owner ^ k)
        def far():
            what(self.over_z(k))

    def here(self, what):
        @pl.when(self.p.z == self.owner)
        def at_owner():
            what()

    def start(self, stage):
        if stage == 3:
            for k in range(1, 4):
                self.from_afar(k, lambda copy: copy.start())
        elif stage == 4:
            self.here(lambda: [copy.start() for copy in self.copies(4)] and None)
        else:
            super().start(stage)

    def wait(self, stage):
        if stage == 3:
            for k in range(1, 4):
                self.from_afar(k, lambda copy: copy.wait_send())
            self.here(lambda: [self.over_z(k).wait_recv() for k in range(1, 4)] and None)
        elif stage == 4:
            self.here(lambda: [copy.wait() for copy in self.copies(4)] and None)
        else:
            super().wait(stage)

    def add(self, stage):
        p, b = self.p, self.b
        if stage == 1:
            b.core[...] = b.core[...] + self.own()
        if stage == 2:
            b.a1[...] = b.a1[...] + b.core[:, p.x, 0]
            b.b1[...] = b.b1[...] + b.core[p.y, :, 1]
        if stage == 3:
            b.r3[0] = b.a1[p.y] + b.a2[...]
            b.r3[1] = b.b1[p.x] + b.b2[...]
        if stage == 4:
            def summed():
                total = b.r3[...].astype(f32)
                for k in range(1, 4):
                    total = total + b.zr[self.owner ^ k].astype(f32)
                b.ag[p.blk] = total.astype(bf16)
            self.here(summed)
        if stage == 5:
            def stored():
                for q in range(8):
                    self.store(slice(q * self.depth, (q + 1) * self.depth), b.ag[q // 2, q % 2])
            self.here(stored)


class Bag:
    def __init__(self):
        self.names, self.items = [], []

    def add(self, name, item):
        if isinstance(item, dict):
            for key, value in item.items():
                self.add(f"{name}.{key}", value)
        else:
            self.names.append(name)
            self.items.append(item)


def group(refs, name):
    return {key[len(name) + 1 :]: ref for key, ref in vars(refs).items() if key.startswith(name + ".")}


def only(shapes, names):
    return {name: shapes[name] for name in names if name in shapes}


class Plan:
    def __init__(self):
        self.actions = {}

    def at(self, point, *actions):
        self.actions.setdefault(point, []).extend(actions)

    def stages(self, piece, first, points):
        for number, point in enumerate(points):
            self.at(point, lambda number=first + number: piece.run(number))

    def run(self, point):
        for action in self.actions.get(point, []):
            action()

    def under(self, step, number, point):
        if point in self.actions:
            @pl.when(step == number)
            def actions():
                self.run(point)


EARLY, LATE = 64, 32


def write_lines(target, lines):
    target[...] = jnp.zeros_like(target)
    at = 0
    for line in lines:
        for k in range(line.shape[1] // LANES):
            target[at : at + 1, :] = line[:, k * LANES : (k + 1) * LANES]
            at += 1


FEED_POINTS = ((7, 11), (11, 16), (16,), ())
HANDED = {1: ("core",), 2: ("a1", "b1"), 3: ("r3",)}


def feed_move_kernel(names, *refs):
    r = types.SimpleNamespace(**dict(zip(names, refs)))
    step, last = pl.program_id(0), pl.num_programs(0) - 1
    place = Place()
    sems = Sems(r.send, r.recv)
    seq, width = r.x.shape
    wide = r.w_up.shape[1]
    nz, unused, share, cols = r.gu.shape[1:]
    depth, dcols = r.gd.shape[-2:]
    nrows = 2 * nz
    plan = Plan()

    ups, downs = [], []
    for i in range(4):
        side = i % 2
        ups.append(
            RowPiece(
                place, sems, (nz, share, cols), group(r, f"u{i}"), r.gu.at[side],
                lambda side=side: r.gu[side, :, place.core],
            )
        )
        bufs = group(r, f"d{i}")
        downs.append(
            ColPiece(
                place, sems, (nz, depth, dcols), bufs, i, whole=r.gd.at[side],
                own=lambda side=side: r.gd[side, place.core],
            )
        )
    for i, points in enumerate(FEED_POINTS):
        for kind, piece in (("up", ups[i]), ("down", downs[i])):
            plan.stages(piece, 1, points)
            if len(points) < 5:
                plan.at(20, lambda kind=kind, piece=piece, i=i, stage=len(points) + 1: hand_over(piece, stage, f"{kind}{i}"))

    def hand_over(piece, stage, name):
        piece.run(stage, False)
        for key in HANDED[stage]:
            getattr(r, f"{name}.{key}")[...] = getattr(piece.b, key)[...]

    gate_a, factor_m, shift_m, gate_m, b_down = vec_rows(r.vec, Vec.gate_a, Vec.factor_m, Vec.shift_m, Vec.gate_m, Vec.b_down)
    chunks = [slice(begin, begin + CHUNK) for begin in range(0, seq, CHUNK)]

    @pl.when(step == 0)
    def before():
        greet(place, 4, nrows)

        def enter(number, unused):
            rows = part(number, CHUNK, CHUNK)
            y = dot(r.ab[rows, :], r.w_out[...])
            r.y[rows, :] = y
            normed, unused = norm_rows(r.x[rows, :].astype(f32) + gate_a * y)
            hidden = normed * factor_m + shift_m
            r.h[rows, :] = hidden.astype(bf16)
            r.ht[:, rows] = hidden.T.astype(bf16)
            grad = gate_m * r.g[rows, :].astype(f32)
            r.dz[rows, :] = grad.astype(bf16)
            r.dzt[:, rows] = grad.T.astype(bf16)
            return 0

        lax.fori_loop(0, len(chunks), enter, 0)
        r.z[...] = jnp.zeros_like(r.z)
        r.dh[...] = jnp.zeros_like(r.dh)

    b_up = r.vec[pl.ds(Vec.b_up + step, 1), :]
    bias_sum = jnp.zeros((1, wide), f32)
    for number, rows in enumerate(chunks):
        for i in range(4):
            plan.under(step, i, 4 * i + number)
        act, du = feed_chunk(r.h[rows, :], r.dz[rows, :], r.w_up, b_up, r.w_down)
        r.act[rows, :] = act
        r.du[rows, :] = du
        bias_sum = bias_sum + jnp.sum(du.astype(f32), axis=0, keepdims=True)
        r.z[rows, :] += dot(act, r.w_down[...])
        r.dh[rows, :] += dot_nt(du, r.w_up[...])
    r.gb[pl.ds(step, 1), :] = bias_sum
    side = step % 2
    r.gu[side] = dot(r.ht[...], r.du[...]).astype(bf16).reshape(r.gu.shape[1:])
    down = dot(r.dzt[...], r.act[...]).astype(bf16)
    for core in range(2):
        half = down[:, core * dcols : (core + 1) * dcols]
        r.gd[side, core] = half.reshape(r.gd.shape[2:])
    for i in range(4):
        @pl.when(step == i)
        def sent():
            ups[i].run(0)
            downs[i].run(0)

    @pl.when(step == last)
    def after():
        plan.run(16)

        def leave(number, sums):
            rows = part(number, CHUNK, CHUNK)
            y = r.y[rows, :]
            middle = r.x[rows, :].astype(f32) + gate_a * y
            normed, inverse = norm_rows(middle)
            z = r.z[rows, :] + b_down
            r.result[rows, :] = (middle + gate_m * z).astype(bf16)
            grad = r.g[rows, :].astype(f32)
            dh = r.dh[rows, :]
            dx = grad + norm_back(dh * factor_m, normed, inverse)
            r.dx[rows, :] = dx
            dyb = (gate_a * dx).astype(bf16)
            r.dy[rows, :] = dyb
            r.datt[rows, :] = dot_nt(dyb, r.w_out[...]).astype(bf16)
            terms = (grad * z, dh, dh * normed, dx * y, r.dz[rows, :].astype(f32))
            return tuple(a + jnp.sum(b, axis=0, keepdims=True) for a, b in zip(sums, terms))

        sums = lax.fori_loop(0, len(chunks), leave, tuple(jnp.zeros((1, width), f32) for unused in range(5)))
        plan.run(18)
        r.g_out[...] = dot_tn(r.ab[...], r.dy[...]).astype(bf16)
        gain_m, scale_m, time = vec_rows(r.vec, Vec.gain_m, Vec.scale_m, Vec.step)
        dgate_m, dshift_m, along_m, dgate_a, grad_b_down = sums
        lines = [dgate_a, dshift_m, along_m * gain_m, dgate_m, along_m * (1.0 + scale_m), grad_b_down]
        lines += [r.gb[i : i + 1, :] for i in range(4)] + [time[:, :LANES]]
        write_lines(r.pack, lines)
        r.early[...] = r.pack[...].astype(bf16)
        plan.run(20)


def feed_move(ab, x, g, vec, w_out, w_up, w_down, nrows):
    seq, width = x.shape
    ff = w_up.shape[1]
    wide = width
    nz, share, depth, dcols = nrows // 2, width // nrows, width // 8, wide // 2
    once = pl.Buffered(buffer_count=1)
    fixed = lambda a: pl.BlockSpec(a.shape, lambda i: (0, 0), pipeline_mode=once)
    col = lambda r: pl.BlockSpec((r, wide), lambda i: (0, i))
    shape = jax.ShapeDtypeStruct
    ins, outs, scratch = Bag(), Bag(), Bag()
    for name, spec in (
        ("ab", fixed(ab)), ("x", fixed(x)), ("g", fixed(g)), ("vec", fixed(vec)), ("w_out", fixed(w_out)),
        ("w_up", col(width)), ("w_down", pl.BlockSpec((wide, width), lambda i: (i, 0))),
    ):
        ins.add(name, spec)
    for name, dims, kind in (
        ("result", (seq, width), bf16), ("dx", (seq, width), f32), ("datt", (seq, width), bf16),
        ("g_out", (width, width), bf16), ("early", (EARLY, LANES), bf16),
    ):
        outs.add(name, shape(dims, kind))
    row_bufs, col_bufs = RowPiece.scratch(nz, share, wide), ColPiece.scratch(nz, depth, dcols)
    for i, points in enumerate(FEED_POINTS):
        if len(points) < 5:
            for kind, bufs in (("up", row_bufs), ("down", col_bufs)):
                for key in HANDED[len(points) + 1]:
                    outs.add(f"{kind}{i}.{key}", shape(bufs[key].shape, bf16))
    for name in ("h", "dz", "act", "du", "dy"):
        scratch.add(name, pltpu.VMEM((seq, width), bf16))
    for name in ("ht", "dzt"):
        scratch.add(name, pltpu.VMEM((width, seq), bf16))
    for name in ("y", "z", "dh"):
        scratch.add(name, pltpu.VMEM((seq, width), f32))
    scratch.add("gb", pltpu.VMEM((8, wide), f32))
    scratch.add("pack", pltpu.VMEM((EARLY, LANES), f32))
    scratch.add("gu", pltpu.VMEM((2, nz, 2, share, wide), bf16))
    scratch.add("gd", pltpu.VMEM((2, 2, 2, 2, 2, depth, dcols), bf16))
    for i, points in enumerate(FEED_POINTS):
        kept = ROW_BUFS[: (1, 3, 6)[len(points)]]
        scratch.add(f"u{i}", only(row_bufs, kept))
        scratch.add(f"d{i}", only(col_bufs, kept))
    count = 4 * (RowPiece.SEMS + ColPiece.SEMS)
    scratch.add("send", pltpu.SemaphoreType.DMA((count,)))
    scratch.add("recv", pltpu.SemaphoreType.DMA((count,)))
    results = pl.pallas_call(
        functools.partial(feed_move_kernel, ins.names + outs.names + scratch.names),
        grid=(ff // wide,),
        in_specs=ins.items,
        out_specs=[pl.BlockSpec(o.shape, lambda i, n=len(o.shape): (0,) * n) for o in outs.items],
        out_shape=outs.items,
        scratch_shapes=scratch.items,
        compiler_params=pltpu.CompilerParams(collective_id=3, has_side_effects=True, vmem_limit_bytes=62 * MIB),
        cost_estimate=pl.CostEstimate(
            flops=12 * seq * width * ff, bytes_accessed=30 * seq * width, transcendentals=seq * ff
        ),
    )(ab, x, g, vec, w_out, w_up, w_down)
    return dict(zip(outs.names, results))


class Gather:
    def __init__(self, place, sems, source, target):
        self.p, self.sems, self.source, self.target = place, sems, source, target
        self.nblk, self.nrows = target.shape[:2]
        self.base = sems.take(self.nblk + self.nrows)

    def copies(self, stage):
        p = self.p
        if stage == 0:
            return [
                self.sems.copy(self.base + k, self.source, self.target.at[p.blk, p.row], p.along_rows(k))
                for k in range(1, self.nrows)
            ]
        return [
            self.sems.copy(self.base + self.nrows + k, self.target.at[p.blk], self.target.at[p.blk], p.along_blk(k))
            for k in range(1, self.nblk)
        ]

    def run(self, stage):
        if stage:
            for copy in self.copies(stage - 1):
                copy.wait()
        else:
            self.target[self.p.blk, self.p.row] = self.source[...]
        if stage < 2:
            for copy in self.copies(stage):
                copy.start()


class Return:
    def __init__(self, place, sems, source, target, local):
        self.p, self.sems, self.source, self.target, self.local = place, sems, source, target, local
        self.rows, self.nblk = target.shape[0], source.shape[0]
        self.base = sems.take(self.nblk)
        self.mine = jnp.minimum(place.blk, self.rows - 1)

    def copy(self, k):
        device = self.p.along_blk(k)
        return self.sems.copy(self.base + k, self.source.at[device[0]], self.target.at[self.mine], device)

    def own(self):
        return pltpu.make_async_copy(self.source.at[self.p.blk], self.target.at[self.mine], self.local)

    def start(self, ks):
        @pl.when(self.p.blk < self.rows)
        def sent():
            for k in ks:
                (self.copy(k) if k else self.own()).start()

    def finish(self):
        @pl.when(self.p.blk < self.rows)
        def left():
            self.own().wait()
            for k in range(1, self.nblk):
                self.copy(k).wait_send()

        for k in range(1, self.nblk):
            @pl.when(partner(self.p.blk, k) < self.rows)
            def arrived():
                self.copy(k).wait_recv()


def greet(place, nblk, nrows):
    barrier = pltpu.get_barrier_semaphore()
    for k in range(1, nblk):
        pl.semaphore_signal(barrier, inc=1, device_id=place.along_blk(k), device_id_type=MESH)
    for k in range(1, nrows):
        pl.semaphore_signal(barrier, inc=1, device_id=place.along_rows(k), device_id_type=MESH)
    pl.semaphore_wait(barrier, nblk + nrows - 2)


BEHIND_POINTS = ((8, 11), (8, 11), (6, 10, 13), (7, 10, 12, 15))
OUTER_POINTS = (5, 9, 11, 13, 15)
EARLY_POINTS = (8, 16)
RESULT_POINTS = (0, 0, 0, 0)
LATE_POINTS = ((9, 11, 13, 15, 16), (12, 13, 15, 17, 18), (12, 13, 15, 17, 19))


def behind_kernel(names, *refs):
    r = types.SimpleNamespace(**dict(zip(names, refs)))
    step, last = pl.program_id(0), pl.num_programs(0) - 1
    place = Place()
    sems = Sems(r.send, r.recv)
    nblk, stretch, width = r.x.shape
    nrows = r.early_g.shape[1]
    nz, unused, share, cols = r.gq.shape[1:]
    depth, dcols = getattr(r, "d.ag").shape[-2:]
    seq = nblk * stretch
    dims, ddims = (nz, share, cols), (nz, depth, dcols)

    def store_at(ref, begin):
        def store(rows, col, value):
            ref[rows, begin + col : begin + col + value.shape[1]] = value
        return store

    def store_qkv(j):
        def store(rows, col, value):
            for k in range(value.shape[1] // LANES):
                lane = col + k * LANES
                at = lane // (2 * LANES) * width + j * 2 * LANES + lane % (2 * LANES)
                r.share_qkv[rows, at : at + LANES] = value[:, k * LANES : (k + 1) * LANES]
        return store

    def store_down(rows, value):
        r.share_down[rows, :] = value

    shared = group(r, "d")
    carried = []
    for i, points in enumerate(FEED_POINTS):
        if len(points) < 5:
            up = RowPiece(
                place, sems, dims, dict(group(r, f"u{i}"), **group(r, f"up{i}")), store=store_at(r.share_up, i * cols)
            )
            down = ColPiece(
                place, sems, ddims, dict(shared, **group(r, f"d{i}"), **group(r, f"down{i}")), i, store=store_down
            )
            carried.append((len(points) + 1, up, down))
    outer = RowPiece(
        place, sems, dims, group(r, "o"), r.g_out, lambda: r.own_out[...], store_at(r.share_out, 0)
    )
    load = pltpu.make_async_copy(r.g_out.at[:, place.core], r.own_out, r.local.at[2])
    late_pieces = [
        kind(
            place, sems, dims, group(r, f"q{j}"), r.gq.at[j], lambda j=j: r.gq[j, :, place.core], store_qkv(j)
        )
        for j, kind in enumerate((RowPiece, RowPiece, RowPiece))
    ]
    results = Return(place, sems, r.result, r.tok_out, r.local.at[0])
    grads = Return(place, sems, r.gt, r.grad_out, r.local.at[1])
    early = Gather(place, sems, r.early_s, r.early_g)
    late = Gather(place, sems, r.late_b, r.late_g)

    def open_up():
        greet(place, nblk, nrows)
        load.start()
        for stage, up, down in carried:
            up.start(stage)
            down.start(stage)
        outer.run(0)
        r.share_down[...] = jnp.zeros_like(r.share_down)

    def start_early():
        r.early_s[...] = r.early[...]
        early.run(0)

    plan = Plan()
    plan.at(0, open_up)
    plan.at(1, start_early, load.wait)
    for (stage, up, down), points in zip(carried, BEHIND_POINTS):
        for piece in (up, down):
            plan.stages(piece, stage + 1, points)
    plan.stages(outer, 1, OUTER_POINTS)
    plan.stages(early, 1, EARLY_POINTS)
    for k, point in zip((3, 1, 2, 0), RESULT_POINTS):
        plan.at(point, lambda k=k: results.start([k]))
    for piece, points in zip(late_pieces, LATE_POINTS):
        plan.stages(piece, 1, points)

    for i in range(6):
        plan.under(step, i, 2 * i)
    side = step % 2 * LANES

    def store(rows, *grads):
        for i, grad in enumerate(grads):
            r.dqkv[rows, pl.ds(pl.multiple_of(2 * i * LANES + side, LANES), LANES)] = grad

    attend_back_pair(r, store)
    for i in range(6):
        plan.under(step, i, 2 * i + 1)

    @pl.when(step % 2 == 1)
    def projections():
        number = step // 2
        grad_w = dot(r.ht[...], r.dqkv[...]).astype(bf16)
        r.gq[number] = grad_w.reshape(r.gq.shape[1:])
        for j, piece in enumerate(late_pieces):
            @pl.when(number == j)
            def sent():
                piece.run(0)

        @pl.when(number == 0)
        def fresh():
            r.dh[...] = jnp.zeros_like(r.dh)

        def onto(begin, unused):
            rows = part(begin, CHUNK, CHUNK)
            added = dot_nt(r.dqkv[rows, : 2 * LANES], r.wq[...])
            added = added + dot_nt(r.dqkv[rows, 2 * LANES : 4 * LANES], r.wk[...])
            r.dh[rows, :] += added + dot_nt(r.dqkv[rows, 4 * LANES :], r.wv[...])
            return unused

        lax.fori_loop(0, seq // CHUNK, onto, 0)

    @pl.when(step == last)
    def tail():
        factor, gain, scale = vec_rows(r.vec, Vec.factor_a, Vec.gain_a, Vec.scale_a)
        total = [jnp.zeros((1, width), f32) for unused in range(2)]

        def chunk(k):
            slot = partner(place.blk, k)
            rows = pl.ds(pl.multiple_of(slot * stretch, stretch), stretch)
            normed, inverse = norm_rows(r.x[slot].astype(f32))
            dh = r.dh[rows, :]
            r.gt[slot] = (r.dx[rows, :] + norm_back(dh * factor, normed, inverse)).astype(bf16)
            grads.start([k])
            total[0] = total[0] + jnp.sum(dh, axis=0, keepdims=True)
            total[1] = total[1] + jnp.sum(dh * normed, axis=0, keepdims=True)

        plan.run(12)
        chunk(3)
        plan.run(13)
        chunk(1)
        plan.run(14)
        chunk(2)
        chunk(0)
        write_lines(r.late_s, (total[0], total[1] * gain, total[1] * (1.0 + scale)))
        r.late_b[...] = r.late_s[...].astype(bf16)
        late.run(0)
        plan.run(15)
        plan.run(16)
        r.early_out[...] = r.early_g[...]
        late.run(1)
        plan.run(17)
        late.run(2)
        r.late_out[...] = r.late_g[...]
        plan.run(18)
        plan.run(19)
        results.finish()
        grads.finish()


def behind(q, k, v, grads, att, inv, eb, cosine, sine, w_qkv, hidden_t, x, dx, vec, early, handed, g_out, result,
           rows_dev, nrows):
    seq, width = q.shape
    nblk, stretch, unused = x.shape
    nz, share, cols, depth, dcols = nrows // 2, width // nrows, width, width // 8, width // 2
    pair = pl.BlockSpec((seq, LANES), lambda i: (0, i))
    once = pl.Buffered(buffer_count=1)
    fixed = lambda a: pl.BlockSpec(a.shape, lambda i: (0,) * len(a.shape), pipeline_mode=once)
    away = pl.BlockSpec(memory_space=pl.ANY)
    per = width // (2 * LANES)
    weight = lambda n: pl.BlockSpec((width, 2 * LANES), lambda i: (0, n * per + i // 2))
    shape = jax.ShapeDtypeStruct
    ins, args, outs, scratch = Bag(), [], Bag(), Bag()
    for name, spec, value in (
        ("q", pair, q), ("k", pair, k), ("v", pair, v), ("datt", pair, grads), ("att", pair, att), ("inv", pair, inv),
        ("eb", pl.BlockSpec((1, 2, seq, seq), lambda i: (i, 0, 0, 0)), eb), ("cos", fixed(cosine), cosine), ("sin", fixed(sine), sine),
        ("wq", weight(0), w_qkv), ("wk", weight(1), w_qkv), ("wv", weight(2), w_qkv),
        ("ht", fixed(hidden_t), hidden_t), ("x", fixed(x), x), ("dx", fixed(dx), dx), ("vec", fixed(vec), vec),
        ("early", fixed(early), early), *((name, fixed(value), value) for name, value in handed.items()),
        ("g_out", away, g_out), ("result", away, result),
    ):
        ins.add(name, spec)
        args.append(value)
    back = shape((rows_dev, stretch, width), bf16)
    late = (LATE, LANES)
    for name, value in (
        ("tok_out", back), ("grad_out", back), ("share_qkv", shape((share, 3 * width), bf16)),
        ("share_out", shape((share, cols), bf16)), ("share_up", shape((share, 4 * cols), bf16)),
        ("share_down", shape((8 * depth, dcols), bf16)),
        ("early_out", shape((nblk, nrows) + early.shape, bf16)), ("late_out", shape((nblk, nrows) + late, bf16)),
    ):
        outs.add(name, value)
    for name, dims, kind in (
        ("da", (2, seq, LANES), bf16), ("ds", (2, seq, seq), bf16),
        ("dqkv", (seq, 6 * LANES), bf16), ("dh", (seq, width), f32), ("gq", (3, nz, 2, share, cols), bf16),
        ("gt", (nblk, stretch, width), bf16), ("early_s", early.shape, bf16), ("late_s", late, f32),
        ("late_b", late, bf16), ("early_g", (nblk, nrows) + early.shape, bf16),
        ("late_g", (nblk, nrows) + late, bf16), ("own_out", (nz, share, cols), bf16),
    ):
        scratch.add(name, pltpu.VMEM(dims, kind))
    near, cross = RowPiece.scratch(nz, share, cols), ColPiece.scratch(nz, depth, dcols)
    for i, points in enumerate(FEED_POINTS):
        if len(points) < 5:
            kept = ROW_BUFS[(1, 3, 6)[len(points)] :]
            scratch.add(f"u{i}", only(near, kept))
            scratch.add(f"d{i}", only(cross, kept))
    scratch.add("d", ColPiece.shared(nz, depth, dcols))
    scratch.add("o", near)
    for j in range(3):
        scratch.add(f"q{j}", near)
    count = 8 * RowPiece.SEMS + 4 * ColPiece.SEMS + 2 * nblk + 2 * (nblk + nrows)
    scratch.add("send", pltpu.SemaphoreType.DMA((count,)))
    scratch.add("recv", pltpu.SemaphoreType.DMA((count,)))
    scratch.add("local", pltpu.SemaphoreType.DMA((3,)))
    results = pl.pallas_call(
        functools.partial(behind_kernel, ins.names + outs.names + scratch.names),
        grid=(width // LANES,),
        in_specs=ins.items,
        out_specs=[away, away] + [pl.BlockSpec(o.shape, lambda i, n=len(o.shape): (0,) * n) for o in outs.items[2:]],
        out_shape=outs.items,
        scratch_shapes=scratch.items,
        compiler_params=pltpu.CompilerParams(collective_id=2, has_side_effects=True, vmem_limit_bytes=62 * MIB),
        cost_estimate=pl.CostEstimate(
            flops=52 * seq * seq * width, bytes_accessed=40 * seq * width, transcendentals=H * seq * seq
        ),
    )(*args)
    return dict(zip(outs.names, results))


FETCH = ("tok", "grad", "early", "late", "table", "ada", "up", "qkv", "outer", "down")


def finish_kernel(names, *refs):
    r = types.SimpleNamespace(**dict(zip(names, refs)))
    row = lax.axis_index("rows")
    loads = {name: pltpu.make_async_copy(getattr(r, name + "_in"), getattr(r, name), r.local.at[i]) for i, name in enumerate(FETCH)}
    for load in loads.values():
        load.start()
    moves = []
    for i, (name, target) in enumerate((("tok", r.out), ("grad", r.grad_tokens))):
        loads[name].wait()
        moves.append(pltpu.make_async_copy(getattr(r, name), target, r.local.at[len(FETCH) + i]))
        moves[-1].start()
    for name in ("early", "late", "table", "ada"):
        loads[name].wait()
    rows_dev = r.out.shape[0]
    nblk, nrows = r.early.shape[:2]
    count = rows_dev * nrows
    width = r.out.shape[-1]
    per = width // LANES
    for b in range(rows_dev):
        r.early_s[b] = r.early[b].astype(f32)
        r.late_s[b] = r.late[b].astype(f32)
    r.mod[...] = jnp.zeros_like(r.mod)

    def of_all(ref, line):
        return [ref[b, :, line, :] for b in range(rows_dev)]

    for i in range(6 * per):
        blocks = of_all(r.late_s, i) if i < 2 * per else of_all(r.early_s, i - 2 * per)
        for b, block in enumerate(blocks):
            r.mod[b * nrows : (b + 1) * nrows, i * LANES : (i + 1) * LANES] = block
    total = jnp.sum(r.early_s[...], axis=(0, 1))
    late_total = jnp.sum(r.late_s[...], axis=(0, 1))

    ff = r.b_up.shape[0]
    r.gain_m[...] = total[4 * per : 5 * per]
    r.b_down[...] = total[5 * per : 6 * per]
    r.b_up[...] = total[6 * per : 6 * per + ff]
    r.gain_a[...] = late_total[2 * per : 3 * per]
    r.b_ada[: 2 * per, :] = late_total[: 2 * per]
    r.b_ada[2 * per :, :] = total[: 4 * per]
    mod = r.mod[...]
    mod_b = mod.astype(bf16)
    steps = r.steps
    steps[...] = jnp.full(steps.shape, -1.0, f32)
    for b, block in enumerate(of_all(r.early_s, 6 * per + ff)):
        steps[b * nrows : (b + 1) * nrows, :] = block
    entries = r.table.shape[0]
    hot = (steps[:, :entries] == lane_of((1, entries)).astype(f32)).astype(f32).astype(bf16)
    conds = dot(hot, r.table[...])
    r.act_t[...] = jnp.concatenate([silu(conds), jnp.zeros((LANES - conds.shape[0], conds.shape[1]), f32)]).T
    share = r.w_ada.shape[0]
    mine = r.act_t[pl.ds(pl.multiple_of(row * share, share), share), : conds.shape[0]]
    r.w_ada[...] = sum(dot(term, mod_b) for term in in_three(mine))
    grad_act = dot_nt(mod_b, r.ada[...])
    sigmoid = 1.0 / (1.0 + jnp.exp(-conds))
    grad_cond = grad_act * sigmoid * (1.0 + conds * (1.0 - sigmoid))
    r.grad_table[...] = sum(dot_tn(hot, term) for term in in_three(grad_cond))
    for name in ("up", "qkv", "outer", "down"):
        loads[name].wait()
    r.w_up[...] = r.up[...].astype(f32)
    r.w_qkv[...] = r.qkv[...].astype(f32)
    r.w_out[...] = r.outer[...].astype(f32)

    r.w_down[...] = r.down[...].astype(f32).T
    for move in moves:
        move.wait()


def finish(o, table, w_ada):
    rows_dev, stretch, width = o["tok_out"].shape
    nblk, nrows = o["early_out"].shape[:2]
    shape = jax.ShapeDtypeStruct
    away, near = pl.BlockSpec(memory_space=pl.ANY), pl.BlockSpec(memory_space=pltpu.VMEM)
    args, outs, scratch = [], Bag(), Bag()
    fetched = dict(
        tok=o["tok_out"], grad=o["grad_out"], early=o["early_out"], late=o["late_out"], table=table, ada=w_ada,
        up=o["share_up"], qkv=o["share_qkv"], outer=o["share_out"], down=o["share_down"],
    )
    for name in FETCH:
        args.append(fetched[name])
        scratch.add(name, pltpu.VMEM(fetched[name].shape, fetched[name].dtype))
    names = [name + "_in" for name in FETCH] + ["out", "grad_tokens"]
    six, share, per = 6 * width, width // nrows, width // LANES
    ff = o["share_up"].shape[1]
    for name, dims in (
        ("grad_table", table.shape), ("w_ada", (w_ada.shape[0] // nrows, six)), ("b_ada", (6 * per, LANES)),
        ("gain_a", (per, LANES)), ("w_qkv", (share, 3 * width)), ("w_out", (share, width)), ("gain_m", (per, LANES)),
        ("w_up", (share, ff)), ("b_up", (ff // LANES, LANES)), ("w_down", (ff // nrows, width)),
        ("b_down", (per, LANES)),
    ):
        outs.add(name, shape(dims, f32))
    lines = 32
    for name, dims in (
        ("early_s", (rows_dev, nrows, EARLY, LANES)), ("late_s", (rows_dev, nrows, LATE, LANES)), ("mod", (lines, six)),
        ("steps", (lines, LANES)), ("act_t", (LANES, LANES)),
    ):
        scratch.add(name, pltpu.VMEM(dims, f32))
    scratch.add("local", pltpu.SemaphoreType.DMA((2 + len(FETCH),)))
    moved = shape((rows_dev, stretch, width), bf16)
    return pl.pallas_call(
        functools.partial(finish_kernel, names + outs.names + scratch.names),
        in_specs=[away] * len(args),
        out_specs=[away, away] + [near] * len(outs.items),
        out_shape=[moved, moved] + outs.items,
        scratch_shapes=scratch.items,
        compiler_params=pltpu.CompilerParams(vmem_limit_bytes=62 * MIB),
    )(*args)


def rows_out(whole, rows, me, nblk):
    parts = [lax.dynamic_index_in_dim(whole, me, 0, keepdims=False)]
    for k in range(1, nblk):
        part = lax.dynamic_index_in_dim(whole, me ^ k, 0, keepdims=False)
        pairs = [(s, s ^ k) for s in range(nblk) if s < rows]
        parts.append(lax.ppermute(part, "blk", pairs))
    stacked = jnp.stack(parts)
    return jnp.take(stacked, jnp.arange(rows) ^ me, axis=0)


def pick(array, index, axis=0):
    return lax.dynamic_index_in_dim(array, index, axis, keepdims=False)


def xor_move(array, axis, size, k):
    return lax.ppermute(array, axis, [(s, s ^ k) for s in range(size)])


def halve(array, axis, bit, name, size, k):
    kept = pick(array, bit, axis).astype(f32)
    sent = pick(array, 1 - bit, axis)
    return (kept + xor_move(sent, name, size, k).astype(f32)).astype(bf16)


def reduce_weight(grad, blk, row, nblk, nrows):
    total, cols = grad.shape
    share = total // nrows
    nz = nrows // 2
    core, z = row % 2, row // 2
    x, y = blk % 2, blk // 2
    part = halve(grad.reshape(nz, 2, share, cols), 1, core, "rows", nrows, 1)
    part = part.reshape(nz, 2, share // 2, cols)
    front, back = part[: nz // 2], part[nz // 2 :]
    split = lambda a: jnp.stack([a[..., : cols // 2], a[..., cols // 2 :]])
    front = halve(split(front), 0, x, "blk", nblk, 1)
    back = halve(back, 1, y, "blk", nblk, 2)
    front = halve(front, 1, y, "blk", nblk, 2)
    back = halve(split(back), 0, x, "blk", nblk, 1)
    part = jnp.concatenate([front, back], axis=0)
    if nz <= 4:
        summed = pick(part, z).astype(f32)
        for k in range(1, nz):
            summed = summed + xor_move(pick(part, z ^ k), "rows", nrows, 2 * k).astype(f32)
        part = summed.astype(bf16)
    else:
        k = nz // 2
        while k:
            pairs = part.reshape((2, k) + part.shape[1:])
            part = halve(pairs, 0, (z // k) % 2, "rows", nrows, 2 * k)
            k //= 2
        part = part[0]
    quarters = [part] + [xor_move(part, "blk", nblk, k) for k in range(1, 4)]
    quarters = jnp.take(jnp.stack(quarters), jnp.arange(4) ^ blk, axis=0)
    ordered = quarters.reshape(2, 2, share // 2, cols // 2).transpose(0, 2, 1, 3)
    return ordered.reshape(share, cols).astype(f32)


def per_device(
    tokens, timesteps, lengths, time_table, w_ada, b_ada, gain_attn, w_qkv, w_out, gain_mlp, w_up, b_up,
    w_down, b_down, grad_out
):
    rows_dev, stretch, width = tokens.shape
    nblk, nrows = lax.axis_size("blk"), lax.axis_size("rows")
    blk, row = lax.axis_index("blk"), lax.axis_index("rows")
    seq = stretch * nblk

    x_blocks, g_blocks, hidden_t, q, k, v, cosine, sine, attended, inv, attended_b, eb, vec = ahead(
        tokens, grad_out, w_qkv, w_ada, lengths, timesteps, time_table, b_ada, gain_attn, gain_mlp, b_down, b_up, nblk
    )
    x_row = x_blocks.reshape(seq, width)

    ff = b_up.shape[0]
    fed = (attended_b, x_row, g_blocks.reshape(seq, width), vec, w_out, w_up, w_down)

    if (nblk, nrows) == (4, 8):
        f = feed_move(*fed, nrows)
        nz, share = nrows // 2, width // nrows
        o = behind(
            q, k, v, f["datt"], attended, inv, eb, cosine, sine, w_qkv, hidden_t, x_blocks, f["dx"], vec, f["early"],
            {name: value for name, value in f.items() if "." in name}, f["g_out"].reshape(nz, 2, share, width),
            f["result"].reshape(nblk, stretch, width), rows_dev, nrows,
        )
        out, grad_tokens, *rest = finish(o, time_table, w_ada)
        flat = (2, 3, 6, 8, 10)
        return (out, grad_tokens, *(value.reshape(-1) if i in flat else value for i, value in enumerate(rest)))

    shift_a, scale_a, gate_a, shift_m, scale_m, gate_m, factor_a, factor_m, gain_a, gain_m, step = vec[:11]
    result, grad_mid, grad_att, grad_w_out, grad_w_up, grad_w_down, gb_up, sums = feed(*fed)
    dgate_m, dshift_m, along_m, dgate_a, grad_b_down = (sums[i] for i in range(5))
    out = rows_out(result.reshape(nblk, stretch, width), rows_dev, blk, nblk)
    share_w_down = reduce_weight(grad_w_down.transpose(2, 0, 1, 3).reshape(width, ff).T, blk, row, nblk, nrows)
    share_w_up = reduce_weight(grad_w_up.transpose(1, 0, 2).reshape(width, ff), blk, row, nblk, nrows)
    share_w_out = reduce_weight(grad_w_out, blk, row, nblk, nrows)
    dq, dk, dv = attend_back(q, k, v, grad_att, attended, inv, eb, cosine, sine)
    grad_qkv = jnp.concatenate([dq, dk, dv], axis=-1)
    grad_w_qkv = dot(hidden_t, grad_qkv).astype(bf16)
    share_w_qkv = reduce_weight(grad_w_qkv, blk, row, nblk, nrows)
    grad_ha = dot_nt(grad_qkv, w_qkv)
    normed_a, inverse_a = norm_rows(x_row.astype(f32))
    along_a = jnp.sum(grad_ha * normed_a, axis=0)
    grad_in = (grad_mid + norm_back(grad_ha * factor_a, normed_a, inverse_a)).astype(bf16)
    grad_tokens = rows_out(grad_in.reshape(nblk, stretch, width), rows_dev, blk, nblk)
    count = 6 * width + ff + LANES
    packed = jnp.concatenate(
        [
            dgate_a, dshift_m, along_m * gain_m, dgate_m, along_m * (1.0 + scale_m), grad_b_down, gb_up[0],
            step[:LANES], jnp.sum(grad_ha, axis=0), along_a * gain_a, along_a * (1.0 + scale_a),
        ]
    )
    gathered = gather_all(packed, nblk, nrows).reshape(nblk, nrows, -1)
    early = gathered[:rows_dev].reshape(rows_dev * nrows, -1)
    dshift_a, dscale_a, part_gain_a = (early[:, count + i * width : count + (i + 1) * width] for i in range(3))

    table, ada_full = time_table.astype(f32), w_ada.astype(f32)
    grad_mod = jnp.concatenate([dshift_a, dscale_a, early[:, : 4 * width]], axis=-1)
    smalls = jnp.sum(early, axis=0)
    grad_gain_m, total_b_down = smalls[4 * width : 5 * width], smalls[5 * width : 6 * width]
    total_b_up = smalls[6 * width : 6 * width + ff]
    steps = early[:, 6 * width + ff].astype(jnp.int32)
    onehot = (steps[:, None] == jnp.arange(table.shape[0], dtype=jnp.int32)[None, :]).astype(f32)
    conds = jnp.dot(onehot, table, precision=highest)
    share = conds.shape[1] // nrows
    my_conds = lax.dynamic_slice_in_dim(conds, row * share, share, axis=1)
    grad_w_ada = jnp.dot(jax.nn.silu(my_conds).T, grad_mod, precision=highest)
    grad_cond_act = lax.dot_general(
        grad_mod, ada_full, (((1,), (1,)), ((), ())), precision=highest, preferred_element_type=f32
    )
    sigmoid = jax.nn.sigmoid(conds)
    grad_cond = grad_cond_act * sigmoid * (1.0 + conds * (1.0 - sigmoid))
    grad_table = jnp.dot(onehot.T, grad_cond, precision=highest)
    return (
        out,
        grad_tokens,
        grad_table,
        grad_w_ada,
        jnp.sum(grad_mod, axis=0),
        jnp.sum(part_gain_a, axis=0),
        share_w_qkv,
        share_w_out,
        grad_gain_m,
        share_w_up,
        total_b_up,
        share_w_down,
        total_b_down,
    )


def solution(mesh):
    whole, split = P(), P("rows", None)
    tokens = P("rows", "blk", None)
    return jax.shard_map(
        per_device,
        mesh=mesh,
        in_specs=(tokens, P("rows"), split) + (whole,) * 11 + (tokens,),
        out_specs=(
            tokens, tokens, whole, split, whole, whole, split, split, whole, split, whole, split, whole
        ),
        check_vma=False,
    )
```

```python
import functools
import math
import types

import jax
import jax.numpy as jnp
import numpy as np
from jax import lax
from jax.experimental import pallas as pl
from jax.experimental.pallas import tpu as pltpu
from jax.sharding import PartitionSpec as P

H = 12
NDOC = 8
LANES = 128
CHUNK = 256
MIB = 1 << 20

epsilon = 1e-05
highest = lax.Precision.HIGHEST
bf16 = jnp.bfloat16
f32 = jnp.float32
MESH = pl.DeviceIdType.MESH


def dot(a, b):
    return jnp.dot(a, b, preferred_element_type=f32)


def dot_nt(a, b):
    return lax.dot_general(a, b, (((1,), (1,)), ((), ())), preferred_element_type=f32)


def dot_tn(a, b):
    return lax.dot_general(a, b, (((0,), (0,)), ((), ())), preferred_element_type=f32)


def norm_rows(values):
    centre = jnp.mean(values, axis=-1, keepdims=True)
    centred = values - centre
    spread = jnp.mean(centred * centred, axis=-1, keepdims=True)
    inverse = lax.rsqrt(spread + epsilon)
    return (centred * inverse, inverse)


def norm_back(grad_normed, normed, inverse):
    first = jnp.mean(grad_normed, axis=-1, keepdims=True)
    second = jnp.mean(grad_normed * normed, axis=-1, keepdims=True)
    return inverse * (grad_normed - first - normed * second)


def lane_of(shape):
    return lax.broadcasted_iota(jnp.int32, shape, len(shape) - 1)


def swap_halves(values, half):
    lane = lane_of(values.shape)
    width = values.shape[-1]
    ahead = pltpu.roll(values, width - half, values.ndim - 1)
    behind = pltpu.roll(values, half, values.ndim - 1)
    return jnp.where(lane % (2 * half) < half, ahead, behind)


def in_three(values):
    high = values.astype(bf16)
    rest = values - high.astype(f32)
    middle = rest.astype(bf16)
    low = (rest - middle.astype(f32)).astype(bf16)
    return (high, middle, low)


def partner(blk, k):
    other = blk
    bit = 1
    while bit <= k:
        if k & bit:
            other = other + bit - 2 * bit * (other // bit % 2)
        bit *= 2
    return other


def remote(source, target, send, recv, blk, row):
    return pltpu.make_async_remote_copy(
        src_ref=source, dst_ref=target, send_sem=send, recv_sem=recv, device_id=(blk, row), device_id_type=MESH
    )


class Vec:
    shift_a, scale_a, gate_a, shift_m, scale_m, gate_m, factor_a, factor_m, gain_a, gain_m, step, b_down, b_up = range(13)


def silu(values):
    return values / (1.0 + jnp.exp(-values))


def ahead_kernel(
    tok_ref, grad_ref, w_ref, ada_ref, lengths_ref, steps_ref, table_ref, b_ada_ref, gain_a_ref, gain_m_ref, b_down_ref, b_up_ref, freq_ref,
    x_out, g_out, ht_out, q_out, k_out, v_out, cos_out, sin_out, att_ref, inv_ref, ab_ref, eb_ref, vec_ref,
    x_s, own_s, ht_s, q_s, k_s, v_s, cos_s, sin_s, w_s, ada_s, fq_s, fk_s, zero_s, send_x, recv_x, send_g, recv_g, local
):
    step, last = pl.program_id(0), pl.num_programs(0) - 1
    blk, row = lax.axis_index("blk"), lax.axis_index("rows")
    rows_dev, stretch, width = tok_ref.shape
    nblk = x_s.shape[0]
    half = width // H // 2
    scale = 1.0 / math.sqrt(2 * half)
    has_row = blk < rows_dev
    mine = jnp.minimum(blk, rows_dev - 1)
    kept = (
        (x_s, x_out), (ht_s, ht_out), (q_s, q_out), (k_s, k_out), (v_s, v_out), (cos_s, cos_out), (sin_s, sin_out)
    )
    free = len(kept)

    def move(k, source, target, send, recv, other):
        return remote(source.at[jnp.minimum(other, rows_dev - 1)], target.at[blk], send.at[k], recv.at[k], other, row)

    def each_sent(source, target, send, recv, what):
        for k in range(1, nblk):
            other = partner(blk, k)

            @pl.when(other < rows_dev)
            def sent():
                what(move(k, source, target, send, recv, other))

    def store(i):
        return pltpu.make_async_copy(kept[i][0], kept[i][1], local.at[i])

    def own_grad():
        return pltpu.make_async_copy(grad_ref.at[mine], g_out.at[blk], local.at[free + 3])

    def chunk(source):
        rows = pl.ds(pl.multiple_of(source * stretch, stretch), stretch)
        normed, unused = norm_rows(x_s[source].astype(f32))
        hidden = normed * vec(Vec.factor_a) + vec(Vec.shift_a)
        hidden_b = hidden.astype(bf16)
        ht_s[:, rows] = hidden.T.astype(bf16)
        cosine, sine = cos_s[rows, :], sin_s[rows, :]
        for part in range(3):
            out = dot(hidden_b, w_s[:, part * width : (part + 1) * width])
            for group in range(width // LANES):
                cols = slice(group * LANES, (group + 1) * LANES)
                piece = out[:, cols]
                if part == 2:
                    v_s[rows, cols] = piece.astype(bf16)
                    continue
                turned = (piece * cosine + swap_halves(piece, half) * sine).astype(bf16)
                if part == 0:
                    q_s[rows, cols] = (turned.astype(f32) * scale).astype(bf16)
                else:
                    k_s[rows, cols] = turned

    def vec(at):
        return vec_ref[at : at + 1, :]

    def prepare():
        wide = table_ref.shape[0]
        time = steps_ref[mine]
        hot = (lane_of((16, wide)) == time).astype(f32).astype(bf16)
        terms = in_three(silu(dot(hot, table_ref[...])))
        line = lax.broadcasted_iota(jnp.int32, (16, 1), 0)
        three = jnp.zeros(terms[0].shape, f32)
        for i, term in enumerate(terms):
            three = jnp.where(line == i, term.astype(f32), three)
        modulate = jnp.sum(dot(three.astype(bf16), ada_s[...]), axis=0, keepdims=True)
        flat = lambda ref: jnp.concatenate([ref[i : i + 1, :] for i in range(ref.shape[0])], axis=1).astype(f32)
        modulate = modulate + flat(b_ada_ref)
        gains = [flat(gain_a_ref), flat(gain_m_ref)]
        rows = [modulate[:, i * width : (i + 1) * width] for i in range(6)]
        rows += [gains[0] * (1.0 + rows[1]), gains[1] * (1.0 + rows[4])] + gains
        rows += [jnp.full((1, width), time, jnp.int32).astype(f32), flat(b_down_ref)]
        b_up = flat(b_up_ref)
        rows += [b_up[:, i * width : (i + 1) * width] for i in range(b_up.shape[1] // width)]
        vec_ref[...] = jnp.zeros_like(vec_ref)
        for i, value in enumerate(rows):
            vec_ref[i : i + 1, :] = value
        shape = fq_s.shape
        slots = lax.broadcasted_iota(jnp.int32, shape, 0)
        feature = lane_of(shape) % (2 * half)
        doc, start = jnp.zeros(shape, jnp.int32), jnp.zeros(shape, jnp.int32)
        last_end = jnp.int32(0)
        for i in range(lengths_ref.shape[1]):
            last_end = last_end + lengths_ref[mine, i]
            past = slots >= last_end
            doc = doc + past.astype(jnp.int32)
            start = jnp.where(past, last_end, start)
        fq_s[...] = jnp.where(feature == doc, -1e30, 0.0).astype(bf16)
        fk_s[...] = jnp.where((feature == doc) | (feature >= NDOC), 0.0, 1.0).astype(bf16)
        angle = (slots - start).astype(f32) * freq_ref[...]
        cos_s[...] = jnp.cos(angle)
        sine = jnp.sin(angle)
        sin_s[...] = jnp.where(feature < half, -sine, sine)

    @pl.when(step == 0)
    def begin():
        barrier = pltpu.get_barrier_semaphore()
        for k in range(1, nblk):
            pl.semaphore_signal(barrier, inc=1, device_id=(partner(blk, k), row), device_id_type=MESH)
        ada = pltpu.make_async_copy(ada_ref, ada_s, local.at[free])
        weights = pltpu.make_async_copy(w_ref, w_s, local.at[free + 1])
        own = pltpu.make_async_copy(tok_ref.at[mine], own_s, local.at[free + 2])
        for copy in (ada, weights, own):
            copy.start()
        pl.semaphore_wait(barrier, nblk - 1)
        each_sent(tok_ref, x_s, send_x, recv_x, lambda copy: copy.start())
        ada.wait()
        prepare()
        own.wait()

        @pl.when(has_row)
        def mine_first():
            x_s[blk] = own_s[...]

        @pl.when(jnp.logical_not(has_row))
        def nothing():
            x_s[...] = jnp.zeros_like(x_s)

        weights.wait()
        for k in range(nblk):
            source = partner(blk, k)
            if k:
                @pl.when(has_row)
                def arrived():
                    move(k, tok_ref, x_s, send_x, recv_x, source).wait_recv()

            chunk(source)
        each_sent(tok_ref, x_s, send_x, recv_x, lambda copy: copy.wait_send())
        each_sent(grad_ref, g_out, send_g, recv_g, lambda copy: copy.start())
        zero_s[...] = jnp.zeros_like(zero_s)

        @pl.when(has_row)
        def own_part():
            own_grad().start()

        @pl.when(jnp.logical_not(has_row))
        def no_part():
            for i in range(nblk):
                pltpu.make_async_copy(zero_s, g_out.at[i], local.at[free + 4 + i]).start()

        for i in range(len(kept)):
            store(i).start()

    cols = pl.ds(pl.multiple_of(step * LANES, LANES), LANES)
    seq = q_s.shape[0]
    first = lane_of((1, LANES)) < LANES // 2
    owns = (first, jnp.logical_not(first))
    one = jnp.ones((), bf16)
    keys = [jnp.where(own, k_s[:, cols], fk_s[...]) for own in owns]
    values = [jnp.where(own, v_s[:, cols], one) for own in owns]

    def score_of(start, head):
        rows = slice(start, start + CHUNK)
        return dot_nt(jnp.where(owns[head], q_s[rows, cols], fq_s[rows, :]), keys[head])

    items = [(start, head) for start in range(0, seq, CHUNK) for head in range(2)]
    ahead_score = score_of(*items[0])
    pieces = [None, None]
    for number, (start, head) in enumerate(items):
        score = ahead_score
        if number + 1 < len(items):
            ahead_score = score_of(*items[number + 1])
        rows = slice(start, start + CHUNK)
        top = jnp.max(score, axis=-1, keepdims=True)
        weight = jnp.exp(score - top).astype(bf16)
        eb_ref[0, head, rows, :] = weight
        mixed = dot(weight, values[head])
        inverse = 1.0 / pltpu.roll(mixed, LANES // 2, 1)
        pieces[head] = (mixed * inverse, inverse)
        if head == 1:
            attended = jnp.where(first, pieces[0][0], pieces[1][0])
            att_ref[rows, :] = attended
            ab_ref[rows, :] = attended.astype(bf16)
            inv_ref[rows, :] = jnp.where(first, pieces[0][1], pieces[1][1])

    @pl.when(step == last)
    def end():
        for i in range(len(kept)):
            store(i).wait()
        each_sent(grad_ref, g_out, send_g, recv_g, lambda copy: copy.wait_send())

        @pl.when(has_row)
        def received():
            own_grad().wait()
            for k in range(1, nblk):
                move(k, grad_ref, g_out, send_g, recv_g, partner(blk, k)).wait_recv()

        @pl.when(jnp.logical_not(has_row))
        def cleared():
            for i in range(nblk):
                pltpu.make_async_copy(zero_s, g_out.at[i], local.at[free + 4 + i]).wait()


def lines_of(vector):
    return vector.reshape(-1, LANES)


def ahead(tokens, grads, w_qkv, w_ada, lengths, timesteps, table, b_ada, gain_a, gain_m, b_down, b_up, nblk):
    rows_dev, stretch, width = tokens.shape
    seq = nblk * stretch
    head_dim = width // H
    freqs = np.float32(10000.0) ** (-np.arange(head_dim // 2, dtype=np.float32) * np.float32(2.0 / head_dim))
    freqs = np.concatenate([freqs] * 4)[None, :]
    small = [table, *(lines_of(a) for a in (b_ada, gain_a, gain_m, b_down, b_up)), freqs]
    pair = pl.BlockSpec((seq, LANES), lambda i: (0, i))
    fixed = lambda a: pl.BlockSpec(a.shape, lambda i: (0, 0), pipeline_mode=pl.Buffered(buffer_count=1))
    away = pl.BlockSpec(memory_space=pl.ANY)
    numbers = pl.BlockSpec(memory_space=pltpu.SMEM)
    blocks, flat, turn = (nblk, stretch, width), (seq, width), (seq, LANES)
    shape = jax.ShapeDtypeStruct
    vec = (16, width)
    return pl.pallas_call(
        ahead_kernel,
        grid=(width // LANES,),
        in_specs=[away] * 4 + [numbers] * 2 + [fixed(a) for a in small],
        out_specs=[away] * 8 + [pair] * 3
        + [pl.BlockSpec((1, 2, seq, seq), lambda i: (i, 0, 0, 0)), pl.BlockSpec(vec, lambda i: (0, 0))],
        out_shape=[
            shape(blocks, bf16), shape(blocks, bf16), shape(flat[::-1], bf16),
            shape(flat, bf16), shape(flat, bf16), shape(flat, bf16), shape(turn, f32), shape(turn, f32),
            shape(flat, f32), shape(flat, f32), shape(flat, bf16), shape((width // LANES, 2, seq, seq), bf16),
            shape(vec, f32),
        ],
        scratch_shapes=[
            pltpu.VMEM(blocks, bf16), pltpu.VMEM((stretch, width), bf16), pltpu.VMEM(flat[::-1], bf16),
            pltpu.VMEM(flat, bf16), pltpu.VMEM(flat, bf16), pltpu.VMEM(flat, bf16),
            pltpu.VMEM(turn, f32), pltpu.VMEM(turn, f32), pltpu.VMEM(w_qkv.shape, bf16), pltpu.VMEM(w_ada.shape, bf16),
            pltpu.VMEM(turn, bf16), pltpu.VMEM(turn, bf16), pltpu.VMEM((stretch, width), bf16),
        ] + [pltpu.SemaphoreType.DMA((nblk,))] * 4 + [pltpu.SemaphoreType.DMA((11 + nblk,))],
        compiler_params=pltpu.CompilerParams(
            collective_id=1, has_side_effects=True, vmem_limit_bytes=60 * MIB
        ),
        cost_estimate=pl.CostEstimate(
            flops=22 * seq * seq * width, bytes_accessed=24 * seq * width, transcendentals=H * seq * seq
        ),
    )(tokens, grads, w_qkv, w_ada, lengths, timesteps, *small)


def attend_back_pair(r, store):
    seq = r.q.shape[0]
    half = LANES // 4
    scale = 1.0 / math.sqrt(2 * half)
    lane = lane_of((1, LANES))
    first = lane < 2 * half
    owns = (first, jnp.logical_not(first))
    where = lane % (2 * half)
    one = jnp.ones((), bf16)
    scaled = r.datt[...].astype(f32) * r.inv[...]
    both = scaled * r.att[...]
    scaled_b = scaled.astype(bf16)
    values = []
    for head, own in enumerate(owns):
        total = -jnp.sum(jnp.where(own, both, 0.0), axis=-1, keepdims=True)
        delta = in_three(jnp.broadcast_to(total, both.shape))
        feature = jnp.zeros_like(scaled_b)
        for i in range(3):
            feature = jnp.where(where == i, delta[i], feature)
        r.da[head] = jnp.where(own, scaled_b, feature)
        values.append(jnp.where(own, r.v[...], one))
    queries_t = r.q[...].astype(f32).T.astype(bf16)
    scaled_t = scaled_b.astype(f32).T.astype(bf16)

    def grad_prob(start, head):
        return dot_nt(r.da[head, start : start + CHUNK, :], values[head])

    items = [(start, head) for start in range(0, seq, CHUNK) for head in range(2)]
    ahead_grad = grad_prob(*items[0])
    grad_q = {}
    for number, (start, head) in enumerate(items):
        grad_p = ahead_grad
        if number + 1 < len(items):
            ahead_grad = grad_prob(*items[number + 1])
        rows = slice(start, start + CHUNK)
        grad_s = (r.eb[0, head, rows, :].astype(f32) * grad_p).astype(bf16)
        r.ds[head, rows, :] = grad_s
        grad_q[start, head] = dot(grad_s, r.k[...])
    upper = lax.broadcasted_iota(jnp.int32, (LANES, 1), 0) < 2 * half
    grad_k = [dot(queries_t, r.ds[head]) for head in range(2)]
    grad_v = [dot(scaled_t, r.eb[0, head]) for head in range(2)]
    grad_k = jnp.where(upper, grad_k[0], grad_k[1]).T
    grad_v = jnp.where(upper, grad_v[0], grad_v[1]).T
    for start in range(0, seq, CHUNK):
        rows = slice(start, start + CHUNK)
        cosine, sine = r.cos[rows, :], r.sin[rows, :]
        turned = []
        for grad in (jnp.where(first, grad_q[start, 0], grad_q[start, 1]) * scale, grad_k[rows, :]):
            turned.append((grad * cosine - swap_halves(grad, half) * sine).astype(bf16))
        store(rows, turned[0], turned[1], grad_v[rows, :].astype(bf16))


def attend_back_kernel(names, *refs):
    r = types.SimpleNamespace(**dict(zip(names, refs)))

    def store(rows, *grads):
        for ref, grad in zip((r.dq, r.dk, r.dv), grads):
            ref[rows, :] = grad

    attend_back_pair(r, store)


def attend_back(q, k, v, grads, att, inv, eb, cosine, sine):
    seq, width = q.shape
    pair = pl.BlockSpec((seq, LANES), lambda i: (0, i))
    fixed = pl.BlockSpec((seq, LANES), lambda i: (0, 0))
    names = list(dict(q=0, k=0, v=0, datt=0, att=0, inv=0, eb=0, cos=0, sin=0, dq=0, dk=0, dv=0, da=0, ds=0))
    return pl.pallas_call(
        functools.partial(attend_back_kernel, names),
        grid=(width // LANES,),
        in_specs=[pair] * 6 + [pl.BlockSpec((1, 2, seq, seq), lambda i: (i, 0, 0, 0)), fixed, fixed],
        out_specs=[pair] * 3,
        out_shape=[jax.ShapeDtypeStruct((seq, width), bf16)] * 3,
        scratch_shapes=[pltpu.VMEM((2, seq, LANES), bf16), pltpu.VMEM((2, seq, seq), bf16)],
        compiler_params=pltpu.CompilerParams(vmem_limit_bytes=56 * MIB),
        cost_estimate=pl.CostEstimate(
            flops=32 * seq * seq * width, bytes_accessed=24 * seq * width + 2 * H * seq * seq, transcendentals=0
        ),
    )(q, k, v, grads, att, inv, eb, cosine, sine)


GELU = math.sqrt(2.0 / math.pi)
CUBE = 0.044715


def vec_rows(ref, *lines):
    return [ref[at : at + 1, :] for at in lines]


def feed_chunk(hidden, grad, w_up_ref, b_up, w_down_ref):
    u = dot(hidden, w_up_ref[...]) + b_up
    square = u * u
    turn = jnp.tanh(GELU * u * (1.0 + CUBE * square))
    half = 0.5 * (1.0 + turn)
    slope = half + (0.5 * GELU) * u * (1.0 - turn * turn) * (1.0 + 3.0 * CUBE * square)
    du = (dot_nt(grad, w_down_ref[...]) * slope).astype(bf16)
    return ((u * half).astype(bf16), du)


def feed_kernel(
    ab_ref, x_ref, g_ref, vec_ref, w_out_ref, w_up_ref, w_down_ref,
    result_ref, dx_ref, datt_ref, g_out_ref, g_up_ref, g_down_ref, gb_up_ref, sums_ref,
    h_s, ht_s, dz_s, dzt_s, y_s, z_s, dh_s, act_s, du_s, dyt_s
):
    step, last = pl.program_id(0), pl.num_programs(0) - 1
    seq, width = x_ref.shape
    wide = w_up_ref.shape[1]
    gate_a, factor_m, shift_m, gate_m, b_down = vec_rows(vec_ref, Vec.gate_a, Vec.factor_m, Vec.shift_m, Vec.gate_m, Vec.b_down)
    chunks = [slice(begin, begin + CHUNK) for begin in range(0, seq, CHUNK)]

    @pl.when(step == 0)
    def before():
        for rows in chunks:
            y = dot(ab_ref[rows, :], w_out_ref[...])
            y_s[rows, :] = y
            normed, unused = norm_rows(x_ref[rows, :].astype(f32) + gate_a * y)
            hidden = normed * factor_m + shift_m
            h_s[rows, :] = hidden.astype(bf16)
            ht_s[:, rows] = hidden.T.astype(bf16)
            grad = gate_m * g_ref[rows, :].astype(f32)
            dz_s[rows, :] = grad.astype(bf16)
            dzt_s[:, rows] = grad.T.astype(bf16)
        z_s[...] = jnp.zeros_like(z_s)
        dh_s[...] = jnp.zeros_like(dh_s)

    b_up = vec_ref[pl.ds(Vec.b_up + step, 1), :]
    bias_sum = jnp.zeros((1, wide), f32)
    for rows in chunks:
        act, du = feed_chunk(h_s[rows, :], dz_s[rows, :], w_up_ref, b_up, w_down_ref)
        act_s[rows, :] = act
        du_s[rows, :] = du
        bias_sum = bias_sum + jnp.sum(du.astype(f32), axis=0, keepdims=True)
        z_s[rows, :] += dot(act, w_down_ref[...])
        dh_s[rows, :] += dot_nt(du, w_up_ref[...])
    gb_up_ref[...] = bias_sum
    g_up_ref[0] = dot(ht_s[...], du_s[...]).astype(bf16)
    down = dot(dzt_s[...], act_s[...]).astype(bf16)
    g_down_ref[0, 0] = down[:, : wide // 2]
    g_down_ref[0, 1] = down[:, wide // 2 :]

    @pl.when(step == last)
    def after():
        sums = [jnp.zeros((1, width), f32) for unused in range(5)]
        for rows in chunks:
            y = y_s[rows, :]
            middle = x_ref[rows, :].astype(f32) + gate_a * y
            normed, inverse = norm_rows(middle)
            z = z_s[rows, :] + b_down
            result_ref[rows, :] = (middle + gate_m * z).astype(bf16)
            grad = g_ref[rows, :].astype(f32)
            dh = dh_s[rows, :]
            dx = grad + norm_back(dh * factor_m, normed, inverse)
            dx_ref[rows, :] = dx
            dy = gate_a * dx
            dyb = dy.astype(bf16)
            dyt_s[rows, :] = dyb
            datt_ref[rows, :] = dot_nt(dyb, w_out_ref[...]).astype(bf16)
            terms = (grad * z, dh, dh * normed, dx * y, dz_s[rows, :].astype(f32))
            sums = [a + jnp.sum(b, axis=0, keepdims=True) for a, b in zip(sums, terms)]
        g_out_ref[...] = dot_tn(ab_ref[...], dyt_s[...]).astype(bf16)
        for i in range(5):
            sums_ref[i : i + 1, :] = sums[i]


def feed(ab, x, g, vec, w_out, w_up, w_down):
    seq, width = x.shape
    ff = w_up.shape[1]
    wide = width
    fixed = lambda a: pl.BlockSpec(a.shape, lambda i: (0, 0))
    one = lambda shape: pl.BlockSpec(shape, lambda i: (0, 0))
    col = lambda r: pl.BlockSpec((r, wide), lambda i: (0, i))
    shape = jax.ShapeDtypeStruct
    return pl.pallas_call(
        feed_kernel,
        grid=(ff // wide,),
        in_specs=[
            fixed(ab), fixed(x), fixed(g), fixed(vec), fixed(w_out), col(width),
            pl.BlockSpec((wide, width), lambda i: (i, 0)),
        ],
        out_specs=[
            one((seq, width)), one((seq, width)), one((seq, width)), one((width, width)),
            pl.BlockSpec((1, width, wide), lambda i: (i, 0, 0)),
            pl.BlockSpec((1, 2, width, wide // 2), lambda i: (i, 0, 0, 0)), col(1), one((8, width)),
        ],
        out_shape=[
            shape((seq, width), bf16), shape((seq, width), f32), shape((seq, width), bf16),
            shape((width, width), bf16), shape((ff // wide, width, wide), bf16),
            shape((ff // wide, 2, width, wide // 2), bf16),
            shape((1, ff), f32), shape((8, width), f32),
        ],
        scratch_shapes=[
            pltpu.VMEM((seq, width), bf16), pltpu.VMEM((width, seq), bf16),
            pltpu.VMEM((seq, width), bf16), pltpu.VMEM((width, seq), bf16),
            pltpu.VMEM((seq, width), f32), pltpu.VMEM((seq, width), f32), pltpu.VMEM((seq, width), f32),
            pltpu.VMEM((seq, wide), bf16), pltpu.VMEM((seq, wide), bf16), pltpu.VMEM((seq, width), bf16),
        ],
        compiler_params=pltpu.CompilerParams(vmem_limit_bytes=60 * MIB),
        cost_estimate=pl.CostEstimate(
            flops=12 * seq * width * ff, bytes_accessed=30 * seq * width, transcendentals=seq * ff
        ),
    )(ab, x, g, vec, w_out, w_up, w_down)


def gather_kernel(nblk, nrows, in_ref, out_ref, send_r, recv_r, send_b, recv_b):
    blk, row = lax.axis_index("blk"), lax.axis_index("rows")
    barrier = pltpu.get_barrier_semaphore()
    for step in range(1, nblk):
        pl.semaphore_signal(
            barrier, inc=1, device_id=(lax.rem(blk + step, nblk), row), device_id_type=MESH
        )

    def greet(step, unused):
        pl.semaphore_signal(
            barrier, inc=1, device_id=(blk, lax.rem(row + step, nrows)), device_id_type=MESH
        )
        return unused

    lax.fori_loop(1, nrows, greet, 0)
    pl.semaphore_wait(barrier, nblk + nrows - 2)
    out_ref[blk, row] = in_ref[...]

    def over_rows(step):
        other = lax.rem(row + step, nrows)
        return pltpu.make_async_remote_copy(
            src_ref=in_ref,
            dst_ref=out_ref.at[blk, row],
            send_sem=send_r.at[step],
            recv_sem=recv_r.at[step],
            device_id=(blk, other),
            device_id_type=MESH,
        )

    def over_blk(step):
        other = lax.rem(blk + step, nblk)
        return pltpu.make_async_remote_copy(
            src_ref=out_ref.at[blk],
            dst_ref=out_ref.at[blk],
            send_sem=send_b.at[step],
            recv_sem=recv_b.at[step],
            device_id=(other, row),
            device_id_type=MESH,
        )

    def start(step, unused):
        over_rows(step).start()
        return unused

    def finish(step, unused):
        over_rows(step).wait()
        return unused

    lax.fori_loop(1, nrows, start, 0)
    lax.fori_loop(1, nrows, finish, 0)
    for step in range(1, nblk):
        over_blk(step).start()
    for step in range(1, nblk):
        over_blk(step).wait()


def gather_all(vector, nblk, nrows):
    count = vector.shape[0] // LANES
    return pl.pallas_call(
        functools.partial(gather_kernel, nblk, nrows),
        out_shape=jax.ShapeDtypeStruct((nblk, nrows, count, LANES), f32),
        in_specs=[pl.BlockSpec(memory_space=pltpu.VMEM)],
        out_specs=pl.BlockSpec(memory_space=pltpu.VMEM),
        scratch_shapes=[
            pltpu.SemaphoreType.DMA((nrows,)),
            pltpu.SemaphoreType.DMA((nrows,)),
            pltpu.SemaphoreType.DMA((nblk,)),
            pltpu.SemaphoreType.DMA((nblk,)),
        ],
        compiler_params=pltpu.CompilerParams(collective_id=0, has_side_effects=True),
    )(vector.reshape(count, LANES))


class Place:
    def __init__(self):
        self.blk, self.row = lax.axis_index("blk"), lax.axis_index("rows")
        self.x, self.y = self.blk % 2, self.blk // 2
        self.core, self.z = self.row % 2, self.row // 2

    def along_blk(self, k):
        return (partner(self.blk, k), self.row)

    def along_rows(self, k):
        return (self.blk, partner(self.row, k))


class Sems:
    def __init__(self, send, recv):
        self.send, self.recv, self.used = send, recv, 0

    def take(self, count):
        self.used += count
        return self.used - count

    def copy(self, index, source, target, device):
        return remote(source, target, self.send.at[index], self.recv.at[index], *device)


def part(index, size, step):
    return pl.ds(pl.multiple_of(index * size, step), size)


class Piece:
    def __init__(self, place, sems, dims, bufs, whole=None, own=None, store=None):
        self.p, self.sems, self.base = place, sems, sems.take(self.SEMS)
        self.whole, self.own, self.store = whole, own, store
        self.b = types.SimpleNamespace(**bufs)
        self.nz, share, cols = dims
        self.hs, self.hc, self.hz = share // 2, cols // 2, self.nz // 2

    def start(self, stage):
        for copy in self.copies(stage):
            copy.start()

    def wait(self, stage):
        for copy in self.copies(stage):
            copy.wait()

    def take_own(self):
        def onto(i, unused):
            self.b.core[i] = self.b.core[i] + self.own(i)
            return unused

        lax.fori_loop(0, self.b.core.shape[0], onto, 0)

    def run(self, stage, go_on=True):
        if stage:
            self.wait(stage - 1)
            self.add(stage)
        if stage < 5 and go_on:
            self.start(stage)


ROW_BUFS = ("core", "a1", "b1", "a2", "b2", "r3", "zr", "ag")
FAR_BUFS = ("core", "z1", "z2", "pr", "ag")


def shapes_of(names, shapes):
    return {name: pltpu.VMEM(shape, bf16) for name, shape in zip(names, shapes)}


class RowPiece(Piece):
    SEMS = 11

    @staticmethod
    def scratch(nz, share, cols):
        hs, hc = share // 2, cols // 2
        return shapes_of(
            ROW_BUFS,
            [
                (nz, share, cols), (nz // 2, share, hc), (nz // 2, hs, cols), (nz // 2, hs, hc), (nz // 2, hs, hc),
                (nz, hs, hc), (nz, hs, hc), (4, hs, hc),
            ],
        )

    def row(self, y):
        return part(y, self.hs, 16)

    def col(self, x):
        return part(x, self.hc, LANES)

    def copies(self, stage):
        p, at, b, copy = self.p, self.base, self.b, self.sems.copy
        low, high = slice(0, self.hz), slice(self.hz, self.nz)
        if stage == 0:
            return [copy(at, self.whole.at[:, 1 - p.core], b.core, p.along_rows(1))]
        if stage == 1:
            return [
                copy(at + 1, b.core.at[low, :, self.col(1 - p.x)], b.a1, p.along_blk(1)),
                copy(at + 2, b.core.at[high, self.row(1 - p.y), :], b.b1, p.along_blk(2)),
            ]
        if stage == 2:
            return [
                copy(at + 3, b.a1.at[:, self.row(1 - p.y), :], b.a2, p.along_blk(2)),
                copy(at + 4, b.b1.at[:, :, self.col(1 - p.x)], b.b2, p.along_blk(1)),
            ]
        if stage == 3:
            return [
                copy(at + 4 + k, b.r3.at[partner(p.z, k)], b.zr.at[p.z], p.along_rows(2 * k))
                for k in range(1, self.nz)
            ]
        return [copy(at + 7 + k, b.ag.at[p.blk], b.ag.at[p.blk], p.along_blk(k)) for k in range(1, 4)]

    def add(self, stage):
        p, b = self.p, self.b
        row, col = self.row(p.y), self.col(p.x)
        if stage == 1:
            self.take_own()
        if stage == 2:
            b.a1[...] = b.a1[...] + b.core[: self.hz, :, col]
            b.b1[...] = b.b1[...] + b.core[self.hz :, row, :]
        if stage == 3:
            b.r3[: self.hz] = b.a1[:, row, :] + b.a2[...]
            b.r3[self.hz :] = b.b1[:, :, col] + b.b2[...]
        if stage == 4:
            total = b.r3[p.z].astype(f32)
            for k in range(1, self.nz):
                total = total + b.zr[partner(p.z, k)].astype(f32)
            b.ag[p.blk] = total.astype(bf16)
        if stage == 5:
            for q in range(4):
                rows = slice(q // 2 * self.hs, (q // 2 + 1) * self.hs)
                self.store(rows, q % 2 * self.hc, b.ag[q])


class FarPiece(Piece):
    SEMS = 9

    @staticmethod
    def scratch(nz, share, cols):
        hs, hc = share // 2, cols // 2
        return shapes_of(
            FAR_BUFS,
            [(nz, share, cols), (nz // 2, share, cols), (share, cols), (4, hs, hc), (4, hs, hc)],
        )

    def quarter(self, blk):
        return (part(blk // 2, self.hs, 16), part(blk % 2, self.hc, LANES))

    def copies(self, stage):
        p, at, b, copy = self.p, self.base, self.b, self.sems.copy
        low, high = p.z % 2, p.z // 2
        if stage == 0:
            return [copy(at, self.whole.at[:, 1 - p.core], b.core, p.along_rows(1))]
        if stage == 1:
            return [
                copy(at + 1, b.core.at[1 - low], b.z1.at[0], p.along_rows(2)),
                copy(at + 2, b.core.at[3 - low], b.z1.at[1], p.along_rows(2)),
            ]
        if stage == 2:
            return [copy(at + 3, b.z1.at[1 - high], b.z2, p.along_rows(4))]
        if stage == 3:
            return [
                copy(at + 3 + k, b.z2.at[self.quarter(partner(p.blk, k))], b.pr.at[p.blk], p.along_blk(k))
                for k in range(1, 4)
            ]
        return [copy(at + 3 + k, b.ag.at[p.blk], b.ag.at[p.blk], p.along_blk(k)) for k in range(1, 4)]

    def add(self, stage):
        p, b = self.p, self.b
        low, high = p.z % 2, p.z // 2
        if stage == 1:
            self.take_own()
        if stage == 2:
            for i in range(2):
                b.z1[i] = b.z1[i] + b.core[2 * i + low]
        if stage == 3:
            b.z2[...] = b.z2[...] + b.z1[high]
        if stage == 4:
            rows, cols = self.quarter(p.blk)
            total = b.z2[rows, cols].astype(f32)
            for k in range(1, 4):
                total = total + b.pr[partner(p.blk, k)].astype(f32)
            b.ag[p.blk] = total.astype(bf16)
        if stage == 5:
            for q in range(4):
                rows = slice(q // 2 * self.hs, (q // 2 + 1) * self.hs)
                self.store(rows, q % 2 * self.hc, b.ag[q])


class ColPiece(Piece):
    SEMS = 12

    @staticmethod
    def scratch(nz, depth, cols):
        return shapes_of(
            ROW_BUFS[:6],
            [
                (2, 2, 2, depth, cols), (2, depth, cols), (2, depth, cols), (depth, cols), (depth, cols),
                (2, depth, cols),
            ],
        )

    @staticmethod
    def shared(nz, depth, cols):
        return shapes_of(("zr", "ag"), [(nz, 2, depth, cols), (4, 2, depth, cols)])

    def __init__(self, place, sems, dims, bufs, owner, **kinds):
        super().__init__(place, sems, dims, bufs, **kinds)
        self.owner = owner
        self.depth = dims[1]

    def copies(self, stage):
        p, at, b, copy = self.p, self.base, self.b, self.sems.copy
        if stage == 0:
            return [copy(at, self.whole.at[1 - p.core], b.core, p.along_rows(1))]
        if stage == 1:
            return [
                copy(at + 1, b.core.at[:, 1 - p.x, 0], b.a1, p.along_blk(1)),
                copy(at + 2, b.core.at[1 - p.y, :, 1], b.b1, p.along_blk(2)),
            ]
        if stage == 2:
            return [
                copy(at + 3, b.a1.at[1 - p.y], b.a2, p.along_blk(2)),
                copy(at + 4, b.b1.at[1 - p.x], b.b2, p.along_blk(1)),
            ]
        return [copy(at + 8 + k, b.ag.at[p.blk], b.ag.at[p.blk], p.along_blk(k)) for k in range(1, 4)]

    def over_z(self, k):
        device = (self.p.blk, 2 * self.owner + self.p.core)
        return self.sems.copy(self.base + 5 + k, self.b.r3, self.b.zr.at[self.p.z], device)

    def from_afar(self, k, what):
        @pl.when(self.p.z == self.owner ^ k)
        def far():
            what(self.over_z(k))

    def here(self, what):
        @pl.when(self.p.z == self.owner)
        def at_owner():
            what()

    def start(self, stage):
        if stage == 3:
            for k in range(1, 4):
                self.from_afar(k, lambda copy: copy.start())
        elif stage == 4:
            self.here(lambda: [copy.start() for copy in self.copies(4)] and None)
        else:
            super().start(stage)

    def wait(self, stage):
        if stage == 3:
            for k in range(1, 4):
                self.from_afar(k, lambda copy: copy.wait_send())
            self.here(lambda: [self.over_z(k).wait_recv() for k in range(1, 4)] and None)
        elif stage == 4:
            self.here(lambda: [copy.wait() for copy in self.copies(4)] and None)
        else:
            super().wait(stage)

    def add(self, stage):
        p, b = self.p, self.b
        if stage == 1:
            self.take_own()
        if stage == 2:
            b.a1[...] = b.a1[...] + b.core[:, p.x, 0]
            b.b1[...] = b.b1[...] + b.core[p.y, :, 1]
        if stage == 3:
            b.r3[0] = b.a1[p.y] + b.a2[...]
            b.r3[1] = b.b1[p.x] + b.b2[...]
        if stage == 4:
            def summed():
                total = b.r3[...].astype(f32)
                for k in range(1, 4):
                    total = total + b.zr[self.owner ^ k].astype(f32)
                b.ag[p.blk] = total.astype(bf16)
            self.here(summed)
        if stage == 5:
            def stored():
                for q in range(8):
                    self.store(slice(q * self.depth, (q + 1) * self.depth), b.ag[q // 2, q % 2])
            self.here(stored)


class Bag:
    def __init__(self):
        self.names, self.items = [], []

    def add(self, name, item):
        if isinstance(item, dict):
            for key, value in item.items():
                self.add(f"{name}.{key}", value)
        else:
            self.names.append(name)
            self.items.append(item)


def group(refs, name):
    return {key[len(name) + 1 :]: ref for key, ref in vars(refs).items() if key.startswith(name + ".")}


def only(shapes, names):
    return {name: shapes[name] for name in names if name in shapes}


class Plan:
    def __init__(self):
        self.actions = {}

    def at(self, point, *actions):
        self.actions.setdefault(point, []).extend(actions)

    def stages(self, piece, first, points):
        for number, point in enumerate(points):
            self.at(point, lambda number=first + number: piece.run(number))

    def run(self, point):
        for action in self.actions.get(point, []):
            action()

    def under(self, step, number, point):
        if point in self.actions:
            @pl.when(step == number)
            def actions():
                self.run(point)


EARLY, LATE = 64, 32


def write_lines(target, lines):
    target[...] = jnp.zeros_like(target)
    at = 0
    for line in lines:
        for k in range(line.shape[1] // LANES):
            target[at : at + 1, :] = line[:, k * LANES : (k + 1) * LANES]
            at += 1


FEED_POINTS = ((7, 11), (11, 16), (16,), ())
HANDED = {1: ("core",), 2: ("a1", "b1"), 3: ("r3",)}


def feed_move_kernel(names, *refs):
    r = types.SimpleNamespace(**dict(zip(names, refs)))
    step, last = pl.program_id(0), pl.num_programs(0) - 1
    place = Place()
    sems = Sems(r.send, r.recv)
    seq, width = r.x.shape
    wide = r.w_up.shape[1]
    nz, unused, share, cols = r.gu.shape[1:]
    depth, dcols = r.gd.shape[-2:]
    nrows = 2 * nz
    plan = Plan()

    ups, downs = [], []
    for i in range(4):
        side = i % 2
        ups.append(
            RowPiece(
                place, sems, (nz, share, cols), group(r, f"u{i}"), r.gu.at[side],
                lambda i, side=side: r.gu[side, i, place.core],
            )
        )
        bufs = group(r, f"d{i}")
        downs.append(
            ColPiece(
                place, sems, (nz, depth, dcols), bufs, i, whole=r.gd.at[side],
                own=lambda i, side=side: r.gd[side, place.core, i],
            )
        )
    for i, points in enumerate(FEED_POINTS):
        for kind, piece in (("up", ups[i]), ("down", downs[i])):
            plan.stages(piece, 1, points)
            if len(points) < 5:
                plan.at(20, lambda kind=kind, piece=piece, i=i, stage=len(points) + 1: hand_over(piece, stage, f"{kind}{i}"))

    def hand_over(piece, stage, name):
        piece.run(stage, False)
        for key in HANDED[stage]:
            getattr(r, f"{name}.{key}")[...] = getattr(piece.b, key)[...]

    gate_a, factor_m, shift_m, gate_m, b_down = vec_rows(r.vec, Vec.gate_a, Vec.factor_m, Vec.shift_m, Vec.gate_m, Vec.b_down)
    chunks = [slice(begin, begin + CHUNK) for begin in range(0, seq, CHUNK)]

    @pl.when(step == 0)
    def before():
        greet(place, 4, nrows)

        def enter(number, unused):
            rows = part(number, CHUNK, CHUNK)
            y = dot(r.ab[rows, :], r.w_out[...])
            r.y[rows, :] = y
            normed, unused = norm_rows(r.x[rows, :].astype(f32) + gate_a * y)
            hidden = normed * factor_m + shift_m
            r.h[rows, :] = hidden.astype(bf16)
            r.ht[:, rows] = hidden.T.astype(bf16)
            grad = gate_m * r.g[rows, :].astype(f32)
            r.dz[rows, :] = grad.astype(bf16)
            r.dzt[:, rows] = grad.T.astype(bf16)
            return 0

        lax.fori_loop(0, len(chunks), enter, 0)
        r.z[...] = jnp.zeros_like(r.z)
        r.dh[...] = jnp.zeros_like(r.dh)

    b_up = r.vec[pl.ds(Vec.b_up + step, 1), :]
    bias_sum = jnp.zeros((1, wide), f32)
    for number, rows in enumerate(chunks):
        for i in range(4):
            plan.under(step, i, 4 * i + number)
        act, du = feed_chunk(r.h[rows, :], r.dz[rows, :], r.w_up, b_up, r.w_down)
        r.act[rows, :] = act
        r.du[rows, :] = du
        bias_sum = bias_sum + jnp.sum(du.astype(f32), axis=0, keepdims=True)
        r.z[rows, :] += dot(act, r.w_down[...])
        r.dh[rows, :] += dot_nt(du, r.w_up[...])
    r.gb[pl.ds(step, 1), :] = bias_sum
    side = step % 2
    r.gu[side] = dot(r.ht[...], r.du[...]).astype(bf16).reshape(r.gu.shape[1:])
    down = dot(r.dzt[...], r.act[...]).astype(bf16)
    for core in range(2):
        half = down[:, core * dcols : (core + 1) * dcols]
        r.gd[side, core] = half.reshape(r.gd.shape[2:])
    for i in range(4):
        @pl.when(step == i)
        def sent():
            ups[i].run(0)
            downs[i].run(0)

    @pl.when(step == last)
    def after():
        plan.run(16)

        def leave(number, sums):
            rows = part(number, CHUNK, CHUNK)
            y = r.y[rows, :]
            middle = r.x[rows, :].astype(f32) + gate_a * y
            normed, inverse = norm_rows(middle)
            z = r.z[rows, :] + b_down
            r.result[rows, :] = (middle + gate_m * z).astype(bf16)
            grad = r.g[rows, :].astype(f32)
            dh = r.dh[rows, :]
            dx = grad + norm_back(dh * factor_m, normed, inverse)
            r.dx[rows, :] = dx
            dyb = (gate_a * dx).astype(bf16)
            r.dy[rows, :] = dyb
            r.datt[rows, :] = dot_nt(dyb, r.w_out[...]).astype(bf16)
            terms = (grad * z, dh, dh * normed, dx * y, r.dz[rows, :].astype(f32))
            return tuple(a + jnp.sum(b, axis=0, keepdims=True) for a, b in zip(sums, terms))

        sums = lax.fori_loop(0, len(chunks), leave, tuple(jnp.zeros((1, width), f32) for unused in range(5)))
        plan.run(18)
        r.g_out[...] = dot_tn(r.ab[...], r.dy[...]).astype(bf16)
        gain_m, scale_m, time = vec_rows(r.vec, Vec.gain_m, Vec.scale_m, Vec.step)
        dgate_m, dshift_m, along_m, dgate_a, grad_b_down = sums
        lines = [dgate_a, dshift_m, along_m * gain_m, dgate_m, along_m * (1.0 + scale_m), grad_b_down]
        lines += [r.gb[i : i + 1, :] for i in range(4)] + [time[:, :LANES]]
        write_lines(r.pack, lines)
        r.early[...] = r.pack[...].astype(bf16)
        plan.run(20)


def feed_move(ab, x, g, vec, w_out, w_up, w_down, nrows):
    seq, width = x.shape
    ff = w_up.shape[1]
    wide = width
    nz, share, depth, dcols = nrows // 2, width // nrows, width // 8, wide // 2
    once = pl.Buffered(buffer_count=1)
    fixed = lambda a: pl.BlockSpec(a.shape, lambda i: (0, 0), pipeline_mode=once)
    col = lambda r: pl.BlockSpec((r, wide), lambda i: (0, i))
    shape = jax.ShapeDtypeStruct
    ins, outs, scratch = Bag(), Bag(), Bag()
    for name, spec in (
        ("ab", fixed(ab)), ("x", fixed(x)), ("g", fixed(g)), ("vec", fixed(vec)), ("w_out", fixed(w_out)),
        ("w_up", col(width)), ("w_down", pl.BlockSpec((wide, width), lambda i: (i, 0))),
    ):
        ins.add(name, spec)
    for name, dims, kind in (
        ("result", (seq, width), bf16), ("dx", (seq, width), f32), ("datt", (seq, width), bf16),
        ("g_out", (width, width), bf16), ("early", (EARLY, LANES), bf16),
    ):
        outs.add(name, shape(dims, kind))
    row_bufs, col_bufs = RowPiece.scratch(nz, share, wide), ColPiece.scratch(nz, depth, dcols)
    for i, points in enumerate(FEED_POINTS):
        if len(points) < 5:
            for kind, bufs in (("up", row_bufs), ("down", col_bufs)):
                for key in HANDED[len(points) + 1]:
                    outs.add(f"{kind}{i}.{key}", shape(bufs[key].shape, bf16))
    for name in ("h", "dz", "act", "du", "dy"):
        scratch.add(name, pltpu.VMEM((seq, width), bf16))
    for name in ("ht", "dzt"):
        scratch.add(name, pltpu.VMEM((width, seq), bf16))
    for name in ("y", "z", "dh"):
        scratch.add(name, pltpu.VMEM((seq, width), f32))
    scratch.add("gb", pltpu.VMEM((8, wide), f32))
    scratch.add("pack", pltpu.VMEM((EARLY, LANES), f32))
    scratch.add("gu", pltpu.VMEM((2, nz, 2, share, wide), bf16))
    scratch.add("gd", pltpu.VMEM((2, 2, 2, 2, 2, depth, dcols), bf16))
    for i, points in enumerate(FEED_POINTS):
        kept = ROW_BUFS[: (1, 3, 6)[len(points)]]
        scratch.add(f"u{i}", only(row_bufs, kept))
        scratch.add(f"d{i}", only(col_bufs, kept))
    count = 4 * (RowPiece.SEMS + ColPiece.SEMS)
    scratch.add("send", pltpu.SemaphoreType.DMA((count,)))
    scratch.add("recv", pltpu.SemaphoreType.DMA((count,)))
    results = pl.pallas_call(
        functools.partial(feed_move_kernel, ins.names + outs.names + scratch.names),
        grid=(ff // wide,),
        in_specs=ins.items,
        out_specs=[pl.BlockSpec(o.shape, lambda i, n=len(o.shape): (0,) * n) for o in outs.items],
        out_shape=outs.items,
        scratch_shapes=scratch.items,
        compiler_params=pltpu.CompilerParams(collective_id=3, has_side_effects=True, vmem_limit_bytes=62 * MIB),
        cost_estimate=pl.CostEstimate(
            flops=12 * seq * width * ff, bytes_accessed=30 * seq * width, transcendentals=seq * ff
        ),
    )(ab, x, g, vec, w_out, w_up, w_down)
    return dict(zip(outs.names, results))


class Gather:
    def __init__(self, place, sems, source, target):
        self.p, self.sems, self.source, self.target = place, sems, source, target
        self.nblk, self.nrows = target.shape[:2]
        self.base = sems.take(self.nblk + self.nrows)

    def copies(self, stage):
        p = self.p
        if stage == 0:
            return [
                self.sems.copy(self.base + k, self.source, self.target.at[p.blk, p.row], p.along_rows(k))
                for k in range(1, self.nrows)
            ]
        return [
            self.sems.copy(self.base + self.nrows + k, self.target.at[p.blk], self.target.at[p.blk], p.along_blk(k))
            for k in range(1, self.nblk)
        ]

    def run(self, stage):
        if stage:
            for copy in self.copies(stage - 1):
                copy.wait()
        else:
            self.target[self.p.blk, self.p.row] = self.source[...]
        if stage < 2:
            for copy in self.copies(stage):
                copy.start()


class Return:
    def __init__(self, place, sems, source, target, local):
        self.p, self.sems, self.source, self.target, self.local = place, sems, source, target, local
        self.rows, self.nblk = target.shape[0], source.shape[0]
        self.base = sems.take(self.nblk)
        self.mine = jnp.minimum(place.blk, self.rows - 1)

    def copy(self, k):
        device = self.p.along_blk(k)
        return self.sems.copy(self.base + k, self.source.at[device[0]], self.target.at[self.mine], device)

    def own(self):
        return pltpu.make_async_copy(self.source.at[self.p.blk], self.target.at[self.mine], self.local)

    def start(self, ks):
        @pl.when(self.p.blk < self.rows)
        def sent():
            for k in ks:
                (self.copy(k) if k else self.own()).start()

    def finish(self):
        @pl.when(self.p.blk < self.rows)
        def left():
            self.own().wait()
            for k in range(1, self.nblk):
                self.copy(k).wait_send()

        for k in range(1, self.nblk):
            @pl.when(partner(self.p.blk, k) < self.rows)
            def arrived():
                self.copy(k).wait_recv()


def greet(place, nblk, nrows):
    barrier = pltpu.get_barrier_semaphore()
    for k in range(1, nblk):
        pl.semaphore_signal(barrier, inc=1, device_id=place.along_blk(k), device_id_type=MESH)
    for k in range(1, nrows):
        pl.semaphore_signal(barrier, inc=1, device_id=place.along_rows(k), device_id_type=MESH)
    pl.semaphore_wait(barrier, nblk + nrows - 2)


BEHIND_POINTS = ((8, 11), (8, 11), (6, 10, 13), (7, 10, 12, 15))
OUTER_POINTS = (5, 9, 11, 13, 15)
EARLY_POINTS = (8, 16)
RESULT_POINTS = (0, 0, 0, 0)
LATE_POINTS = ((9, 11, 13, 15, 16), (12, 13, 15, 17, 18), (12, 13, 15, 17, 19))


def behind_kernel(names, *refs):
    r = types.SimpleNamespace(**dict(zip(names, refs)))
    step, last = pl.program_id(0), pl.num_programs(0) - 1
    place = Place()
    sems = Sems(r.send, r.recv)
    nblk, stretch, width = r.x.shape
    nrows = r.early_g.shape[1]
    nz, unused, share, cols = r.gq.shape[1:]
    depth, dcols = getattr(r, "d.ag").shape[-2:]
    seq = nblk * stretch
    dims, ddims = (nz, share, cols), (nz, depth, dcols)

    def store_at(ref, begin):
        def store(rows, col, value):
            ref[rows, begin + col : begin + col + value.shape[1]] = value
        return store

    def store_qkv(j):
        def store(rows, col, value):
            for k in range(value.shape[1] // LANES):
                lane = col + k * LANES
                at = lane // (2 * LANES) * width + j * 2 * LANES + lane % (2 * LANES)
                r.share_qkv[rows, at : at + LANES] = value[:, k * LANES : (k + 1) * LANES]
        return store

    def store_down(rows, value):
        r.share_down[rows, :] = value

    shared = group(r, "d")
    carried = []
    for i, points in enumerate(FEED_POINTS):
        if len(points) < 5:
            up = RowPiece(
                place, sems, dims, dict(group(r, f"u{i}"), **group(r, f"up{i}")), store=store_at(r.share_up, i * cols)
            )
            down = ColPiece(
                place, sems, ddims, dict(shared, **group(r, f"d{i}"), **group(r, f"down{i}")), i, store=store_down
            )
            carried.append((len(points) + 1, up, down))
    outer = RowPiece(
        place, sems, dims, group(r, "o"), r.g_out, lambda i: r.own_out[i], store_at(r.share_out, 0)
    )
    load = pltpu.make_async_copy(r.g_out.at[:, place.core], r.own_out, r.local.at[2])
    late_pieces = [
        kind(
            place, sems, dims, group(r, f"q{j}"), r.gq.at[j], lambda i, j=j: r.gq[j, i, place.core], store_qkv(j)
        )
        for j, kind in enumerate((RowPiece, RowPiece, RowPiece))
    ]
    results = Return(place, sems, r.result, r.tok_out, r.local.at[0])
    grads = Return(place, sems, r.gt, r.grad_out, r.local.at[1])
    early = Gather(place, sems, r.early_s, r.early_g)
    late = Gather(place, sems, r.late_b, r.late_g)

    def open_up():
        greet(place, nblk, nrows)
        load.start()
        for stage, up, down in carried:
            up.start(stage)
            down.start(stage)
        outer.run(0)
        r.share_down[...] = jnp.zeros_like(r.share_down)

    def start_early():
        r.early_s[...] = r.early[...]
        early.run(0)

    plan = Plan()
    plan.at(0, open_up)
    plan.at(1, start_early, load.wait)
    for (stage, up, down), points in zip(carried, BEHIND_POINTS):
        for piece in (up, down):
            plan.stages(piece, stage + 1, points)
    plan.stages(outer, 1, OUTER_POINTS)
    plan.stages(early, 1, EARLY_POINTS)
    for k, point in zip((3, 1, 2, 0), RESULT_POINTS):
        plan.at(point, lambda k=k: results.start([k]))
    for piece, points in zip(late_pieces, LATE_POINTS):
        plan.stages(piece, 1, points)

    for i in range(6):
        plan.under(step, i, 2 * i)
    side = step % 2 * LANES

    def store(rows, *grads):
        for i, grad in enumerate(grads):
            r.dqkv[rows, pl.ds(pl.multiple_of(2 * i * LANES + side, LANES), LANES)] = grad

    attend_back_pair(r, store)
    for i in range(6):
        plan.under(step, i, 2 * i + 1)

    @pl.when(step % 2 == 1)
    def projections():
        number = step // 2
        grad_w = dot(r.ht[...], r.dqkv[...]).astype(bf16)
        r.gq[number] = grad_w.reshape(r.gq.shape[1:])
        for j, piece in enumerate(late_pieces):
            @pl.when(number == j)
            def sent():
                piece.run(0)

        @pl.when(number == 0)
        def fresh():
            r.dh[...] = jnp.zeros_like(r.dh)

        def onto(begin, unused):
            rows = part(begin, CHUNK, CHUNK)
            added = dot_nt(r.dqkv[rows, : 2 * LANES], r.wq[...])
            added = added + dot_nt(r.dqkv[rows, 2 * LANES : 4 * LANES], r.wk[...])
            r.dh[rows, :] += added + dot_nt(r.dqkv[rows, 4 * LANES :], r.wv[...])
            return unused

        lax.fori_loop(0, seq // CHUNK, onto, 0)

    @pl.when(step == last)
    def tail():
        factor, gain, scale = vec_rows(r.vec, Vec.factor_a, Vec.gain_a, Vec.scale_a)
        total = [jnp.zeros((1, width), f32) for unused in range(2)]

        def chunk(k):
            slot = partner(place.blk, k)
            rows = pl.ds(pl.multiple_of(slot * stretch, stretch), stretch)
            normed, inverse = norm_rows(r.x[slot].astype(f32))
            dh = r.dh[rows, :]
            r.gt[slot] = (r.dx[rows, :] + norm_back(dh * factor, normed, inverse)).astype(bf16)
            grads.start([k])
            total[0] = total[0] + jnp.sum(dh, axis=0, keepdims=True)
            total[1] = total[1] + jnp.sum(dh * normed, axis=0, keepdims=True)

        plan.run(12)
        chunk(3)
        plan.run(13)
        chunk(1)
        plan.run(14)
        chunk(2)
        chunk(0)
        write_lines(r.late_s, (total[0], total[1] * gain, total[1] * (1.0 + scale)))
        r.late_b[...] = r.late_s[...].astype(bf16)
        late.run(0)
        plan.run(15)
        plan.run(16)
        r.early_out[...] = r.early_g[...]
        late.run(1)
        plan.run(17)
        late.run(2)
        r.late_out[...] = r.late_g[...]
        plan.run(18)
        plan.run(19)
        results.finish()
        grads.finish()


def behind(q, k, v, grads, att, inv, eb, cosine, sine, w_qkv, hidden_t, x, dx, vec, early, handed, g_out, result,
           rows_dev, nrows):
    seq, width = q.shape
    nblk, stretch, unused = x.shape
    nz, share, cols, depth, dcols = nrows // 2, width // nrows, width, width // 8, width // 2
    pair = pl.BlockSpec((seq, LANES), lambda i: (0, i))
    once = pl.Buffered(buffer_count=1)
    fixed = lambda a: pl.BlockSpec(a.shape, lambda i: (0,) * len(a.shape), pipeline_mode=once)
    away = pl.BlockSpec(memory_space=pl.ANY)
    per = width // (2 * LANES)
    weight = lambda n: pl.BlockSpec((width, 2 * LANES), lambda i: (0, n * per + i // 2))
    shape = jax.ShapeDtypeStruct
    ins, args, outs, scratch = Bag(), [], Bag(), Bag()
    for name, spec, value in (
        ("q", pair, q), ("k", pair, k), ("v", pair, v), ("datt", pair, grads), ("att", pair, att), ("inv", pair, inv),
        ("eb", pl.BlockSpec((1, 2, seq, seq), lambda i: (i, 0, 0, 0)), eb), ("cos", fixed(cosine), cosine), ("sin", fixed(sine), sine),
        ("wq", weight(0), w_qkv), ("wk", weight(1), w_qkv), ("wv", weight(2), w_qkv),
        ("ht", fixed(hidden_t), hidden_t), ("x", fixed(x), x), ("dx", fixed(dx), dx), ("vec", fixed(vec), vec),
        ("early", fixed(early), early), *((name, fixed(value), value) for name, value in handed.items()),
        ("g_out", away, g_out), ("result", away, result),
    ):
        ins.add(name, spec)
        args.append(value)
    back = shape((rows_dev, stretch, width), bf16)
    late = (LATE, LANES)
    for name, value in (
        ("tok_out", back), ("grad_out", back), ("share_qkv", shape((share, 3 * width), bf16)),
        ("share_out", shape((share, cols), bf16)), ("share_up", shape((share, 4 * cols), bf16)),
        ("share_down", shape((8 * depth, dcols), bf16)),
        ("early_out", shape((nblk, nrows) + early.shape, bf16)), ("late_out", shape((nblk, nrows) + late, bf16)),
    ):
        outs.add(name, value)
    for name, dims, kind in (
        ("da", (2, seq, LANES), bf16), ("ds", (2, seq, seq), bf16),
        ("dqkv", (seq, 6 * LANES), bf16), ("dh", (seq, width), f32), ("gq", (3, nz, 2, share, cols), bf16),
        ("gt", (nblk, stretch, width), bf16), ("early_s", early.shape, bf16), ("late_s", late, f32),
        ("late_b", late, bf16), ("early_g", (nblk, nrows) + early.shape, bf16),
        ("late_g", (nblk, nrows) + late, bf16), ("own_out", (nz, share, cols), bf16),
    ):
        scratch.add(name, pltpu.VMEM(dims, kind))
    near, cross = RowPiece.scratch(nz, share, cols), ColPiece.scratch(nz, depth, dcols)
    for i, points in enumerate(FEED_POINTS):
        if len(points) < 5:
            kept = ROW_BUFS[(1, 3, 6)[len(points)] :]
            scratch.add(f"u{i}", only(near, kept))
            scratch.add(f"d{i}", only(cross, kept))
    scratch.add("d", ColPiece.shared(nz, depth, dcols))
    scratch.add("o", near)
    for j in range(3):
        scratch.add(f"q{j}", near)
    count = 8 * RowPiece.SEMS + 4 * ColPiece.SEMS + 2 * nblk + 2 * (nblk + nrows)
    scratch.add("send", pltpu.SemaphoreType.DMA((count,)))
    scratch.add("recv", pltpu.SemaphoreType.DMA((count,)))
    scratch.add("local", pltpu.SemaphoreType.DMA((3,)))
    results = pl.pallas_call(
        functools.partial(behind_kernel, ins.names + outs.names + scratch.names),
        grid=(width // LANES,),
        in_specs=ins.items,
        out_specs=[away, away] + [pl.BlockSpec(o.shape, lambda i, n=len(o.shape): (0,) * n) for o in outs.items[2:]],
        out_shape=outs.items,
        scratch_shapes=scratch.items,
        compiler_params=pltpu.CompilerParams(collective_id=2, has_side_effects=True, vmem_limit_bytes=62 * MIB),
        cost_estimate=pl.CostEstimate(
            flops=52 * seq * seq * width, bytes_accessed=40 * seq * width, transcendentals=H * seq * seq
        ),
    )(*args)
    return dict(zip(outs.names, results))


FETCH = ("tok", "grad", "early", "late", "table", "ada", "up", "qkv", "outer", "down")


def finish_kernel(names, *refs):
    r = types.SimpleNamespace(**dict(zip(names, refs)))
    row = lax.axis_index("rows")
    loads = {name: pltpu.make_async_copy(getattr(r, name + "_in"), getattr(r, name), r.local.at[i]) for i, name in enumerate(FETCH)}
    for load in loads.values():
        load.start()
    moves = []
    for i, (name, target) in enumerate((("tok", r.out), ("grad", r.grad_tokens))):
        loads[name].wait()
        moves.append(pltpu.make_async_copy(getattr(r, name), target, r.local.at[len(FETCH) + i]))
        moves[-1].start()
    for name in ("early", "late", "table", "ada"):
        loads[name].wait()
    rows_dev = r.out.shape[0]
    nblk, nrows = r.early.shape[:2]
    count = rows_dev * nrows
    width = r.out.shape[-1]
    per = width // LANES
    for b in range(rows_dev):
        r.early_s[b] = r.early[b].astype(f32)
        r.late_s[b] = r.late[b].astype(f32)
    r.mod[...] = jnp.zeros_like(r.mod)

    def of_all(ref, line):
        return [ref[b, :, line, :] for b in range(rows_dev)]

    for i in range(6 * per):
        blocks = of_all(r.late_s, i) if i < 2 * per else of_all(r.early_s, i - 2 * per)
        for b, block in enumerate(blocks):
            r.mod[b * nrows : (b + 1) * nrows, i * LANES : (i + 1) * LANES] = block
    total = jnp.sum(r.early_s[...], axis=(0, 1))
    late_total = jnp.sum(r.late_s[...], axis=(0, 1))

    ff = r.b_up.shape[0]
    r.gain_m[...] = total[4 * per : 5 * per]
    r.b_down[...] = total[5 * per : 6 * per]
    r.b_up[...] = total[6 * per : 6 * per + ff]
    r.gain_a[...] = late_total[2 * per : 3 * per]
    r.b_ada[: 2 * per, :] = late_total[: 2 * per]
    r.b_ada[2 * per :, :] = total[: 4 * per]
    mod = r.mod[...]
    mod_b = mod.astype(bf16)
    steps = r.steps
    steps[...] = jnp.full(steps.shape, -1.0, f32)
    for b, block in enumerate(of_all(r.early_s, 6 * per + ff)):
        steps[b * nrows : (b + 1) * nrows, :] = block
    entries = r.table.shape[0]
    hot = (steps[:, :entries] == lane_of((1, entries)).astype(f32)).astype(f32).astype(bf16)
    conds = dot(hot, r.table[...])
    r.act_t[...] = jnp.concatenate([silu(conds), jnp.zeros((LANES - conds.shape[0], conds.shape[1]), f32)]).T
    share = r.w_ada.shape[0]
    mine = r.act_t[pl.ds(pl.multiple_of(row * share, share), share), : conds.shape[0]]
    r.w_ada[...] = sum(dot(term, mod_b) for term in in_three(mine))
    grad_act = dot_nt(mod_b, r.ada[...])
    sigmoid = 1.0 / (1.0 + jnp.exp(-conds))
    grad_cond = grad_act * sigmoid * (1.0 + conds * (1.0 - sigmoid))
    r.grad_table[...] = sum(dot_tn(hot, term) for term in in_three(grad_cond))
    for name in ("up", "qkv", "outer", "down"):
        loads[name].wait()
    r.w_up[...] = r.up[...].astype(f32)
    r.w_qkv[...] = r.qkv[...].astype(f32)
    r.w_out[...] = r.outer[...].astype(f32)

    r.w_down[...] = r.down[...].astype(f32).T
    for move in moves:
        move.wait()


def finish(o, table, w_ada):
    rows_dev, stretch, width = o["tok_out"].shape
    nblk, nrows = o["early_out"].shape[:2]
    shape = jax.ShapeDtypeStruct
    away, near = pl.BlockSpec(memory_space=pl.ANY), pl.BlockSpec(memory_space=pltpu.VMEM)
    args, outs, scratch = [], Bag(), Bag()
    fetched = dict(
        tok=o["tok_out"], grad=o["grad_out"], early=o["early_out"], late=o["late_out"], table=table, ada=w_ada,
        up=o["share_up"], qkv=o["share_qkv"], outer=o["share_out"], down=o["share_down"],
    )
    for name in FETCH:
        args.append(fetched[name])
        scratch.add(name, pltpu.VMEM(fetched[name].shape, fetched[name].dtype))
    names = [name + "_in" for name in FETCH] + ["out", "grad_tokens"]
    six, share, per = 6 * width, width // nrows, width // LANES
    ff = o["share_up"].shape[1]
    for name, dims in (
        ("grad_table", table.shape), ("w_ada", (w_ada.shape[0] // nrows, six)), ("b_ada", (6 * per, LANES)),
        ("gain_a", (per, LANES)), ("w_qkv", (share, 3 * width)), ("w_out", (share, width)), ("gain_m", (per, LANES)),
        ("w_up", (share, ff)), ("b_up", (ff // LANES, LANES)), ("w_down", (ff // nrows, width)),
        ("b_down", (per, LANES)),
    ):
        outs.add(name, shape(dims, f32))
    lines = 32
    for name, dims in (
        ("early_s", (rows_dev, nrows, EARLY, LANES)), ("late_s", (rows_dev, nrows, LATE, LANES)), ("mod", (lines, six)),
        ("steps", (lines, LANES)), ("act_t", (LANES, LANES)),
    ):
        scratch.add(name, pltpu.VMEM(dims, f32))
    scratch.add("local", pltpu.SemaphoreType.DMA((2 + len(FETCH),)))
    moved = shape((rows_dev, stretch, width), bf16)
    return pl.pallas_call(
        functools.partial(finish_kernel, names + outs.names + scratch.names),
        in_specs=[away] * len(args),
        out_specs=[away, away] + [near] * len(outs.items),
        out_shape=[moved, moved] + outs.items,
        scratch_shapes=scratch.items,
        compiler_params=pltpu.CompilerParams(vmem_limit_bytes=62 * MIB),
    )(*args)


def rows_out(whole, rows, me, nblk):
    parts = [lax.dynamic_index_in_dim(whole, me, 0, keepdims=False)]
    for k in range(1, nblk):
        part = lax.dynamic_index_in_dim(whole, me ^ k, 0, keepdims=False)
        pairs = [(s, s ^ k) for s in range(nblk) if s < rows]
        parts.append(lax.ppermute(part, "blk", pairs))
    stacked = jnp.stack(parts)
    return jnp.take(stacked, jnp.arange(rows) ^ me, axis=0)


def pick(array, index, axis=0):
    return lax.dynamic_index_in_dim(array, index, axis, keepdims=False)


def xor_move(array, axis, size, k):
    return lax.ppermute(array, axis, [(s, s ^ k) for s in range(size)])


def halve(array, axis, bit, name, size, k):
    kept = pick(array, bit, axis).astype(f32)
    sent = pick(array, 1 - bit, axis)
    return (kept + xor_move(sent, name, size, k).astype(f32)).astype(bf16)


def reduce_weight(grad, blk, row, nblk, nrows):
    total, cols = grad.shape
    share = total // nrows
    nz = nrows // 2
    core, z = row % 2, row // 2
    x, y = blk % 2, blk // 2
    part = halve(grad.reshape(nz, 2, share, cols), 1, core, "rows", nrows, 1)
    part = part.reshape(nz, 2, share // 2, cols)
    front, back = part[: nz // 2], part[nz // 2 :]
    split = lambda a: jnp.stack([a[..., : cols // 2], a[..., cols // 2 :]])
    front = halve(split(front), 0, x, "blk", nblk, 1)
    back = halve(back, 1, y, "blk", nblk, 2)
    front = halve(front, 1, y, "blk", nblk, 2)
    back = halve(split(back), 0, x, "blk", nblk, 1)
    part = jnp.concatenate([front, back], axis=0)
    if nz <= 4:
        summed = pick(part, z).astype(f32)
        for k in range(1, nz):
            summed = summed + xor_move(pick(part, z ^ k), "rows", nrows, 2 * k).astype(f32)
        part = summed.astype(bf16)
    else:
        k = nz // 2
        while k:
            pairs = part.reshape((2, k) + part.shape[1:])
            part = halve(pairs, 0, (z // k) % 2, "rows", nrows, 2 * k)
            k //= 2
        part = part[0]
    quarters = [part] + [xor_move(part, "blk", nblk, k) for k in range(1, 4)]
    quarters = jnp.take(jnp.stack(quarters), jnp.arange(4) ^ blk, axis=0)
    ordered = quarters.reshape(2, 2, share // 2, cols // 2).transpose(0, 2, 1, 3)
    return ordered.reshape(share, cols).astype(f32)


def per_device(
    tokens, timesteps, lengths, time_table, w_ada, b_ada, gain_attn, w_qkv, w_out, gain_mlp, w_up, b_up,
    w_down, b_down, grad_out
):
    rows_dev, stretch, width = tokens.shape
    nblk, nrows = lax.axis_size("blk"), lax.axis_size("rows")
    blk, row = lax.axis_index("blk"), lax.axis_index("rows")
    seq = stretch * nblk

    x_blocks, g_blocks, hidden_t, q, k, v, cosine, sine, attended, inv, attended_b, eb, vec = ahead(
        tokens, grad_out, w_qkv, w_ada, lengths, timesteps, time_table, b_ada, gain_attn, gain_mlp, b_down, b_up, nblk
    )
    x_row = x_blocks.reshape(seq, width)

    ff = b_up.shape[0]
    fed = (attended_b, x_row, g_blocks.reshape(seq, width), vec, w_out, w_up, w_down)

    if (nblk, nrows) == (4, 8):
        f = feed_move(*fed, nrows)
        nz, share = nrows // 2, width // nrows
        o = behind(
            q, k, v, f["datt"], attended, inv, eb, cosine, sine, w_qkv, hidden_t, x_blocks, f["dx"], vec, f["early"],
            {name: value for name, value in f.items() if "." in name}, f["g_out"].reshape(nz, 2, share, width),
            f["result"].reshape(nblk, stretch, width), rows_dev, nrows,
        )
        out, grad_tokens, *rest = finish(o, time_table, w_ada)
        flat = (2, 3, 6, 8, 10)
        return (out, grad_tokens, *(value.reshape(-1) if i in flat else value for i, value in enumerate(rest)))

    shift_a, scale_a, gate_a, shift_m, scale_m, gate_m, factor_a, factor_m, gain_a, gain_m, step = vec[:11]
    result, grad_mid, grad_att, grad_w_out, grad_w_up, grad_w_down, gb_up, sums = feed(*fed)
    dgate_m, dshift_m, along_m, dgate_a, grad_b_down = (sums[i] for i in range(5))
    out = rows_out(result.reshape(nblk, stretch, width), rows_dev, blk, nblk)
    share_w_down = reduce_weight(grad_w_down.transpose(2, 0, 1, 3).reshape(width, ff).T, blk, row, nblk, nrows)
    share_w_up = reduce_weight(grad_w_up.transpose(1, 0, 2).reshape(width, ff), blk, row, nblk, nrows)
    share_w_out = reduce_weight(grad_w_out, blk, row, nblk, nrows)
    dq, dk, dv = attend_back(q, k, v, grad_att, attended, inv, eb, cosine, sine)
    grad_qkv = jnp.concatenate([dq, dk, dv], axis=-1)
    grad_w_qkv = dot(hidden_t, grad_qkv).astype(bf16)
    share_w_qkv = reduce_weight(grad_w_qkv, blk, row, nblk, nrows)
    grad_ha = dot_nt(grad_qkv, w_qkv)
    normed_a, inverse_a = norm_rows(x_row.astype(f32))
    along_a = jnp.sum(grad_ha * normed_a, axis=0)
    grad_in = (grad_mid + norm_back(grad_ha * factor_a, normed_a, inverse_a)).astype(bf16)
    grad_tokens = rows_out(grad_in.reshape(nblk, stretch, width), rows_dev, blk, nblk)
    count = 6 * width + ff + LANES
    packed = jnp.concatenate(
        [
            dgate_a, dshift_m, along_m * gain_m, dgate_m, along_m * (1.0 + scale_m), grad_b_down, gb_up[0],
            step[:LANES], jnp.sum(grad_ha, axis=0), along_a * gain_a, along_a * (1.0 + scale_a),
        ]
    )
    gathered = gather_all(packed, nblk, nrows).reshape(nblk, nrows, -1)
    early = gathered[:rows_dev].reshape(rows_dev * nrows, -1)
    dshift_a, dscale_a, part_gain_a = (early[:, count + i * width : count + (i + 1) * width] for i in range(3))

    table, ada_full = time_table.astype(f32), w_ada.astype(f32)
    grad_mod = jnp.concatenate([dshift_a, dscale_a, early[:, : 4 * width]], axis=-1)
    smalls = jnp.sum(early, axis=0)
    grad_gain_m, total_b_down = smalls[4 * width : 5 * width], smalls[5 * width : 6 * width]
    total_b_up = smalls[6 * width : 6 * width + ff]
    steps = early[:, 6 * width + ff].astype(jnp.int32)
    onehot = (steps[:, None] == jnp.arange(table.shape[0], dtype=jnp.int32)[None, :]).astype(f32)
    conds = jnp.dot(onehot, table, precision=highest)
    share = conds.shape[1] // nrows
    my_conds = lax.dynamic_slice_in_dim(conds, row * share, share, axis=1)
    grad_w_ada = jnp.dot(jax.nn.silu(my_conds).T, grad_mod, precision=highest)
    grad_cond_act = lax.dot_general(
        grad_mod, ada_full, (((1,), (1,)), ((), ())), precision=highest, preferred_element_type=f32
    )
    sigmoid = jax.nn.sigmoid(conds)
    grad_cond = grad_cond_act * sigmoid * (1.0 + conds * (1.0 - sigmoid))
    grad_table = jnp.dot(onehot.T, grad_cond, precision=highest)
    return (
        out,
        grad_tokens,
        grad_table,
        grad_w_ada,
        jnp.sum(grad_mod, axis=0),
        jnp.sum(part_gain_a, axis=0),
        share_w_qkv,
        share_w_out,
        grad_gain_m,
        share_w_up,
        total_b_up,
        share_w_down,
        total_b_down,
    )


def solution(mesh):
    whole, split = P(), P("rows", None)
    tokens = P("rows", "blk", None)
    return jax.shard_map(
        per_device,
        mesh=mesh,
        in_specs=(tokens, P("rows"), split) + (whole,) * 11 + (tokens,),
        out_specs=(
            tokens, tokens, whole, split, whole, whole, split, split, whole, split, whole, split, whole
        ),
        check_vma=False,
    )
```
